32 devices in a mesh: cols: 8 (over z, x), par: 4 (over y, core).
Axes of the slice: x: 2, y: 2, z: 4, core: 2. Of those that a mesh axis runs over, the one named last changes fastest.
Arguments:
- tile_bounds: int32 [9], replicated, may hold values from 0 to 2048, as said below
- tile_anchor: int32 [64, 2], P(('cols', 'par')), may hold values from 0 to 256, as said below
- tile_picks: int32 [64], P(('cols', 'par')), may hold values from 16 to 64, as said below
- rmo_picks: bfloat16 [64, 64], P(('cols', 'par')), may hold values from -6 to 6
- sensitivity: bfloat16 [64, 64, 3, 16, 128], P(('cols', 'par')), may hold values from -0.75 to 0.75
- dip_class: int32 [32, 8, 256], P(('cols', 'par')), may hold values from 0 to 8
- strength: float32 [3], replicated, may hold values from 0.05 to 0.2
- couple: float32 [3, 3], replicated, may hold values from 0.1 to 1
Outputs:
- model_update: float32 [3, 32, 8, 256], P(None, ('cols', 'par'))
The draws below stay inside these ranges and needn't reach their ends.
Inputs may be any that keep to these rules, and one draw needn't show every extreme that they name: tile_bounds[0] = 0 and tile_bounds[8] = 2048; column tile c holds grid columns tile_bounds[c] to tile_bounds[c + 1] - 1, between 128 and 384 of them, and some column tile holds exactly 384. Fat-ray tile t belongs to column tile t // (2 * 4); it covers depth cells tile_anchor[t, 0] to tile_anchor[t, 0] + 15 and column slots tile_anchor[t, 1] to tile_anchor[t, 1] + 127 of that column tile, all of them among its columns and within the grid. Rays 0 to tile_picks[t] - 1 of tile t are live; some tile has 64 live rays.
All inputs are finite; a program needn't handle non-finite values.
Results may differ from the reference program's by a relative error of at most 0.0003.
Values sent between devices are 32-bit elements; how exact they have to be, the bound alone decides.
No kernel may reach another device: no remote copies, remote signals or barrier semaphores. Data moves between devices by JAX's collectives and lax.ppermute only.
A program may use at most 192 MiB of HBM per device.

```python
import math
import jax
import jax.numpy as jnp
from jax import lax

NPARAM = 3
NT = 2
RAYS = 64
TZ = 16
TC = 128
COL_DEV = 256
LY = 256
PASSES = 6
TILES = 64
NZ = 32
NCOLUMNS = 2048
LX = 8
N_COLS = 8
N_PAR = 4


def tile_layout(key):
    keys = jax.random.split(jax.random.fold_in(key, 7), 5)
    half = N_COLS // 2
    spread = jax.random.randint(keys[0], (half,), -(COL_DEV // 2), COL_DEV // 2 + 1)
    widest = jax.random.randint(keys[1], (), 0, half)
    spread = spread.at[widest].set(COL_DEV // 2)
    side = jax.random.randint(keys[2], (half,), 0, 2) * 2 - 1
    spread = spread * side
    widths = jnp.stack([COL_DEV + spread, COL_DEV - spread], axis=1).reshape(-1)
    bounds = jnp.concatenate([jnp.zeros((1,), jnp.int32), jnp.cumsum(widths).astype(jnp.int32)])
    per_tile = TILES // N_COLS
    owner_tile = jnp.arange(TILES) // per_tile
    tile_width = widths[owner_tile]
    column_first = jax.random.randint(keys[3], (TILES,), 0, tile_width - TC + 1)
    depth_first = jax.random.randint(keys[4], (TILES,), 0, NZ - TZ + 1)
    broadest = jnp.argmax(widths).astype(jnp.int32)
    first_ray_tile = broadest * per_tile
    column_first = column_first.at[first_ray_tile].set(widths[broadest] - TC)
    column_first = column_first.at[first_ray_tile + 1].set(0)
    depth_first = depth_first.at[0].set(NZ - TZ)
    depth_first = depth_first.at[1].set(0)
    anchor = jnp.stack([depth_first, column_first], axis=1).astype(jnp.int32)
    return (bounds.astype(jnp.int32), anchor)


def draw_tile_bounds(key, part):
    return tile_layout(key)[0]


def draw_tile_anchor(key, part):
    return tile_layout(key)[1]


def draw_tile_picks(key, part):
    keys = jax.random.split(jax.random.fold_in(key, 11), 2)
    picks = jax.random.randint(keys[0], (TILES,), RAYS // 4, RAYS + 1)
    fullest = jax.random.randint(keys[1], (), 0, TILES)
    return picks.at[fullest].set(RAYS).astype(jnp.int32)


def plant(array, key, smallest, largest):
    longest = array.shape.index(max(array.shape))
    spots = []
    for shift in (0, 1):
        where = [jax.random.randint(jax.random.fold_in(key, axis), (), 0, length) for axis, length in enumerate(array.shape)]
        where[longest] = (where[longest] + shift) % array.shape[longest]
        spots.append(tuple(where))
    return array.at[spots[0]].set(smallest).at[spots[1]].set(largest)


def level_of(rng, shape, shards, least, top_value):
    factor_of = 1.0
    for position, shards_of in shards:
        draws = jax.random.uniform(jax.random.fold_in(jax.random.fold_in(rng, 6), position), (shards_of,), jnp.float32, least / len(shards), top_value / len(shards))
        factor_of = factor_of * jnp.repeat(jnp.exp(draws), shape[position] // shards_of).reshape((-1,) + (1,) * (len(shape) - 1 - position))
    return factor_of


def noise(key, dims, deviation, bound, cuts=(), held_as=jnp.bfloat16):
    factor_of = level_of(key, dims, cuts, -0.22, 0.18) if cuts else 1.0
    array = jax.random.normal(key, dims, jnp.float32) * deviation * factor_of
    return jnp.minimum(jnp.maximum(array, -bound), bound).astype(held_as)


def setup_inputs(seed: int = 0) -> dict:
    arg_keys = jax.random.split(jax.random.key(seed), 9)
    return {
        "tile_bounds": draw_tile_bounds(jax.random.fold_in(arg_keys[8], 71), 0),
        "tile_anchor": draw_tile_anchor(jax.random.fold_in(arg_keys[8], 71), 0),
        "tile_picks": draw_tile_picks(jax.random.fold_in(arg_keys[8], 71), 0),
        "rmo_picks": noise(arg_keys[3], (TILES, RAYS), 1.0, 6.0, ((0, 32),)),
        "sensitivity": noise(arg_keys[4], (TILES, RAYS, NPARAM, TZ, TC), RAYS ** -0.5, 0.75, ((0, 32),)),
        "dip_class": plant(jax.random.randint(arg_keys[5], (NZ, LX, LY), 0, 9), jax.random.fold_in(arg_keys[5], 1), 0, 8).astype(jnp.int32),
        "strength": jnp.clip(jnp.exp(jax.random.uniform(arg_keys[6], (NPARAM,), jnp.float32, math.log(0.05), math.log(0.2))), 0.05, 0.2),
        "couple": jnp.clip(jnp.exp(jax.random.uniform(arg_keys[7], (NPARAM, NPARAM), jnp.float32, math.log(0.1), math.log(1.0))), 0.1, 1.0),
    }


def next_cells(values, along_dim):
    count = values.shape[along_dim]
    kept = lax.slice_in_dim(values, 1, count, axis=along_dim)
    zeros = jnp.zeros_like(lax.slice_in_dim(values, 0, 1, axis=along_dim))
    return jnp.concatenate([kept, zeros], axis=along_dim)


def prev_cells(values, along_dim):
    count = values.shape[along_dim]
    kept = lax.slice_in_dim(values, 0, count - 1, axis=along_dim)
    zeros = jnp.zeros_like(lax.slice_in_dim(values, 0, 1, axis=along_dim))
    return jnp.concatenate([zeros, kept], axis=along_dim)


def at_depth(padded, tilt):
    return jnp.where(tilt < 0, padded[:, :-2], jnp.where(tilt > 0, padded[:, 2:], padded[:, 1:-1]))


def smooth_pass(padded, dip_class, strength, mixing):
    centre = padded[:, 1:-1]
    tilt_across = (dip_class // 3 - 1)[None]
    tilt_along = (dip_class % 3 - 1)[None]
    east_side = at_depth(next_cells(padded, 2), tilt_across)
    west_side = at_depth(prev_cells(padded, 2), -tilt_across)
    north_side = at_depth(next_cells(padded, 3), tilt_along)
    south_side = at_depth(prev_cells(padded, 3), -tilt_along)
    laplace = east_side + west_side + north_side + south_side - 4.0 * centre
    smooth = centre + strength[:, None, None, None] * laplace
    return jnp.tensordot(mixing, smooth, axes=1, precision=lax.Precision.HIGHEST)


def reference(tile_bounds, tile_anchor, tile_picks, rmo_picks, sensitivity, dip_class, strength, couple):
    owner_tile = jnp.arange(TILES, dtype=jnp.int32) // (NT * N_PAR)
    column_start = (tile_bounds[owner_tile] + tile_anchor[:, 1]).astype(jnp.int32)
    depth_start = tile_anchor[:, 0].astype(jnp.int32)

    def add_tile(gradient, tile_items):
        sens_tile, rmo_tile, live_count, depth_first, column_first = tile_items
        live = jnp.arange(RAYS, dtype=jnp.int32) < live_count
        ray_weight = jnp.where(live, rmo_tile, jnp.zeros_like(rmo_tile))
        partial_value = jnp.dot(ray_weight[None, :], sens_tile.reshape(RAYS, -1), preferred_element_type=jnp.float32)
        partial_value = partial_value.reshape(NPARAM, TZ, TC).astype(gradient.dtype)
        anchor = (jnp.int32(0), depth_first, column_first)
        current = lax.dynamic_slice(gradient, anchor, (NPARAM, TZ, TC))
        return lax.dynamic_update_slice(gradient, current + partial_value, anchor), None

    gradient = jnp.zeros((NPARAM, NZ, NCOLUMNS), jnp.float32)
    gradient, _ = lax.scan(add_tile, gradient, (sensitivity, rmo_picks, tile_picks, depth_start, column_start))
    field = gradient.reshape(NPARAM, NZ, LX, LY)
    mixing = couple / jnp.sum(couple, axis=1, keepdims=True)
    for _ in range(PASSES):
        padded = jnp.pad(field, ((0, 0), (1, 1), (0, 0), (0, 0)))
        field = smooth_pass(padded, dip_class, strength, mixing)
    return field
```

```python
import functools

import jax
import jax.numpy as jnp
from jax import lax
from jax.experimental import pallas as pl
from jax.experimental.pallas import tpu as pltpu
from jax.sharding import PartitionSpec as P

CAP = 384
PASSES = 6


def extended(block, sides, width):
    for axis, dim in sides:
        count = lax.axis_size(axis)
        forward = [(i, i + 1) for i in range(count - 1)]
        backward = [(target, source) for source, target in forward]
        low = lax.ppermute(
            lax.slice_in_dim(block, block.shape[dim] - width, None, axis=dim), axis, forward
        )
        high = lax.ppermute(lax.slice_in_dim(block, 0, width, axis=dim), axis, backward)
        block = jnp.concatenate([low, block, high], axis=dim)
    return block


def next_cells(values, along_dim):
    count = values.shape[along_dim]
    kept = lax.slice_in_dim(values, 1, count, axis=along_dim)
    zeros = jnp.zeros_like(lax.slice_in_dim(values, 0, 1, axis=along_dim))
    return jnp.concatenate([kept, zeros], axis=along_dim)


def prev_cells(values, along_dim):
    count = values.shape[along_dim]
    kept = lax.slice_in_dim(values, 0, count - 1, axis=along_dim)
    zeros = jnp.zeros_like(lax.slice_in_dim(values, 0, 1, axis=along_dim))
    return jnp.concatenate([zeros, kept], axis=along_dim)


def at_depth(padded, tilt):
    return jnp.where(tilt < 0, padded[:, :-2], jnp.where(tilt > 0, padded[:, 2:], padded[:, 1:-1]))


def smooth_pass(padded, dip_class, strength, mixing):
    centre = padded[:, 1:-1]
    tilt_across = (dip_class // 3 - 1)[None]
    tilt_along = (dip_class % 3 - 1)[None]
    east_side = at_depth(next_cells(padded, 2), tilt_across)
    west_side = at_depth(prev_cells(padded, 2), -tilt_across)
    north_side = at_depth(next_cells(padded, 3), tilt_along)
    south_side = at_depth(prev_cells(padded, 3), -tilt_along)
    laplace = east_side + west_side + north_side + south_side - 4.0 * centre
    smooth = centre + strength[:, None, None, None] * laplace
    return jnp.tensordot(mixing, smooth, axes=1, precision=lax.Precision.HIGHEST)


def shards_any(
    tile_bounds, tile_anchor, tile_picks, rmo_picks, sensitivity, dip_class, strength, couple
):
    tile_count, ray_count, param_count, depth_cells, tile_columns = sensitivity.shape
    col_devices = lax.axis_size("cols")
    par_devices = lax.axis_size("par")
    slab_depth, rows_x, rows_y = dip_class.shape
    total_depth = slab_depth * col_devices * par_devices
    live = jnp.arange(ray_count, dtype=jnp.int32)[None, :] < tile_picks[:, None]
    ray_weight = jnp.where(live, rmo_picks, jnp.zeros_like(rmo_picks))
    contribution = jnp.einsum(
        "tr,trk->tk",
        ray_weight,
        sensitivity.reshape(tile_count, ray_count, -1),
        preferred_element_type=jnp.float32,
    )
    contribution = contribution.reshape(tile_count, param_count, depth_cells, tile_columns)

    def add_tile(tile_number, gradient):
        anchor = (jnp.int32(0), tile_anchor[tile_number, 0], tile_anchor[tile_number, 1])
        current = lax.dynamic_slice(gradient, anchor, (param_count, depth_cells, tile_columns))
        return lax.dynamic_update_slice(gradient, current + contribution[tile_number], anchor)

    gradient = jnp.zeros((param_count, total_depth, CAP), jnp.float32)
    gradient = lax.fori_loop(0, tile_count, add_tile, gradient)
    blocks = gradient.reshape(param_count, col_devices, par_devices, slab_depth, CAP)
    reduced = lax.psum_scatter(blocks, "par", scatter_dimension=2, tiled=True)
    summed = lax.all_to_all(reduced, "cols", split_axis=1, concat_axis=4, tiled=True)
    padded_slots = summed.reshape(param_count, slab_depth, col_devices * CAP)
    columns = rows_x * rows_y
    column_ids = jnp.arange(columns, dtype=jnp.int32)
    starts = tile_bounds[:-1]
    below = starts[None, :] <= column_ids[:, None]
    owner_tile = jnp.sum(below.astype(jnp.int32), axis=1) - 1
    tile_start = jnp.max(jnp.where(below, starts[None, :], jnp.zeros_like(starts)[None, :]), axis=1)
    slot_index = owner_tile * CAP + column_ids - tile_start
    field = jnp.take(padded_slots, slot_index, axis=2).reshape(
        param_count, slab_depth, rows_x, rows_y
    )
    mixing = couple / jnp.sum(couple, axis=1, keepdims=True)
    for _ in range(PASSES):
        padded = extended(field, ((("cols", "par"), 1),), 1)
        field = smooth_pass(padded, dip_class, strength, mixing)
    return field


LANES = 128
SUBLANES = 8


def device_index():
    return lax.axis_index("cols") * lax.axis_size("par") + lax.axis_index("par")


def lane_ids(shape):
    return lax.broadcasted_iota(jnp.int32, shape, len(shape) - 1)


def roll_lanes(values, shift):
    width = values.shape[-1]
    shift = shift % width
    return values if shift == 0 else pltpu.roll(values, shift, values.ndim - 1)


def source_kernel(start_ref, anchor_ref, picks_ref, rmo_ref, sens_ref, dip_ref, out_ref, weight_ref):
    tiles, rays, params, tile_depth, tile_columns = sens_ref.shape
    _, rows_x, rows_y = dip_ref.shape
    halves = rows_y // LANES
    diagonal = lax.broadcasted_iota(jnp.int32, (rays, rays), 0) == lane_ids((rays, rays))
    parts = [[[None] * tiles for _ in range(params)] for _ in range(halves)]
    x_rows, depth_rows = [], []
    y_ids = lane_ids((1, rows_y))
    for tile in range(tiles):
        live = lane_ids((1, rays)) < picks_ref[tile]
        weight = jnp.where(live, rmo_ref[tile : tile + 1, :].astype(jnp.float32), 0.0)
        column = jnp.sum(jnp.where(diagonal, weight, 0.0), axis=1, keepdims=True)
        weight_ref[...] = jnp.broadcast_to(column, weight_ref.shape)
        total = jnp.zeros((params, tile_depth, tile_columns), jnp.float32)
        for ray in range(rays):
            total = total + weight_ref[ray : ray + 1, :][None] * sens_ref[tile, ray].astype(jnp.float32)
        depth_first = anchor_ref[tile, 0]
        first = start_ref[0] + anchor_ref[tile, 1]
        first_x = first // rows_y
        first_y = first - first_x * rows_y
        half_of = first_y // LANES
        lane_first = first_y - half_of * LANES
        past = lane_ids((1, LANES)) >= lane_first
        for param in range(params):
            turned = pltpu.roll(total[param], lax.rem(depth_first, tile_depth), 0)
            turned = pltpu.roll(turned, lane_first, 1)
            for half in range(halves):
                after = lax.rem(half_of + 1, halves)
                kept = jnp.logical_or(
                    jnp.logical_and(past, half_of == half),
                    jnp.logical_and(jnp.logical_not(past), after == half),
                )
                parts[half][param][tile] = jnp.where(kept, turned, 0.0)
        x_rows.append((first_x + (y_ids < first_y).astype(jnp.int32)).astype(jnp.float32))
        depth_rows.append(jnp.full((1, rows_y), depth_first, jnp.int32).astype(jnp.float32))
    notes = jnp.concatenate(
        x_rows + depth_rows + [jnp.zeros((SUBLANES - 2 * tiles, rows_y), jnp.float32)], axis=0
    )
    dip = dip_ref[0].astype(jnp.float32)
    width = out_ref.shape[1]
    side = jnp.concatenate([roll_lanes(dip, width), dip, roll_lanes(dip, -width), notes], axis=0)
    for half in range(halves):
        rows = [side[:, half * LANES : (half + 1) * LANES]]
        for param in range(params):
            rows.extend(parts[half][param])
        whole = jnp.concatenate(rows, axis=0)
        count = LANES // width
        out_ref[half * count : (half + 1) * count] = jnp.transpose(whole).reshape(count, width, LANES)


def smooth_kernel(strength_ref, couple_ref, in_ref, out_ref, dip_scratch, *, params, tiles, rows_x, rows_y):
    depth, width, _ = in_ref.shape
    groups = LANES // depth
    halves = rows_x // groups
    side = 3 * rows_x
    rows = 3 * width
    lane = lane_ids((width, LANES))
    z = lane % depth
    low = z < depth // 2
    z_float = z.astype(jnp.float32)

    def add_source(source, field):
        message = in_ref[source]
        swapped = jnp.where(low, roll_lanes(message, -(depth // 2)), roll_lanes(message, depth // 2))
        field = list(field)
        for tile in range(tiles):
            own = low if tile == 0 else jnp.logical_not(low)
            values = jnp.where(own, message, swapped)
            at_x = jnp.broadcast_to(message[:, side + tile : side + tile + 1], (width, LANES))
            first_z = jnp.broadcast_to(
                message[:, side + tiles + tile : side + tiles + tile + 1], (width, LANES)
            )
            behind = z_float - first_z
            inside = jnp.logical_and(behind >= 0.0, behind < float(depth // 2))
            at_x = jnp.where(inside, at_x, -1.0)
            for x in range(rows_x):
                field[x] = field[x] + jnp.where(at_x == float(x), values, 0.0)
        return tuple(field)

    zero = jnp.zeros((width, LANES), jnp.float32)
    field = (zero,) * rows_x
    for source in range(depth):
        field = add_source(source, field)

    block = lane // depth
    current = []
    for param in range(params):
        current.append([])
        for half in range(halves):
            centre = zero
            for group in range(groups):
                moved = roll_lanes(field[half * groups + group], depth * (group - param - 1))
                centre = jnp.where(block == group, moved, centre)
            current[param].append(jnp.concatenate([zero, centre, zero], axis=0))

    for row in range(width):
        dip_scratch[row] = jnp.transpose(
            jnp.concatenate(
                [in_ref[:, row, :], jnp.zeros((LANES - depth, LANES), jnp.float32)], axis=0
            )
        )[:side]
    dip = []
    for half in range(halves):
        bands = []
        for band in range(3):
            merged = zero
            for group in range(groups):
                values = dip_scratch[:, band * rows_x + half * groups + group, :]
                merged = jnp.where(block == group, roll_lanes(values, depth * group), merged)
            bands.append(merged)
        dip.append(jnp.concatenate(bands, axis=0))

    lanes = lane_ids((rows, LANES))
    z = lanes % depth
    block = lanes // depth
    first = block == 0
    last = block == groups - 1
    top = z == 0
    bottom = z == depth - 1
    y = device_index() * width - width + lax.broadcasted_iota(jnp.int32, (rows, LANES), 0)
    in_grid = jnp.logical_and(y >= 0, y < rows_y)

    def from_next_x(values):
        moved = [roll_lanes(v, -depth) for v in values]
        return [
            jnp.where(last, moved[h + 1] if h + 1 < halves else 0.0, moved[h]) for h in range(halves)
        ]

    def from_prev_x(values):
        moved = [roll_lanes(v, depth) for v in values]
        return [jnp.where(first, moved[h - 1] if h > 0 else 0.0, moved[h]) for h in range(halves)]

    def from_next_y(values):
        return [pltpu.roll(v, rows - 1, 0) for v in values]

    def from_prev_y(values):
        return [pltpu.roll(v, 1, 0) for v in values]

    def masks(values):
        return [(v < -0.5, v > 0.5) for v in values]

    tilt_x = [jnp.where(d < 2.5, -1.0, jnp.where(d > 5.5, 1.0, 0.0)) for d in dip]
    tilt_y = [d - 3.0 * (t + 1.0) - 1.0 for d, t in zip(dip, tilt_x)]
    to_west = masks(from_prev_x(tilt_x))
    to_east = masks(from_next_x(tilt_x))
    to_south = masks(from_prev_y(tilt_y))
    to_north = masks(from_next_y(tilt_y))

    strengths = [jnp.full((rows, LANES), strength_ref[q], jnp.float32) for q in range(params)]
    mixing = []
    for p in range(params):
        weights = [jnp.full((rows, LANES), couple_ref[p, q], jnp.float32) for q in range(params)]
        whole = weights[0]
        for weight in weights[1:]:
            whole = whole + weight
        mixing.append([jnp.where(in_grid, weight / whole, 0.0) for weight in weights])

    for _ in range(PASSES):
        smooth = []
        for q in range(params):
            u = current[q]
            above = [jnp.where(top, 0.0, roll_lanes(v, 1)) for v in u]
            below = [jnp.where(bottom, 0.0, roll_lanes(v, -1)) for v in u]

            def plus(tilts):
                return [
                    jnp.where(neg, a, jnp.where(pos, b, v))
                    for (neg, pos), a, v, b in zip(tilts, above, u, below)
                ]

            def minus(tilts):
                return [
                    jnp.where(neg, b, jnp.where(pos, a, v))
                    for (neg, pos), a, v, b in zip(tilts, above, u, below)
                ]

            east = from_next_x(plus(to_west))
            west = from_prev_x(minus(to_east))
            north = from_next_y(plus(to_south))
            south = from_prev_y(minus(to_north))
            smooth.append(
                [
                    v + strengths[q] * (e + w + n + s - 4.0 * v)
                    for v, e, w, n, s in zip(u, east, west, north, south)
                ]
            )
        current = []
        for p in range(params):
            mixed = []
            for half in range(halves):
                value = mixing[p][0] * smooth[0][half]
                for q in range(1, params):
                    value = value + mixing[p][q] * smooth[q][half]
                mixed.append(value)
            current.append(mixed)

    gap = jnp.zeros((LANES // groups - rows, LANES), jnp.float32)
    for half in range(halves):
        pieces = []
        for p in range(params):
            pieces.extend([current[p][half], gap])
        pieces.append(jnp.zeros((LANES // groups, LANES), jnp.float32))
        turned = jnp.transpose(jnp.concatenate(pieces, axis=0))
        for group in range(groups):
            out_ref[:, half * groups + group, :] = turned[group * depth : (group + 1) * depth]


def collect_kernel(in_ref, out_ref, *, width):
    params, _, rows_x, rows_y = out_ref.shape
    groups = params + 1
    slot = LANES // groups
    step = slot // width
    halves = rows_y // LANES
    block = lane_ids((rows_x, LANES)) // slot
    for param in range(params):
        total = jnp.zeros((rows_x, rows_y), jnp.float32)
        for phase in range(step):
            wide = []
            for half in range(halves):
                merged = jnp.zeros((rows_x, LANES), jnp.float32)
                for group in range(groups):
                    values = in_ref[(half * groups + group) * step + phase]
                    merged = jnp.where(block == group, roll_lanes(values, slot * (group - param)), merged)
                wide.append(merged)
            total = total + roll_lanes(jnp.concatenate(wide, axis=1), (phase - 1) * width)
        out_ref[param, 0] = total


def fits(sensitivity, dip_class, devices):
    tiles, _, params, tile_depth, tile_columns = sensitivity.shape
    slab_depth, rows_x, rows_y = dip_class.shape
    depth = slab_depth * devices
    return (
        slab_depth == 1
        and rows_y == devices * SUBLANES
        and PASSES <= SUBLANES
        and rows_y % LANES == 0
        and tile_columns == LANES
        and rows_x == SUBLANES
        and tiles == 2
        and tiles * tile_depth == depth
        and (params + 1) * depth == LANES
        and 4 * SUBLANES == depth
    )


def shards_by_y(
    tile_bounds, tile_anchor, tile_picks, rmo_picks, sensitivity, dip_class, strength, couple
):
    tiles, rays, params, _, _ = sensitivity.shape
    _, rows_x, rows_y = dip_class.shape
    devices = lax.axis_size("cols") * lax.axis_size("par")
    width = rows_y // devices
    own_start = lax.dynamic_slice(tile_bounds, (lax.axis_index("cols"),), (1,))
    smem = pl.BlockSpec(memory_space=pltpu.SMEM)
    vmem = pl.BlockSpec(memory_space=pltpu.VMEM)
    packet = jax.ShapeDtypeStruct((devices, width, LANES), jnp.float32)
    sent = pl.pallas_call(
        source_kernel,
        out_shape=packet,
        in_specs=[smem, smem, smem, vmem, vmem, vmem],
        out_specs=vmem,
        scratch_shapes=[pltpu.VMEM((rays, LANES), jnp.float32)],
        compiler_params=pltpu.CompilerParams(vmem_limit_bytes=32 << 20),
        name="sum_rays",
    )(own_start, tile_anchor, tile_picks, rmo_picks, sensitivity, dip_class)
    received = lax.all_to_all(sent, ("cols", "par"), 0, 0)
    layers = pl.pallas_call(
        functools.partial(smooth_kernel, params=params, tiles=tiles, rows_x=rows_x, rows_y=rows_y),
        out_shape=packet,
        in_specs=[smem, smem, vmem],
        out_specs=vmem,
        scratch_shapes=[pltpu.VMEM((width, 3 * rows_x, LANES), jnp.float32)],
        compiler_params=pltpu.CompilerParams(vmem_limit_bytes=32 << 20),
        name="smooth_block",
    )(strength, couple, received)
    windows = lax.all_to_all(layers, ("cols", "par"), 0, 0)
    return pl.pallas_call(
        functools.partial(collect_kernel, width=width),
        out_shape=jax.ShapeDtypeStruct((params, 1, rows_x, rows_y), jnp.float32),
        in_specs=[vmem],
        out_specs=vmem,
        compiler_params=pltpu.CompilerParams(vmem_limit_bytes=32 << 20),
        name="collect_windows",
    )(windows)


def shards(
    tile_bounds, tile_anchor, tile_picks, rmo_picks, sensitivity, dip_class, strength, couple
):
    devices = lax.axis_size("cols") * lax.axis_size("par")
    plan = shards_by_y if fits(sensitivity, dip_class, devices) else shards_any
    return plan(
        tile_bounds, tile_anchor, tile_picks, rmo_picks, sensitivity, dip_class, strength, couple
    )


def solution(mesh):
    return jax.shard_map(
        shards,
        mesh=mesh,
        in_specs=(
            P(),
            P(("cols", "par"), None),
            P(("cols", "par")),
            P(("cols", "par"), None),
            P(("cols", "par"), None, None, None, None),
            P(("cols", "par"), None, None),
            P(),
            P(),
        ),
        out_specs=P(None, ("cols", "par"), None, None),
        check_vma=False,
    )
```

```python
import functools

import jax
import jax.numpy as jnp
from jax import lax
from jax.experimental import pallas as pl
from jax.experimental.pallas import tpu as pltpu
from jax.sharding import PartitionSpec as P

CAP = 384
PASSES = 6


def extended(block, sides, width):
    for axis, dim in sides:
        count = lax.axis_size(axis)
        forward = [(i, i + 1) for i in range(count - 1)]
        backward = [(target, source) for source, target in forward]
        low = lax.ppermute(
            lax.slice_in_dim(block, block.shape[dim] - width, None, axis=dim), axis, forward
        )
        high = lax.ppermute(lax.slice_in_dim(block, 0, width, axis=dim), axis, backward)
        block = jnp.concatenate([low, block, high], axis=dim)
    return block


def next_cells(values, along_dim):
    count = values.shape[along_dim]
    kept = lax.slice_in_dim(values, 1, count, axis=along_dim)
    zeros = jnp.zeros_like(lax.slice_in_dim(values, 0, 1, axis=along_dim))
    return jnp.concatenate([kept, zeros], axis=along_dim)


def prev_cells(values, along_dim):
    count = values.shape[along_dim]
    kept = lax.slice_in_dim(values, 0, count - 1, axis=along_dim)
    zeros = jnp.zeros_like(lax.slice_in_dim(values, 0, 1, axis=along_dim))
    return jnp.concatenate([zeros, kept], axis=along_dim)


def at_depth(padded, tilt):
    return jnp.where(tilt < 0, padded[:, :-2], jnp.where(tilt > 0, padded[:, 2:], padded[:, 1:-1]))


def smooth_pass(padded, dip_class, strength, mixing):
    centre = padded[:, 1:-1]
    tilt_across = (dip_class // 3 - 1)[None]
    tilt_along = (dip_class % 3 - 1)[None]
    east_side = at_depth(next_cells(padded, 2), tilt_across)
    west_side = at_depth(prev_cells(padded, 2), -tilt_across)
    north_side = at_depth(next_cells(padded, 3), tilt_along)
    south_side = at_depth(prev_cells(padded, 3), -tilt_along)
    laplace = east_side + west_side + north_side + south_side - 4.0 * centre
    smooth = centre + strength[:, None, None, None] * laplace
    return jnp.tensordot(mixing, smooth, axes=1, precision=lax.Precision.HIGHEST)


def shards_any(
    tile_bounds, tile_anchor, tile_picks, rmo_picks, sensitivity, dip_class, strength, couple
):
    tile_count, ray_count, param_count, depth_cells, tile_columns = sensitivity.shape
    col_devices = lax.axis_size("cols")
    par_devices = lax.axis_size("par")
    slab_depth, rows_x, rows_y = dip_class.shape
    total_depth = slab_depth * col_devices * par_devices
    live = jnp.arange(ray_count, dtype=jnp.int32)[None, :] < tile_picks[:, None]
    ray_weight = jnp.where(live, rmo_picks, jnp.zeros_like(rmo_picks))
    contribution = jnp.einsum(
        "tr,trk->tk",
        ray_weight,
        sensitivity.reshape(tile_count, ray_count, -1),
        preferred_element_type=jnp.float32,
    )
    contribution = contribution.reshape(tile_count, param_count, depth_cells, tile_columns)

    def add_tile(tile_number, gradient):
        anchor = (jnp.int32(0), tile_anchor[tile_number, 0], tile_anchor[tile_number, 1])
        current = lax.dynamic_slice(gradient, anchor, (param_count, depth_cells, tile_columns))
        return lax.dynamic_update_slice(gradient, current + contribution[tile_number], anchor)

    gradient = jnp.zeros((param_count, total_depth, CAP), jnp.float32)
    gradient = lax.fori_loop(0, tile_count, add_tile, gradient)
    blocks = gradient.reshape(param_count, col_devices, par_devices, slab_depth, CAP)
    reduced = lax.psum_scatter(blocks, "par", scatter_dimension=2, tiled=True)
    summed = lax.all_to_all(reduced, "cols", split_axis=1, concat_axis=4, tiled=True)
    padded_slots = summed.reshape(param_count, slab_depth, col_devices * CAP)
    columns = rows_x * rows_y
    column_ids = jnp.arange(columns, dtype=jnp.int32)
    starts = tile_bounds[:-1]
    below = starts[None, :] <= column_ids[:, None]
    owner_tile = jnp.sum(below.astype(jnp.int32), axis=1) - 1
    tile_start = jnp.max(jnp.where(below, starts[None, :], jnp.zeros_like(starts)[None, :]), axis=1)
    slot_index = owner_tile * CAP + column_ids - tile_start
    field = jnp.take(padded_slots, slot_index, axis=2).reshape(
        param_count, slab_depth, rows_x, rows_y
    )
    mixing = couple / jnp.sum(couple, axis=1, keepdims=True)
    for _ in range(PASSES):
        padded = extended(field, ((("cols", "par"), 1),), 1)
        field = smooth_pass(padded, dip_class, strength, mixing)
    return field


LANES = 128
SUBLANES = 8
RAY_CHUNKS = 4


def device_index():
    return lax.axis_index("cols") * lax.axis_size("par") + lax.axis_index("par")


def lane_ids(shape):
    return lax.broadcasted_iota(jnp.int32, shape, len(shape) - 1)


def roll_lanes(values, shift):
    width = values.shape[-1]
    shift = shift % width
    return values if shift == 0 else pltpu.roll(values, shift, values.ndim - 1)


def source_kernel(
    bounds_hbm, anchor_hbm, picks_hbm, rmo_hbm, sens_hbm, dip_hbm, strength_hbm, couple_hbm,
    out_ref, factor_ref,
    bounds_ref, anchor_ref, picks_ref, rmo_ref, sens_ref, dip_ref, strength_ref, couple_ref,
    weight_ref, small_sems, sens_sems,
):
    tiles, rays, params, tile_depth, tile_columns = sens_ref.shape
    _, rows_x, rows_y = dip_ref.shape
    devices, width, _ = out_ref.shape
    halves = rows_y // LANES
    per_tile = sens_sems.shape[1]
    chunk = rays // per_tile
    small = [
        pltpu.make_async_copy(hbm, ref, small_sems.at[number])
        for number, (hbm, ref) in enumerate(
            [
                (picks_hbm, picks_ref),
                (rmo_hbm, rmo_ref),
                (bounds_hbm, bounds_ref),
                (anchor_hbm, anchor_ref),
                (dip_hbm, dip_ref),
                (strength_hbm, strength_ref),
                (couple_hbm, couple_ref),
            ]
        )
    ]
    large = [
        [
            pltpu.make_async_copy(
                sens_hbm.at[tile, pl.ds(part * chunk, chunk)],
                sens_ref.at[tile, pl.ds(part * chunk, chunk)],
                sens_sems.at[tile, part],
            )
            for part in range(per_tile)
        ]
        for tile in range(tiles)
    ]
    for copy in small[:2]:
        copy.start()
    for row in large:
        for copy in row:
            copy.start()
    for copy in small[2:]:
        copy.start()

    diagonal = lax.broadcasted_iota(jnp.int32, (rays, rays), 0) == lane_ids((rays, rays))
    for copy in small[:2]:
        copy.wait()
    for tile in range(tiles):
        live = lane_ids((1, rays)) < picks_ref[tile]
        weight = jnp.where(live, rmo_ref[tile : tile + 1, :].astype(jnp.float32), 0.0)
        column = jnp.sum(jnp.where(diagonal, weight, 0.0), axis=1, keepdims=True)
        weight_ref[tile] = jnp.broadcast_to(column, (rays, LANES))
    sums = []
    for tile in range(tiles):
        total = jnp.zeros((params, tile_depth, tile_columns), jnp.float32)
        for ray in range(rays):
            if ray % chunk == 0:
                large[tile][ray // chunk].wait()
            weight = weight_ref[tile, ray : ray + 1, :]
            total = total + weight[None] * sens_ref[tile, ray].astype(jnp.float32)
        sums.append(total)
    for copy in small[2:]:
        copy.wait()

    parts = [[[None] * tiles for _ in range(params)] for _ in range(halves)]
    x_rows, depth_rows = [], []
    y_ids = lane_ids((1, rows_y))
    for tile in range(tiles):
        depth_first = anchor_ref[tile, 0]
        first = bounds_ref[lax.axis_index("cols")] + anchor_ref[tile, 1]
        first_x = first // rows_y
        first_y = first - first_x * rows_y
        half_of = first_y // LANES
        lane_first = first_y - half_of * LANES
        past = lane_ids((1, LANES)) >= lane_first
        for param in range(params):
            turned = pltpu.roll(sums[tile][param], lax.rem(depth_first, tile_depth), 0)
            turned = pltpu.roll(turned, lane_first, 1)
            for half in range(halves):
                after = lax.rem(half_of + 1, halves)
                kept = jnp.logical_or(
                    jnp.logical_and(past, half_of == half),
                    jnp.logical_and(jnp.logical_not(past), after == half),
                )
                parts[half][param][tile] = jnp.where(kept, turned, 0.0)
        x_rows.append((first_x + (y_ids < first_y).astype(jnp.int32)).astype(jnp.float32))
        depth_rows.append(jnp.full((1, rows_y), depth_first, jnp.int32).astype(jnp.float32))
    notes = jnp.concatenate(
        [jnp.zeros((3 * width, rows_y), jnp.float32)]
        + x_rows
        + depth_rows
        + [jnp.zeros((width - 2 * tiles, rows_y), jnp.float32)],
        axis=0,
    )
    dip = dip_ref[0].astype(jnp.float32)
    in_window = lane_ids((rows_x, LANES)) < 3 * width
    count = LANES // width
    for half in range(halves):
        rows = [notes[:, half * LANES : (half + 1) * LANES]]
        for param in range(params):
            rows.extend(parts[half][param])
        turned = jnp.transpose(jnp.concatenate(rows, axis=0))
        for place in range(count):
            device = half * count + place
            window = roll_lanes(dip, width - device * width)[:, :LANES]
            out_ref[device] = jnp.where(in_window, window, turned[place * width : (place + 1) * width])

    for q in range(params):
        factor_ref[q : q + 1, :] = jnp.full((1, LANES), strength_ref[q], jnp.float32)
    for p in range(params):
        weights = [jnp.full((1, LANES), couple_ref[p, q], jnp.float32) for q in range(params)]
        whole = weights[0]
        for weight in weights[1:]:
            whole = whole + weight
        for q in range(params):
            row = (p + 1) * params + q
            factor_ref[row : row + 1, :] = weights[q] / whole


def smooth_kernel(factor_ref, in_ref, out_ref, *, params, tiles, rows_x, rows_y):
    depth, width, _ = in_ref.shape
    groups = LANES // depth
    halves = rows_x // groups
    rows = 3 * width
    side = rows
    lane = lane_ids((width, LANES))
    z = lane % depth
    low = z < depth // 2
    z_float = z.astype(jnp.float32)

    def add_source(source, field):
        message = in_ref[source]
        swapped = jnp.where(low, roll_lanes(message, -(depth // 2)), roll_lanes(message, depth // 2))
        field = list(field)
        for tile in range(tiles):
            own = low if tile == 0 else jnp.logical_not(low)
            values = jnp.where(own, message, swapped)
            at_x = jnp.broadcast_to(message[:, side + tile : side + tile + 1], (width, LANES))
            first_z = jnp.broadcast_to(
                message[:, side + tiles + tile : side + tiles + tile + 1], (width, LANES)
            )
            behind = z_float - first_z
            inside = jnp.logical_and(behind >= 0.0, behind < float(depth // 2))
            at_x = jnp.where(inside, at_x, -1.0)
            for x in range(rows_x):
                field[x] = field[x] + jnp.where(at_x == float(x), values, 0.0)
        return tuple(field)

    zero = jnp.zeros((width, LANES), jnp.float32)
    field = (zero,) * rows_x
    for source in range(depth):
        field = add_source(source, field)

    block = lane // depth
    current = []
    for param in range(params):
        current.append([])
        for half in range(halves):
            centre = zero
            for group in range(groups):
                moved = roll_lanes(field[half * groups + group], depth * (group - param - 1))
                centre = jnp.where(block == group, moved, centre)
            current[param].append(jnp.concatenate([zero, centre, zero], axis=0))

    dip = []
    for half in range(halves):
        layers = [in_ref[:, half * groups + group, :] for group in range(groups)]
        dip.append(jnp.transpose(jnp.concatenate(layers, axis=0))[:rows])

    lanes = lane_ids((rows, LANES))
    z = lanes % depth
    block = lanes // depth
    first = block == 0
    last = block == groups - 1
    top = z == 0
    bottom = z == depth - 1
    y = device_index() * width - width + lax.broadcasted_iota(jnp.int32, (rows, LANES), 0)
    in_grid = jnp.logical_and(y >= 0, y < rows_y)

    def from_next_x(values):
        moved = [roll_lanes(v, -depth) for v in values]
        return [
            jnp.where(last, moved[h + 1] if h + 1 < halves else 0.0, moved[h]) for h in range(halves)
        ]

    def from_prev_x(values):
        moved = [roll_lanes(v, depth) for v in values]
        return [jnp.where(first, moved[h - 1] if h > 0 else 0.0, moved[h]) for h in range(halves)]

    def from_next_y(values):
        return [pltpu.roll(v, rows - 1, 0) for v in values]

    def from_prev_y(values):
        return [pltpu.roll(v, 1, 0) for v in values]

    def masks(values):
        return [(v < -0.5, v > 0.5) for v in values]

    tilt_x = [jnp.where(d < 2.5, -1.0, jnp.where(d > 5.5, 1.0, 0.0)) for d in dip]
    tilt_y = [d - 3.0 * (t + 1.0) - 1.0 for d, t in zip(dip, tilt_x)]
    to_west = masks(from_prev_x(tilt_x))
    to_east = masks(from_next_x(tilt_x))
    to_south = masks(from_prev_y(tilt_y))
    to_north = masks(from_next_y(tilt_y))

    def factor(row):
        return jnp.broadcast_to(factor_ref[row : row + 1, :], (rows, LANES))

    strengths = [factor(q) for q in range(params)]
    mixing = [
        [jnp.where(in_grid, factor((p + 1) * params + q), 0.0) for q in range(params)]
        for p in range(params)
    ]

    for _ in range(PASSES):
        smooth = []
        for q in range(params):
            u = current[q]
            above = [jnp.where(top, 0.0, roll_lanes(v, 1)) for v in u]
            below = [jnp.where(bottom, 0.0, roll_lanes(v, -1)) for v in u]

            def plus(tilts):
                return [
                    jnp.where(neg, a, jnp.where(pos, b, v))
                    for (neg, pos), a, v, b in zip(tilts, above, u, below)
                ]

            def minus(tilts):
                return [
                    jnp.where(neg, b, jnp.where(pos, a, v))
                    for (neg, pos), a, v, b in zip(tilts, above, u, below)
                ]

            east = from_next_x(plus(to_west))
            west = from_prev_x(minus(to_east))
            north = from_next_y(plus(to_south))
            south = from_prev_y(minus(to_north))
            smooth.append(
                [
                    v + strengths[q] * (e + w + n + s - 4.0 * v)
                    for v, e, w, n, s in zip(u, east, west, north, south)
                ]
            )
        current = []
        for p in range(params):
            mixed = []
            for half in range(halves):
                value = mixing[p][0] * smooth[0][half]
                for q in range(1, params):
                    value = value + mixing[p][q] * smooth[q][half]
                mixed.append(value)
            current.append(mixed)

    pieces = []
    for half in range(halves):
        for p in range(params):
            pieces.append(current[p][half][width - PASSES : 2 * width + PASSES])
    used = halves * params * (width + 2 * PASSES)
    pieces.append(jnp.zeros((LANES - used, LANES), jnp.float32))
    turned = jnp.transpose(jnp.concatenate(pieces, axis=0))
    for group in range(groups):
        out_ref[:, group, :] = turned[group * depth : (group + 1) * depth]


def collect_kernel(in_ref, out_ref, *, width):
    params, _, rows_x, rows_y = out_ref.shape
    sources, groups, _ = in_ref.shape
    span = width + 2 * PASSES
    halves = rows_x // groups
    lane = lane_ids((rows_x, LANES))
    totals = [[jnp.zeros((rows_x, LANES), jnp.float32) for _ in range(rows_y // LANES)] for _ in range(params)]
    for source in range(sources):
        message = in_ref[source]
        stacked = jnp.concatenate(
            [roll_lanes(message, -half * params * span) for half in range(halves)], axis=0
        )
        first = source * width - PASSES
        for param in range(params):
            placed = roll_lanes(stacked, first - param * span)
            for column in range(rows_y // LANES):
                low, high = first - column * LANES, first - column * LANES + span
                if high <= 0 or low >= LANES:
                    continue
                inside = jnp.logical_and(lane >= low, lane < high)
                totals[param][column] = totals[param][column] + jnp.where(inside, placed, 0.0)
    for param in range(params):
        for column in range(rows_y // LANES):
            out_ref[param, 0, :, column * LANES : (column + 1) * LANES] = totals[param][column]


def fits(sensitivity, dip_class, devices):
    tiles, rays, params, tile_depth, tile_columns = sensitivity.shape
    slab_depth, rows_x, rows_y = dip_class.shape
    depth = slab_depth * devices
    return (
        slab_depth == 1
        and rows_y == devices * SUBLANES
        and PASSES <= SUBLANES
        and rows_y % LANES == 0
        and tile_columns == LANES
        and rows_x == SUBLANES
        and tiles == 2
        and tiles * tile_depth == depth
        and (params + 1) * depth == LANES
        and 4 * SUBLANES == depth
        and rays % RAY_CHUNKS == 0
        and rows_x * params * (SUBLANES + 2 * PASSES) <= 4 * LANES
    )


def shards_by_y(
    tile_bounds, tile_anchor, tile_picks, rmo_picks, sensitivity, dip_class, strength, couple
):
    tiles, rays, params, _, _ = sensitivity.shape
    _, rows_x, rows_y = dip_class.shape
    devices = lax.axis_size("cols") * lax.axis_size("par")
    width = rows_y // devices
    groups = LANES // devices
    hbm = pl.BlockSpec(memory_space=pltpu.HBM)
    vmem = pl.BlockSpec(memory_space=pltpu.VMEM)
    arguments = (
        tile_bounds, tile_anchor, tile_picks, rmo_picks, sensitivity, dip_class, strength, couple
    )
    homes = (
        pltpu.SMEM, pltpu.SMEM, pltpu.SMEM, pltpu.VMEM, pltpu.VMEM, pltpu.VMEM, pltpu.SMEM, pltpu.SMEM
    )
    sent, factors = pl.pallas_call(
        source_kernel,
        out_shape=(
            jax.ShapeDtypeStruct((devices, width, LANES), jnp.float32),
            jax.ShapeDtypeStruct(((params + 1) * params, LANES), jnp.float32),
        ),
        in_specs=[hbm] * len(arguments),
        out_specs=(vmem, vmem),
        scratch_shapes=[home(array.shape, array.dtype) for home, array in zip(homes, arguments)]
        + [
            pltpu.VMEM((tiles, rays, LANES), jnp.float32),
            pltpu.SemaphoreType.DMA((len(arguments) - 1,)),
            pltpu.SemaphoreType.DMA((tiles, RAY_CHUNKS)),
        ],
        compiler_params=pltpu.CompilerParams(vmem_limit_bytes=32 << 20),
        name="sum_rays",
    )(*arguments)
    received = lax.all_to_all(sent, ("cols", "par"), 0, 0)
    layers = pl.pallas_call(
        functools.partial(smooth_kernel, params=params, tiles=tiles, rows_x=rows_x, rows_y=rows_y),
        out_shape=jax.ShapeDtypeStruct((devices, groups, LANES), jnp.float32),
        in_specs=[vmem, vmem],
        out_specs=vmem,
        compiler_params=pltpu.CompilerParams(vmem_limit_bytes=32 << 20),
        name="smooth_block",
    )(factors, received)
    windows = lax.all_to_all(layers, ("cols", "par"), 0, 0)
    return pl.pallas_call(
        functools.partial(collect_kernel, width=width),
        out_shape=jax.ShapeDtypeStruct((params, 1, rows_x, rows_y), jnp.float32),
        in_specs=[vmem],
        out_specs=vmem,
        compiler_params=pltpu.CompilerParams(vmem_limit_bytes=32 << 20),
        name="collect_windows",
    )(windows)


def shards(
    tile_bounds, tile_anchor, tile_picks, rmo_picks, sensitivity, dip_class, strength, couple
):
    devices = lax.axis_size("cols") * lax.axis_size("par")
    plan = shards_by_y if fits(sensitivity, dip_class, devices) else shards_any
    return plan(
        tile_bounds, tile_anchor, tile_picks, rmo_picks, sensitivity, dip_class, strength, couple
    )


def solution(mesh):
    return jax.shard_map(
        shards,
        mesh=mesh,
        in_specs=(
            P(),
            P(("cols", "par"), None),
            P(("cols", "par")),
            P(("cols", "par"), None),
            P(("cols", "par"), None, None, None, None),
            P(("cols", "par"), None, None),
            P(),
            P(),
        ),
        out_specs=P(None, ("cols", "par"), None, None),
        check_vma=False,
    )
```

```python
import functools

import jax
import jax.numpy as jnp
from jax import lax
from jax.experimental import pallas as pl
from jax.experimental.pallas import tpu as pltpu
from jax.sharding import PartitionSpec as P

CAP = 384
PASSES = 6


def extended(block, sides, width):
    for axis, dim in sides:
        count = lax.axis_size(axis)
        forward = [(i, i + 1) for i in range(count - 1)]
        backward = [(target, source) for source, target in forward]
        low = lax.ppermute(
            lax.slice_in_dim(block, block.shape[dim] - width, None, axis=dim), axis, forward
        )
        high = lax.ppermute(lax.slice_in_dim(block, 0, width, axis=dim), axis, backward)
        block = jnp.concatenate([low, block, high], axis=dim)
    return block


def next_cells(values, along_dim):
    count = values.shape[along_dim]
    kept = lax.slice_in_dim(values, 1, count, axis=along_dim)
    zeros = jnp.zeros_like(lax.slice_in_dim(values, 0, 1, axis=along_dim))
    return jnp.concatenate([kept, zeros], axis=along_dim)


def prev_cells(values, along_dim):
    count = values.shape[along_dim]
    kept = lax.slice_in_dim(values, 0, count - 1, axis=along_dim)
    zeros = jnp.zeros_like(lax.slice_in_dim(values, 0, 1, axis=along_dim))
    return jnp.concatenate([zeros, kept], axis=along_dim)


def at_depth(padded, tilt):
    return jnp.where(tilt < 0, padded[:, :-2], jnp.where(tilt > 0, padded[:, 2:], padded[:, 1:-1]))


def smooth_pass(padded, dip_class, strength, mixing):
    centre = padded[:, 1:-1]
    tilt_across = (dip_class // 3 - 1)[None]
    tilt_along = (dip_class % 3 - 1)[None]
    east_side = at_depth(next_cells(padded, 2), tilt_across)
    west_side = at_depth(prev_cells(padded, 2), -tilt_across)
    north_side = at_depth(next_cells(padded, 3), tilt_along)
    south_side = at_depth(prev_cells(padded, 3), -tilt_along)
    laplace = east_side + west_side + north_side + south_side - 4.0 * centre
    smooth = centre + strength[:, None, None, None] * laplace
    return jnp.tensordot(mixing, smooth, axes=1, precision=lax.Precision.HIGHEST)


def shards_any(
    tile_bounds, tile_anchor, tile_picks, rmo_picks, sensitivity, dip_class, strength, couple
):
    tile_count, ray_count, param_count, depth_cells, tile_columns = sensitivity.shape
    col_devices = lax.axis_size("cols")
    par_devices = lax.axis_size("par")
    slab_depth, rows_x, rows_y = dip_class.shape
    total_depth = slab_depth * col_devices * par_devices
    live = jnp.arange(ray_count, dtype=jnp.int32)[None, :] < tile_picks[:, None]
    ray_weight = jnp.where(live, rmo_picks, jnp.zeros_like(rmo_picks))
    contribution = jnp.einsum(
        "tr,trk->tk",
        ray_weight,
        sensitivity.reshape(tile_count, ray_count, -1),
        preferred_element_type=jnp.float32,
    )
    contribution = contribution.reshape(tile_count, param_count, depth_cells, tile_columns)

    def add_tile(tile_number, gradient):
        anchor = (jnp.int32(0), tile_anchor[tile_number, 0], tile_anchor[tile_number, 1])
        current = lax.dynamic_slice(gradient, anchor, (param_count, depth_cells, tile_columns))
        return lax.dynamic_update_slice(gradient, current + contribution[tile_number], anchor)

    gradient = jnp.zeros((param_count, total_depth, CAP), jnp.float32)
    gradient = lax.fori_loop(0, tile_count, add_tile, gradient)
    blocks = gradient.reshape(param_count, col_devices, par_devices, slab_depth, CAP)
    reduced = lax.psum_scatter(blocks, "par", scatter_dimension=2, tiled=True)
    summed = lax.all_to_all(reduced, "cols", split_axis=1, concat_axis=4, tiled=True)
    padded_slots = summed.reshape(param_count, slab_depth, col_devices * CAP)
    columns = rows_x * rows_y
    column_ids = jnp.arange(columns, dtype=jnp.int32)
    starts = tile_bounds[:-1]
    below = starts[None, :] <= column_ids[:, None]
    owner_tile = jnp.sum(below.astype(jnp.int32), axis=1) - 1
    tile_start = jnp.max(jnp.where(below, starts[None, :], jnp.zeros_like(starts)[None, :]), axis=1)
    slot_index = owner_tile * CAP + column_ids - tile_start
    field = jnp.take(padded_slots, slot_index, axis=2).reshape(
        param_count, slab_depth, rows_x, rows_y
    )
    mixing = couple / jnp.sum(couple, axis=1, keepdims=True)
    for _ in range(PASSES):
        padded = extended(field, ((("cols", "par"), 1),), 1)
        field = smooth_pass(padded, dip_class, strength, mixing)
    return field


LANES = 128
SUBLANES = 8
RAY_CHUNKS = 4


def device_index():
    return lax.axis_index("cols") * lax.axis_size("par") + lax.axis_index("par")


def lane_ids(shape):
    return lax.broadcasted_iota(jnp.int32, shape, len(shape) - 1)


def roll_lanes(values, shift):
    width = values.shape[-1]
    shift = shift % width
    return values if shift == 0 else pltpu.roll(values, shift, values.ndim - 1)


def source_kernel(
    bounds_hbm, anchor_hbm, picks_hbm, rmo_hbm, sens_hbm, dip_hbm, strength_hbm, couple_hbm,
    out_ref,
    bounds_ref, anchor_ref, picks_ref, rmo_ref, sens_ref, dip_ref, strength_ref, couple_ref,
    weight_ref, small_sems, sens_sems,
):
    tiles, rays, params, tile_depth, tile_columns = sens_ref.shape
    _, rows_x, rows_y = dip_ref.shape
    devices, width, _ = out_ref.shape
    halves = rows_y // LANES
    per_tile = sens_sems.shape[1]
    chunk = rays // per_tile
    small = [
        pltpu.make_async_copy(hbm, ref, small_sems.at[number])
        for number, (hbm, ref) in enumerate(
            [
                (picks_hbm, picks_ref),
                (rmo_hbm, rmo_ref),
                (bounds_hbm, bounds_ref),
                (anchor_hbm, anchor_ref),
                (dip_hbm, dip_ref),
                (strength_hbm, strength_ref),
                (couple_hbm, couple_ref),
            ]
        )
    ]
    large = [
        [
            pltpu.make_async_copy(
                sens_hbm.at[tile, pl.ds(part * chunk, chunk)],
                sens_ref.at[tile, pl.ds(part * chunk, chunk)],
                sens_sems.at[tile, part],
            )
            for part in range(per_tile)
        ]
        for tile in range(tiles)
    ]
    for copy in small[:2]:
        copy.start()
    for row in large:
        for copy in row:
            copy.start()
    for copy in small[2:]:
        copy.start()

    diagonal = lax.broadcasted_iota(jnp.int32, (rays, rays), 0) == lane_ids((rays, rays))
    for copy in small[:2]:
        copy.wait()
    for tile in range(tiles):
        live = lane_ids((1, rays)) < picks_ref[tile]
        weight = jnp.where(live, rmo_ref[tile : tile + 1, :].astype(jnp.float32), 0.0)
        column = jnp.sum(jnp.where(diagonal, weight, 0.0), axis=1, keepdims=True)
        weight_ref[tile] = jnp.broadcast_to(column, (rays, LANES))
    sums = []
    for tile in range(tiles):
        total = jnp.zeros((params, tile_depth, tile_columns), jnp.float32)
        for ray in range(rays):
            if ray % chunk == 0:
                large[tile][ray // chunk].wait()
            weight = weight_ref[tile, ray : ray + 1, :]
            total = total + weight[None] * sens_ref[tile, ray].astype(jnp.float32)
        sums.append(total)
    for copy in small[2:]:
        copy.wait()

    parts = [[[None] * tiles for _ in range(params)] for _ in range(halves)]
    x_rows, depth_rows = [], []
    y_ids = lane_ids((1, rows_y))
    for tile in range(tiles):
        depth_first = anchor_ref[tile, 0]
        first = bounds_ref[lax.axis_index("cols")] + anchor_ref[tile, 1]
        first_x = first // rows_y
        first_y = first - first_x * rows_y
        half_of = first_y // LANES
        lane_first = first_y - half_of * LANES
        past = lane_ids((1, LANES)) >= lane_first
        for param in range(params):
            turned = pltpu.roll(sums[tile][param], lax.rem(depth_first, tile_depth), 0)
            turned = pltpu.roll(turned, lane_first, 1)
            for half in range(halves):
                after = lax.rem(half_of + 1, halves)
                kept = jnp.logical_or(
                    jnp.logical_and(past, half_of == half),
                    jnp.logical_and(jnp.logical_not(past), after == half),
                )
                parts[half][param][tile] = jnp.where(kept, turned, 0.0)
        x_rows.append((first_x + (y_ids < first_y).astype(jnp.int32)).astype(jnp.float32))
        depth_rows.append(jnp.full((1, rows_y), depth_first, jnp.int32).astype(jnp.float32))
    place_in_packet = lax.rem(y_ids, width)

    def packet_lane(values):
        lane = jnp.zeros((1, rows_y), jnp.float32)
        for q, value in enumerate(values):
            lane = jnp.where(place_in_packet == q, value, lane)
        return lane

    factor_rows = [packet_lane([strength_ref[q] for q in range(params)])]
    for p in range(params):
        weights = [jnp.full((1, rows_y), couple_ref[p, q], jnp.float32) for q in range(params)]
        whole = weights[0]
        for weight in weights[1:]:
            whole = whole + weight
        factor_rows.append(packet_lane([weight / whole for weight in weights]))
    notes = jnp.concatenate(
        [jnp.zeros((3 * width, rows_y), jnp.float32)] + x_rows + depth_rows + factor_rows, axis=0
    )
    dip = dip_ref[0].astype(jnp.float32)
    in_window = lane_ids((rows_x, LANES)) < 3 * width
    count = LANES // width
    for half in range(halves):
        rows = [notes[:, half * LANES : (half + 1) * LANES]]
        for param in range(params):
            rows.extend(parts[half][param])
        turned = jnp.transpose(jnp.concatenate(rows, axis=0))
        for place in range(count):
            device = half * count + place
            window = roll_lanes(dip, width - device * width)[:, :LANES]
            out_ref[device] = jnp.where(in_window, window, turned[place * width : (place + 1) * width])


def smooth_kernel(in_ref, out_ref, *, params, tiles, rows_x, rows_y):
    depth, width, _ = in_ref.shape
    groups = LANES // depth
    halves = rows_x // groups
    rows = 3 * width
    side = rows
    lane = lane_ids((width, LANES))
    z = lane % depth
    low = z < depth // 2
    z_float = z.astype(jnp.float32)

    def add_source(source, field):
        message = in_ref[source]
        swapped = jnp.where(low, roll_lanes(message, -(depth // 2)), roll_lanes(message, depth // 2))
        field = list(field)
        for tile in range(tiles):
            own = low if tile == 0 else jnp.logical_not(low)
            values = jnp.where(own, message, swapped)
            at_x = jnp.broadcast_to(message[:, side + tile : side + tile + 1], (width, LANES))
            first_z = jnp.broadcast_to(
                message[:, side + tiles + tile : side + tiles + tile + 1], (width, LANES)
            )
            behind = z_float - first_z
            inside = jnp.logical_and(behind >= 0.0, behind < float(depth // 2))
            at_x = jnp.where(inside, at_x, -1.0)
            for x in range(rows_x):
                field[x] = field[x] + jnp.where(at_x == float(x), values, 0.0)
        return tuple(field)

    zero = jnp.zeros((width, LANES), jnp.float32)
    field = (zero,) * rows_x
    for source in range(depth):
        field = add_source(source, field)

    block = lane // depth
    current = []
    for param in range(params):
        current.append([])
        for half in range(halves):
            centre = zero
            for group in range(groups):
                moved = roll_lanes(field[half * groups + group], depth * (group - param - 1))
                centre = jnp.where(block == group, moved, centre)
            current[param].append(jnp.concatenate([zero, centre, zero], axis=0))

    dip = []
    for half in range(halves):
        layers = [in_ref[:, half * groups + group, :] for group in range(groups)]
        dip.append(jnp.transpose(jnp.concatenate(layers, axis=0))[:rows])

    lanes = lane_ids((rows, LANES))
    z = lanes % depth
    block = lanes // depth
    first = block == 0
    last = block == groups - 1
    top = z == 0
    bottom = z == depth - 1
    y = device_index() * width - width + lax.broadcasted_iota(jnp.int32, (rows, LANES), 0)
    in_grid = jnp.logical_and(y >= 0, y < rows_y)

    def from_next_x(values):
        moved = [roll_lanes(v, -depth) for v in values]
        return [
            jnp.where(last, moved[h + 1] if h + 1 < halves else 0.0, moved[h]) for h in range(halves)
        ]

    def from_prev_x(values):
        moved = [roll_lanes(v, depth) for v in values]
        return [jnp.where(first, moved[h - 1] if h > 0 else 0.0, moved[h]) for h in range(halves)]

    def from_next_y(values):
        return [pltpu.roll(v, rows - 1, 0) for v in values]

    def from_prev_y(values):
        return [pltpu.roll(v, 1, 0) for v in values]

    def masks(values):
        return [(v < -0.5, v > 0.5) for v in values]

    tilt_x = [jnp.where(d < 2.5, -1.0, jnp.where(d > 5.5, 1.0, 0.0)) for d in dip]
    tilt_y = [d - 3.0 * (t + 1.0) - 1.0 for d, t in zip(dip, tilt_x)]
    to_west = masks(from_prev_x(tilt_x))
    to_east = masks(from_next_x(tilt_x))
    to_south = masks(from_prev_y(tilt_y))
    to_north = masks(from_next_y(tilt_y))

    def factor(lane, q):
        at = side + 2 * tiles + lane
        return jnp.broadcast_to(in_ref[0, q : q + 1, at : at + 1], (rows, LANES))

    strengths = [factor(0, q) for q in range(params)]
    mixing = [
        [jnp.where(in_grid, factor(p + 1, q), 0.0) for q in range(params)] for p in range(params)
    ]

    for _ in range(PASSES):
        smooth = []
        for q in range(params):
            u = current[q]
            above = [jnp.where(top, 0.0, roll_lanes(v, 1)) for v in u]
            below = [jnp.where(bottom, 0.0, roll_lanes(v, -1)) for v in u]

            def plus(tilts):
                return [
                    jnp.where(neg, a, jnp.where(pos, b, v))
                    for (neg, pos), a, v, b in zip(tilts, above, u, below)
                ]

            def minus(tilts):
                return [
                    jnp.where(neg, b, jnp.where(pos, a, v))
                    for (neg, pos), a, v, b in zip(tilts, above, u, below)
                ]

            east = from_next_x(plus(to_west))
            west = from_prev_x(minus(to_east))
            north = from_next_y(plus(to_south))
            south = from_prev_y(minus(to_north))
            smooth.append(
                [
                    v + strengths[q] * (e + w + n + s - 4.0 * v)
                    for v, e, w, n, s in zip(u, east, west, north, south)
                ]
            )
        current = []
        for p in range(params):
            mixed = []
            for half in range(halves):
                value = mixing[p][0] * smooth[0][half]
                for q in range(1, params):
                    value = value + mixing[p][q] * smooth[q][half]
                mixed.append(value)
            current.append(mixed)

    pieces = []
    for half in range(halves):
        for p in range(params):
            pieces.append(current[p][half][width - PASSES : 2 * width + PASSES])
    used = halves * params * (width + 2 * PASSES)
    pieces.append(jnp.zeros((LANES - used, LANES), jnp.float32))
    turned = jnp.transpose(jnp.concatenate(pieces, axis=0))
    for group in range(groups):
        out_ref[:, group, :] = turned[group * depth : (group + 1) * depth]


def collect_kernel(in_ref, out_ref, *, width):
    params, _, rows_x, rows_y = out_ref.shape
    sources, groups, _ = in_ref.shape
    span = width + 2 * PASSES
    halves = rows_x // groups
    lane = lane_ids((rows_x, LANES))
    totals = [[jnp.zeros((rows_x, LANES), jnp.float32) for _ in range(rows_y // LANES)] for _ in range(params)]
    for source in range(sources):
        message = in_ref[source]
        stacked = jnp.concatenate(
            [roll_lanes(message, -half * params * span) for half in range(halves)], axis=0
        )
        first = source * width - PASSES
        for param in range(params):
            placed = roll_lanes(stacked, first - param * span)
            for column in range(rows_y // LANES):
                low, high = first - column * LANES, first - column * LANES + span
                if high <= 0 or low >= LANES:
                    continue
                inside = jnp.logical_and(lane >= low, lane < high)
                totals[param][column] = totals[param][column] + jnp.where(inside, placed, 0.0)
    for param in range(params):
        for column in range(rows_y // LANES):
            out_ref[param, 0, :, column * LANES : (column + 1) * LANES] = totals[param][column]


def fits(sensitivity, dip_class, devices):
    tiles, rays, params, tile_depth, tile_columns = sensitivity.shape
    slab_depth, rows_x, rows_y = dip_class.shape
    depth = slab_depth * devices
    return (
        slab_depth == 1
        and rows_y == devices * SUBLANES
        and PASSES <= SUBLANES
        and rows_y % LANES == 0
        and tile_columns == LANES
        and rows_x == SUBLANES
        and tiles == 2
        and tiles * tile_depth == depth
        and (params + 1) * depth == LANES
        and 3 * SUBLANES + 2 * tiles + params + 1 == depth
        and rays % RAY_CHUNKS == 0
        and rows_x * params * (SUBLANES + 2 * PASSES) <= 4 * LANES
    )


def shards_by_y(
    tile_bounds, tile_anchor, tile_picks, rmo_picks, sensitivity, dip_class, strength, couple
):
    tiles, rays, params, _, _ = sensitivity.shape
    _, rows_x, rows_y = dip_class.shape
    devices = lax.axis_size("cols") * lax.axis_size("par")
    width = rows_y // devices
    groups = LANES // devices
    hbm = pl.BlockSpec(memory_space=pltpu.HBM)
    vmem = pl.BlockSpec(memory_space=pltpu.VMEM)
    arguments = (
        tile_bounds, tile_anchor, tile_picks, rmo_picks, sensitivity, dip_class, strength, couple
    )
    homes = (
        pltpu.SMEM, pltpu.SMEM, pltpu.SMEM, pltpu.VMEM, pltpu.VMEM, pltpu.VMEM, pltpu.SMEM, pltpu.SMEM
    )
    sent = pl.pallas_call(
        source_kernel,
        out_shape=jax.ShapeDtypeStruct((devices, width, LANES), jnp.float32),
        in_specs=[hbm] * len(arguments),
        out_specs=vmem,
        scratch_shapes=[home(array.shape, array.dtype) for home, array in zip(homes, arguments)]
        + [
            pltpu.VMEM((tiles, rays, LANES), jnp.float32),
            pltpu.SemaphoreType.DMA((len(arguments) - 1,)),
            pltpu.SemaphoreType.DMA((tiles, RAY_CHUNKS)),
        ],
        name="sum_rays",
    )(*arguments)
    received = lax.all_to_all(sent, ("cols", "par"), 0, 0)
    layers = pl.pallas_call(
        functools.partial(smooth_kernel, params=params, tiles=tiles, rows_x=rows_x, rows_y=rows_y),
        out_shape=jax.ShapeDtypeStruct((devices, groups, LANES), jnp.float32),
        in_specs=[vmem],
        out_specs=vmem,
        compiler_params=pltpu.CompilerParams(vmem_limit_bytes=32 << 20),
        name="smooth_block",
    )(received)
    windows = lax.all_to_all(layers, ("cols", "par"), 0, 0)
    return pl.pallas_call(
        functools.partial(collect_kernel, width=width),
        out_shape=jax.ShapeDtypeStruct((params, 1, rows_x, rows_y), jnp.float32),
        in_specs=[vmem],
        out_specs=vmem,
        compiler_params=pltpu.CompilerParams(vmem_limit_bytes=32 << 20),
        name="collect_windows",
    )(windows)


def shards(
    tile_bounds, tile_anchor, tile_picks, rmo_picks, sensitivity, dip_class, strength, couple
):
    devices = lax.axis_size("cols") * lax.axis_size("par")
    plan = shards_by_y if fits(sensitivity, dip_class, devices) else shards_any
    return plan(
        tile_bounds, tile_anchor, tile_picks, rmo_picks, sensitivity, dip_class, strength, couple
    )


def solution(mesh):
    return jax.shard_map(
        shards,
        mesh=mesh,
        in_specs=(
            P(),
            P(("cols", "par"), None),
            P(("cols", "par")),
            P(("cols", "par"), None),
            P(("cols", "par"), None, None, None, None),
            P(("cols", "par"), None, None),
            P(),
            P(),
        ),
        out_specs=P(None, ("cols", "par"), None, None),
        check_vma=False,
    )
```

```python
import functools

import jax
import jax.numpy as jnp
from jax import lax
from jax.experimental import pallas as pl
from jax.experimental.pallas import tpu as pltpu
from jax.sharding import PartitionSpec as P

CAP = 384
PASSES = 6


def extended(block, sides, width):
    for axis, dim in sides:
        count = lax.axis_size(axis)
        forward = [(i, i + 1) for i in range(count - 1)]
        backward = [(target, source) for source, target in forward]
        low = lax.ppermute(
            lax.slice_in_dim(block, block.shape[dim] - width, None, axis=dim), axis, forward
        )
        high = lax.ppermute(lax.slice_in_dim(block, 0, width, axis=dim), axis, backward)
        block = jnp.concatenate([low, block, high], axis=dim)
    return block


def next_cells(values, along_dim):
    count = values.shape[along_dim]
    kept = lax.slice_in_dim(values, 1, count, axis=along_dim)
    zeros = jnp.zeros_like(lax.slice_in_dim(values, 0, 1, axis=along_dim))
    return jnp.concatenate([kept, zeros], axis=along_dim)


def prev_cells(values, along_dim):
    count = values.shape[along_dim]
    kept = lax.slice_in_dim(values, 0, count - 1, axis=along_dim)
    zeros = jnp.zeros_like(lax.slice_in_dim(values, 0, 1, axis=along_dim))
    return jnp.concatenate([zeros, kept], axis=along_dim)


def at_depth(padded, tilt):
    return jnp.where(tilt < 0, padded[:, :-2], jnp.where(tilt > 0, padded[:, 2:], padded[:, 1:-1]))


def smooth_pass(padded, dip_class, strength, mixing):
    centre = padded[:, 1:-1]
    tilt_across = (dip_class // 3 - 1)[None]
    tilt_along = (dip_class % 3 - 1)[None]
    east_side = at_depth(next_cells(padded, 2), tilt_across)
    west_side = at_depth(prev_cells(padded, 2), -tilt_across)
    north_side = at_depth(next_cells(padded, 3), tilt_along)
    south_side = at_depth(prev_cells(padded, 3), -tilt_along)
    laplace = east_side + west_side + north_side + south_side - 4.0 * centre
    smooth = centre + strength[:, None, None, None] * laplace
    return jnp.tensordot(mixing, smooth, axes=1, precision=lax.Precision.HIGHEST)


def shards_any(
    tile_bounds, tile_anchor, tile_picks, rmo_picks, sensitivity, dip_class, strength, couple
):
    tile_count, ray_count, param_count, depth_cells, tile_columns = sensitivity.shape
    col_devices = lax.axis_size("cols")
    par_devices = lax.axis_size("par")
    slab_depth, rows_x, rows_y = dip_class.shape
    total_depth = slab_depth * col_devices * par_devices
    live = jnp.arange(ray_count, dtype=jnp.int32)[None, :] < tile_picks[:, None]
    ray_weight = jnp.where(live, rmo_picks, jnp.zeros_like(rmo_picks))
    contribution = jnp.einsum(
        "tr,trk->tk",
        ray_weight,
        sensitivity.reshape(tile_count, ray_count, -1),
        preferred_element_type=jnp.float32,
    )
    contribution = contribution.reshape(tile_count, param_count, depth_cells, tile_columns)

    def add_tile(tile_number, gradient):
        anchor = (jnp.int32(0), tile_anchor[tile_number, 0], tile_anchor[tile_number, 1])
        current = lax.dynamic_slice(gradient, anchor, (param_count, depth_cells, tile_columns))
        return lax.dynamic_update_slice(gradient, current + contribution[tile_number], anchor)

    gradient = jnp.zeros((param_count, total_depth, CAP), jnp.float32)
    gradient = lax.fori_loop(0, tile_count, add_tile, gradient)
    blocks = gradient.reshape(param_count, col_devices, par_devices, slab_depth, CAP)
    reduced = lax.psum_scatter(blocks, "par", scatter_dimension=2, tiled=True)
    summed = lax.all_to_all(reduced, "cols", split_axis=1, concat_axis=4, tiled=True)
    padded_slots = summed.reshape(param_count, slab_depth, col_devices * CAP)
    columns = rows_x * rows_y
    column_ids = jnp.arange(columns, dtype=jnp.int32)
    starts = tile_bounds[:-1]
    below = starts[None, :] <= column_ids[:, None]
    owner_tile = jnp.sum(below.astype(jnp.int32), axis=1) - 1
    tile_start = jnp.max(jnp.where(below, starts[None, :], jnp.zeros_like(starts)[None, :]), axis=1)
    slot_index = owner_tile * CAP + column_ids - tile_start
    field = jnp.take(padded_slots, slot_index, axis=2).reshape(
        param_count, slab_depth, rows_x, rows_y
    )
    mixing = couple / jnp.sum(couple, axis=1, keepdims=True)
    for _ in range(PASSES):
        padded = extended(field, ((("cols", "par"), 1),), 1)
        field = smooth_pass(padded, dip_class, strength, mixing)
    return field


LANES = 128
SUBLANES = 8
RAY_CHUNKS = 4


def device_index():
    return lax.axis_index("cols") * lax.axis_size("par") + lax.axis_index("par")


def lane_ids(shape):
    return lax.broadcasted_iota(jnp.int32, shape, len(shape) - 1)


def roll_lanes(values, shift):
    width = values.shape[-1]
    shift = shift % width
    return values if shift == 0 else pltpu.roll(values, shift, values.ndim - 1)


def source_kernel(
    bounds_hbm, anchor_hbm, picks_hbm, rmo_hbm, sens_hbm, dip_hbm, strength_hbm, couple_hbm,
    out_ref,
    bounds_ref, anchor_ref, picks_ref, rmo_ref, sens_ref, dip_ref, strength_ref, couple_ref,
    weight_ref, small_sems, sens_sems,
):
    tiles, rays, params, tile_depth, tile_columns = sens_ref.shape
    _, rows_x, rows_y = dip_ref.shape
    devices, width, _ = out_ref.shape
    halves = rows_y // LANES
    per_tile = sens_sems.shape[1]
    chunk = rays // per_tile
    small = [
        pltpu.make_async_copy(hbm, ref, small_sems.at[number])
        for number, (hbm, ref) in enumerate(
            [
                (picks_hbm, picks_ref),
                (rmo_hbm, rmo_ref),
                (bounds_hbm, bounds_ref),
                (anchor_hbm, anchor_ref),
                (dip_hbm, dip_ref),
                (strength_hbm, strength_ref),
                (couple_hbm, couple_ref),
            ]
        )
    ]
    large = [
        [
            pltpu.make_async_copy(
                sens_hbm.at[tile, pl.ds(part * chunk, chunk)],
                sens_ref.at[tile, pl.ds(part * chunk, chunk)],
                sens_sems.at[tile, part],
            )
            for part in range(per_tile)
        ]
        for tile in range(tiles)
    ]
    for copy in small[:2]:
        copy.start()
    for row in large:
        for copy in row:
            copy.start()
    for copy in small[2:]:
        copy.start()

    diagonal = lax.broadcasted_iota(jnp.int32, (rays, rays), 0) == lane_ids((rays, rays))
    for copy in small[:2]:
        copy.wait()
    for tile in range(tiles):
        live = lane_ids((1, rays)) < picks_ref[tile]
        weight = jnp.where(live, rmo_ref[tile : tile + 1, :].astype(jnp.float32), 0.0)
        column = jnp.sum(jnp.where(diagonal, weight, 0.0), axis=1, keepdims=True)
        weight_ref[tile] = jnp.broadcast_to(column, (rays, LANES))
    sums = []
    for tile in range(tiles):
        total = jnp.zeros((params, tile_depth, tile_columns), jnp.float32)
        for ray in range(rays):
            if ray % chunk == 0:
                large[tile][ray // chunk].wait()
            weight = weight_ref[tile, ray : ray + 1, :]
            total = total + weight[None] * sens_ref[tile, ray].astype(jnp.float32)
        sums.append(total)
    for copy in small[2:]:
        copy.wait()

    parts = [[[None] * tiles for _ in range(params)] for _ in range(halves)]
    x_rows, depth_rows = [], []
    y_ids = lane_ids((1, rows_y))
    for tile in range(tiles):
        depth_first = anchor_ref[tile, 0]
        first = bounds_ref[lax.axis_index("cols")] + anchor_ref[tile, 1]
        first_x = first // rows_y
        first_y = first - first_x * rows_y
        half_of = first_y // LANES
        lane_first = first_y - half_of * LANES
        past = lane_ids((1, LANES)) >= lane_first
        for param in range(params):
            turned = pltpu.roll(sums[tile][param], lax.rem(depth_first, tile_depth), 0)
            turned = pltpu.roll(turned, lane_first, 1)
            for half in range(halves):
                after = lax.rem(half_of + 1, halves)
                kept = jnp.logical_or(
                    jnp.logical_and(past, half_of == half),
                    jnp.logical_and(jnp.logical_not(past), after == half),
                )
                parts[half][param][tile] = jnp.where(kept, turned, 0.0)
        x_rows.append((first_x + (y_ids < first_y).astype(jnp.int32)).astype(jnp.float32))
        depth_rows.append(jnp.full((1, rows_y), depth_first, jnp.int32).astype(jnp.float32))
    place_in_packet = lax.rem(y_ids, width)

    def packet_lane(values):
        lane = jnp.zeros((1, rows_y), jnp.float32)
        for q, value in enumerate(values):
            lane = jnp.where(place_in_packet == q, value, lane)
        return lane

    factor_rows = [packet_lane([strength_ref[q] for q in range(params)])]
    for p in range(params):
        weights = [jnp.full((1, rows_y), couple_ref[p, q], jnp.float32) for q in range(params)]
        whole = weights[0]
        for weight in weights[1:]:
            whole = whole + weight
        factor_rows.append(packet_lane([weight / whole for weight in weights]))
    notes = jnp.concatenate(
        [jnp.zeros((3 * width, rows_y), jnp.float32)] + x_rows + depth_rows + factor_rows, axis=0
    )
    dip = dip_ref[0].astype(jnp.float32)
    in_window = lane_ids((rows_x, LANES)) < 3 * width
    count = LANES // width
    for half in range(halves):
        rows = [notes[:, half * LANES : (half + 1) * LANES]]
        for param in range(params):
            rows.extend(parts[half][param])
        turned = jnp.transpose(jnp.concatenate(rows, axis=0))
        for place in range(count):
            device = half * count + place
            window = roll_lanes(dip, width - device * width)[:, :LANES]
            out_ref[device] = jnp.where(in_window, window, turned[place * width : (place + 1) * width])


def smooth_kernel(in_ref, out_ref, *, params, tiles, rows_x, rows_y):
    depth, width, _ = in_ref.shape
    groups = LANES // depth
    halves = rows_x // groups
    rows = 3 * width
    side = rows
    lane = lane_ids((width, LANES))
    z = lane % depth
    low = z < depth // 2
    z_float = z.astype(jnp.float32)

    def add_source(source, field):
        message = in_ref[source]
        swapped = jnp.where(low, roll_lanes(message, -(depth // 2)), roll_lanes(message, depth // 2))
        field = list(field)
        for tile in range(tiles):
            own = low if tile == 0 else jnp.logical_not(low)
            values = jnp.where(own, message, swapped)
            at_x = jnp.broadcast_to(message[:, side + tile : side + tile + 1], (width, LANES))
            first_z = jnp.broadcast_to(
                message[:, side + tiles + tile : side + tiles + tile + 1], (width, LANES)
            )
            behind = z_float - first_z
            inside = jnp.logical_and(behind >= 0.0, behind < float(depth // 2))
            at_x = jnp.where(inside, at_x, -1.0)
            for x in range(rows_x):
                field[x] = field[x] + jnp.where(at_x == float(x), values, 0.0)
        return tuple(field)

    zero = jnp.zeros((width, LANES), jnp.float32)
    field = (zero,) * rows_x
    for source in range(depth):
        field = add_source(source, field)

    block = lane // depth
    current = []
    for param in range(params):
        current.append([])
        for half in range(halves):
            centre = zero
            for group in range(groups):
                moved = roll_lanes(field[half * groups + group], depth * (group - param - 1))
                centre = jnp.where(block == group, moved, centre)
            current[param].append(jnp.concatenate([zero, centre, zero], axis=0))

    dip = []
    for half in range(halves):
        layers = [in_ref[:, half * groups + group, :] for group in range(groups)]
        dip.append(jnp.transpose(jnp.concatenate(layers, axis=0))[:rows])

    lanes = lane_ids((rows, LANES))
    z = lanes % depth
    block = lanes // depth
    first = block == 0
    last = block == groups - 1
    top = z == 0
    bottom = z == depth - 1
    y = device_index() * width - width + lax.broadcasted_iota(jnp.int32, (rows, LANES), 0)
    in_grid = jnp.logical_and(y >= 0, y < rows_y)

    def from_next_x(values):
        moved = [roll_lanes(v, -depth) for v in values]
        return [
            jnp.where(last, moved[h + 1] if h + 1 < halves else 0.0, moved[h]) for h in range(halves)
        ]

    def from_prev_x(values):
        moved = [roll_lanes(v, depth) for v in values]
        return [jnp.where(first, moved[h - 1] if h > 0 else 0.0, moved[h]) for h in range(halves)]

    def from_next_y(values):
        return [pltpu.roll(v, rows - 1, 0) for v in values]

    def from_prev_y(values):
        return [pltpu.roll(v, 1, 0) for v in values]

    def masks(values):
        return [(v < -0.5, v > 0.5) for v in values]

    tilt_x = [jnp.where(d < 2.5, -1.0, jnp.where(d > 5.5, 1.0, 0.0)) for d in dip]
    tilt_y = [d - 3.0 * (t + 1.0) - 1.0 for d, t in zip(dip, tilt_x)]
    to_west = masks(from_prev_x(tilt_x))
    to_east = masks(from_next_x(tilt_x))
    to_south = masks(from_prev_y(tilt_y))
    to_north = masks(from_next_y(tilt_y))

    def factor(lane, q):
        at = side + 2 * tiles + lane
        return jnp.broadcast_to(in_ref[0, q : q + 1, at : at + 1], (rows, LANES))

    strengths = [factor(0, q) for q in range(params)]
    mixing = [
        [jnp.where(in_grid, factor(p + 1, q), 0.0) for q in range(params)] for p in range(params)
    ]

    for _ in range(PASSES):
        smooth = []
        for q in range(params):
            u = current[q]
            above = [jnp.where(top, 0.0, roll_lanes(v, 1)) for v in u]
            below = [jnp.where(bottom, 0.0, roll_lanes(v, -1)) for v in u]

            def plus(tilts):
                return [
                    jnp.where(neg, a, jnp.where(pos, b, v))
                    for (neg, pos), a, v, b in zip(tilts, above, u, below)
                ]

            def minus(tilts):
                return [
                    jnp.where(neg, b, jnp.where(pos, a, v))
                    for (neg, pos), a, v, b in zip(tilts, above, u, below)
                ]

            east = from_next_x(plus(to_west))
            west = from_prev_x(minus(to_east))
            north = from_next_y(plus(to_south))
            south = from_prev_y(minus(to_north))
            smooth.append(
                [
                    v + strengths[q] * (e + w + n + s - 4.0 * v)
                    for v, e, w, n, s in zip(u, east, west, north, south)
                ]
            )
        current = []
        for p in range(params):
            mixed = []
            for half in range(halves):
                value = mixing[p][0] * smooth[0][half]
                for q in range(1, params):
                    value = value + mixing[p][q] * smooth[q][half]
                mixed.append(value)
            current.append(mixed)

    pieces = []
    for half in range(halves):
        for p in range(params):
            pieces.append(current[p][half][width - PASSES : 2 * width + PASSES])
    used = halves * params * (width + 2 * PASSES)
    pieces.append(jnp.zeros((LANES - used, LANES), jnp.float32))
    turned = jnp.transpose(jnp.concatenate(pieces, axis=0))
    for group in range(groups):
        out_ref[:, group, :] = turned[group * depth : (group + 1) * depth]


def collect_kernel(in_ref, out_ref, *, width):
    params, _, rows_x, rows_y = out_ref.shape
    sources, groups, _ = in_ref.shape
    span = width + 2 * PASSES
    halves = rows_x // groups
    lane = lane_ids((rows_x, LANES))
    totals = [[jnp.zeros((rows_x, LANES), jnp.float32) for _ in range(rows_y // LANES)] for _ in range(params)]
    for source in range(sources):
        message = in_ref[source]
        stacked = jnp.concatenate(
            [roll_lanes(message, -half * params * span) for half in range(halves)], axis=0
        )
        first = source * width - PASSES
        for param in range(params):
            placed = roll_lanes(stacked, first - param * span)
            for column in range(rows_y // LANES):
                low, high = first - column * LANES, first - column * LANES + span
                if high <= 0 or low >= LANES:
                    continue
                inside = jnp.logical_and(lane >= low, lane < high)
                totals[param][column] = totals[param][column] + jnp.where(inside, placed, 0.0)
    for param in range(params):
        for column in range(rows_y // LANES):
            out_ref[param, 0, :, column * LANES : (column + 1) * LANES] = totals[param][column]


def fits(sensitivity, dip_class, devices):
    tiles, rays, params, tile_depth, tile_columns = sensitivity.shape
    slab_depth, rows_x, rows_y = dip_class.shape
    depth = slab_depth * devices
    return (
        slab_depth == 1
        and rows_y == devices * SUBLANES
        and PASSES <= SUBLANES
        and rows_y % LANES == 0
        and tile_columns == LANES
        and rows_x == SUBLANES
        and tiles == 2
        and tiles * tile_depth == depth
        and (params + 1) * depth == LANES
        and 3 * SUBLANES + 2 * tiles + params + 1 == depth
        and rays % RAY_CHUNKS == 0
        and rows_x * params * (SUBLANES + 2 * PASSES) <= 4 * LANES
    )


def shards_by_y(
    tile_bounds, tile_anchor, tile_picks, rmo_picks, sensitivity, dip_class, strength, couple
):
    tiles, rays, params, _, _ = sensitivity.shape
    _, rows_x, rows_y = dip_class.shape
    devices = lax.axis_size("cols") * lax.axis_size("par")
    width = rows_y // devices
    groups = LANES // devices
    hbm = pl.BlockSpec(memory_space=pltpu.HBM)
    vmem = pl.BlockSpec(memory_space=pltpu.VMEM)
    arguments = (
        tile_bounds, tile_anchor, tile_picks, rmo_picks, sensitivity, dip_class, strength, couple
    )
    homes = (
        pltpu.SMEM, pltpu.SMEM, pltpu.SMEM, pltpu.VMEM, pltpu.VMEM, pltpu.VMEM, pltpu.SMEM, pltpu.SMEM
    )
    sent = pl.pallas_call(
        source_kernel,
        out_shape=pltpu.VMEM((devices, width, LANES), jnp.float32),
        in_specs=[hbm] * len(arguments),
        out_specs=vmem,
        scratch_shapes=[home(array.shape, array.dtype) for home, array in zip(homes, arguments)]
        + [
            pltpu.VMEM((tiles, rays, LANES), jnp.float32),
            pltpu.SemaphoreType.DMA((len(arguments) - 1,)),
            pltpu.SemaphoreType.DMA((tiles, RAY_CHUNKS)),
        ],
        compiler_params=pltpu.CompilerParams(vmem_limit_bytes=32 << 20),
        name="sum_rays",
    )(*(pltpu.with_memory_space_constraint(array, pltpu.HBM) for array in arguments))
    received = lax.all_to_all(sent, ("cols", "par"), 0, 0)
    layers = pl.pallas_call(
        functools.partial(smooth_kernel, params=params, tiles=tiles, rows_x=rows_x, rows_y=rows_y),
        out_shape=jax.ShapeDtypeStruct((devices, groups, LANES), jnp.float32),
        in_specs=[vmem],
        out_specs=vmem,
        compiler_params=pltpu.CompilerParams(vmem_limit_bytes=32 << 20),
        name="smooth_block",
    )(received)
    windows = lax.all_to_all(layers, ("cols", "par"), 0, 0)
    return pl.pallas_call(
        functools.partial(collect_kernel, width=width),
        out_shape=jax.ShapeDtypeStruct((params, 1, rows_x, rows_y), jnp.float32),
        in_specs=[vmem],
        out_specs=vmem,
        compiler_params=pltpu.CompilerParams(vmem_limit_bytes=32 << 20),
        name="collect_windows",
    )(windows)


def shards(
    tile_bounds, tile_anchor, tile_picks, rmo_picks, sensitivity, dip_class, strength, couple
):
    devices = lax.axis_size("cols") * lax.axis_size("par")
    plan = shards_by_y if fits(sensitivity, dip_class, devices) else shards_any
    return plan(
        tile_bounds, tile_anchor, tile_picks, rmo_picks, sensitivity, dip_class, strength, couple
    )


def solution(mesh):
    return jax.shard_map(
        shards,
        mesh=mesh,
        in_specs=(
            P(),
            P(("cols", "par"), None),
            P(("cols", "par")),
            P(("cols", "par"), None),
            P(("cols", "par"), None, None, None, None),
            P(("cols", "par"), None, None),
            P(),
            P(),
        ),
        out_specs=P(None, ("cols", "par"), None, None),
        check_vma=False,
    )
```

```python
import functools

import jax
import jax.numpy as jnp
from jax import lax
from jax.experimental import pallas as pl
from jax.experimental.pallas import tpu as pltpu
from jax.sharding import PartitionSpec as P

CAP = 384
PASSES = 6


def extended(block, sides, width):
    for axis, dim in sides:
        count = lax.axis_size(axis)
        forward = [(i, i + 1) for i in range(count - 1)]
        backward = [(target, source) for source, target in forward]
        low = lax.ppermute(
            lax.slice_in_dim(block, block.shape[dim] - width, None, axis=dim), axis, forward
        )
        high = lax.ppermute(lax.slice_in_dim(block, 0, width, axis=dim), axis, backward)
        block = jnp.concatenate([low, block, high], axis=dim)
    return block


def next_cells(values, along_dim):
    count = values.shape[along_dim]
    kept = lax.slice_in_dim(values, 1, count, axis=along_dim)
    zeros = jnp.zeros_like(lax.slice_in_dim(values, 0, 1, axis=along_dim))
    return jnp.concatenate([kept, zeros], axis=along_dim)


def prev_cells(values, along_dim):
    count = values.shape[along_dim]
    kept = lax.slice_in_dim(values, 0, count - 1, axis=along_dim)
    zeros = jnp.zeros_like(lax.slice_in_dim(values, 0, 1, axis=along_dim))
    return jnp.concatenate([zeros, kept], axis=along_dim)


def at_depth(padded, tilt):
    return jnp.where(tilt < 0, padded[:, :-2], jnp.where(tilt > 0, padded[:, 2:], padded[:, 1:-1]))


def smooth_pass(padded, dip_class, strength, mixing):
    centre = padded[:, 1:-1]
    tilt_across = (dip_class // 3 - 1)[None]
    tilt_along = (dip_class % 3 - 1)[None]
    east_side = at_depth(next_cells(padded, 2), tilt_across)
    west_side = at_depth(prev_cells(padded, 2), -tilt_across)
    north_side = at_depth(next_cells(padded, 3), tilt_along)
    south_side = at_depth(prev_cells(padded, 3), -tilt_along)
    laplace = east_side + west_side + north_side + south_side - 4.0 * centre
    smooth = centre + strength[:, None, None, None] * laplace
    return jnp.tensordot(mixing, smooth, axes=1, precision=lax.Precision.HIGHEST)


def shards_any(
    tile_bounds, tile_anchor, tile_picks, rmo_picks, sensitivity, dip_class, strength, couple
):
    tile_count, ray_count, param_count, depth_cells, tile_columns = sensitivity.shape
    col_devices = lax.axis_size("cols")
    par_devices = lax.axis_size("par")
    slab_depth, rows_x, rows_y = dip_class.shape
    total_depth = slab_depth * col_devices * par_devices
    live = jnp.arange(ray_count, dtype=jnp.int32)[None, :] < tile_picks[:, None]
    ray_weight = jnp.where(live, rmo_picks, jnp.zeros_like(rmo_picks))
    contribution = jnp.einsum(
        "tr,trk->tk",
        ray_weight,
        sensitivity.reshape(tile_count, ray_count, -1),
        preferred_element_type=jnp.float32,
    )
    contribution = contribution.reshape(tile_count, param_count, depth_cells, tile_columns)

    def add_tile(tile_number, gradient):
        anchor = (jnp.int32(0), tile_anchor[tile_number, 0], tile_anchor[tile_number, 1])
        current = lax.dynamic_slice(gradient, anchor, (param_count, depth_cells, tile_columns))
        return lax.dynamic_update_slice(gradient, current + contribution[tile_number], anchor)

    gradient = jnp.zeros((param_count, total_depth, CAP), jnp.float32)
    gradient = lax.fori_loop(0, tile_count, add_tile, gradient)
    blocks = gradient.reshape(param_count, col_devices, par_devices, slab_depth, CAP)
    reduced = lax.psum_scatter(blocks, "par", scatter_dimension=2, tiled=True)
    summed = lax.all_to_all(reduced, "cols", split_axis=1, concat_axis=4, tiled=True)
    padded_slots = summed.reshape(param_count, slab_depth, col_devices * CAP)
    columns = rows_x * rows_y
    column_ids = jnp.arange(columns, dtype=jnp.int32)
    starts = tile_bounds[:-1]
    below = starts[None, :] <= column_ids[:, None]
    owner_tile = jnp.sum(below.astype(jnp.int32), axis=1) - 1
    tile_start = jnp.max(jnp.where(below, starts[None, :], jnp.zeros_like(starts)[None, :]), axis=1)
    slot_index = owner_tile * CAP + column_ids - tile_start
    field = jnp.take(padded_slots, slot_index, axis=2).reshape(
        param_count, slab_depth, rows_x, rows_y
    )
    mixing = couple / jnp.sum(couple, axis=1, keepdims=True)
    for _ in range(PASSES):
        padded = extended(field, ((("cols", "par"), 1),), 1)
        field = smooth_pass(padded, dip_class, strength, mixing)
    return field


LANES = 128
SUBLANES = 8
RAY_CHUNKS = 2


def device_index():
    return lax.axis_index("cols") * lax.axis_size("par") + lax.axis_index("par")


def lane_ids(shape):
    return lax.broadcasted_iota(jnp.int32, shape, len(shape) - 1)


def roll_lanes(values, shift):
    width = values.shape[-1]
    shift = shift % width
    return values if shift == 0 else pltpu.roll(values, shift, values.ndim - 1)


def source_kernel(
    bounds_hbm, anchor_hbm, picks_hbm, rmo_hbm, sens_hbm, dip_hbm, strength_hbm, couple_hbm,
    out_ref,
    bounds_ref, anchor_ref, picks_ref, rmo_ref, sens_ref, dip_ref, strength_ref, couple_ref,
    weight_ref, small_sems, sens_sems,
):
    tiles, rays, params, tile_depth, tile_columns = sens_ref.shape
    _, rows_x, rows_y = dip_ref.shape
    devices, width, _ = out_ref.shape
    halves = rows_y // LANES
    per_tile = sens_sems.shape[1]
    chunk = rays // per_tile
    small = [
        pltpu.make_async_copy(hbm, ref, small_sems.at[number])
        for number, (hbm, ref) in enumerate(
            [
                (picks_hbm, picks_ref),
                (rmo_hbm, rmo_ref),
                (bounds_hbm, bounds_ref),
                (anchor_hbm, anchor_ref),
                (dip_hbm, dip_ref),
                (strength_hbm, strength_ref),
                (couple_hbm, couple_ref),
            ]
        )
    ]
    large = [
        [
            pltpu.make_async_copy(
                sens_hbm.at[tile, pl.ds(part * chunk, chunk)],
                sens_ref.at[tile, pl.ds(part * chunk, chunk)],
                sens_sems.at[tile, part],
            )
            for part in range(per_tile)
        ]
        for tile in range(tiles)
    ]
    for copy in small[:2]:
        copy.start()
    for row in large:
        for copy in row:
            copy.start()
    for copy in small[2:]:
        copy.start()

    diagonal = lax.broadcasted_iota(jnp.int32, (rays, rays), 0) == lane_ids((rays, rays))
    for copy in small:
        copy.wait()
    for tile in range(tiles):
        live = lane_ids((1, rays)) < picks_ref[tile]
        weight = jnp.where(live, rmo_ref[tile : tile + 1, :].astype(jnp.float32), 0.0)
        column = jnp.sum(jnp.where(diagonal, weight, 0.0), axis=1, keepdims=True)
        weight_ref[tile] = jnp.broadcast_to(column, (rays, LANES))

    y_ids = lane_ids((1, rows_y))
    place_in_packet = lax.rem(y_ids, width)

    def packet_lane(values):
        lane = jnp.zeros((1, rows_y), jnp.float32)
        for q, value in enumerate(values):
            lane = jnp.where(place_in_packet == q, value, lane)
        return lane

    factor_rows = [packet_lane([strength_ref[q] for q in range(params)])]
    for p in range(params):
        weights = [jnp.full((1, rows_y), couple_ref[p, q], jnp.float32) for q in range(params)]
        whole = weights[0]
        for weight in weights[1:]:
            whole = whole + weight
        factor_rows.append(packet_lane([weight / whole for weight in weights]))

    first_depth, lane_first, place_rows, first_half = [], [], [], []
    for tile in range(tiles):
        first_depth.append(anchor_ref[tile, 0])
        first = bounds_ref[lax.axis_index("cols")] + anchor_ref[tile, 1]
        first_x = first // rows_y
        first_y = first - first_x * rows_y
        first_half.append(first_y // LANES)
        lane_first.append(first_y - first_half[tile] * LANES)
        at_x = first_x + (y_ids < first_y).astype(jnp.int32)
        place_rows.append((at_x * devices + first_depth[tile]).astype(jnp.float32))
    notes = jnp.concatenate(
        [jnp.zeros((3 * width, rows_y), jnp.float32)]
        + place_rows
        + factor_rows
        + [jnp.zeros((devices - 3 * width - tiles - params - 1, rows_y), jnp.float32)],
        axis=0,
    )
    dip = dip_ref[0].astype(jnp.float32)
    count = LANES // width
    for device in range(devices):
        out_ref[device] = roll_lanes(dip, width - device * width)[:, :LANES]

    parts = [[[None] * tiles for _ in range(params)] for _ in range(halves)]
    for tile in range(tiles):
        total = jnp.zeros((params, tile_depth, tile_columns), jnp.float32)
        for ray in range(rays):
            if ray % chunk == 0:
                large[tile][ray // chunk].wait()
            weight = weight_ref[tile, ray : ray + 1, :]
            total = total + weight[None] * sens_ref[tile, ray].astype(jnp.float32)
        past = lane_ids((1, LANES)) >= lane_first[tile]
        for param in range(params):
            turned = pltpu.roll(total[param], lax.rem(first_depth[tile], tile_depth), 0)
            turned = pltpu.roll(turned, lane_first[tile], 1)
            for half in range(halves):
                after = lax.rem(first_half[tile] + 1, halves)
                kept = jnp.logical_or(
                    jnp.logical_and(past, first_half[tile] == half),
                    jnp.logical_and(jnp.logical_not(past), after == half),
                )
                parts[half][param][tile] = jnp.where(kept, turned, 0.0)
    in_window = lane_ids((rows_x, LANES)) < 3 * width
    for half in range(halves):
        rows = [notes[:, half * LANES : (half + 1) * LANES]]
        for param in range(params):
            rows.extend(parts[half][param])
        turned = jnp.transpose(jnp.concatenate(rows, axis=0))
        for place in range(count):
            device = half * count + place
            out_ref[device] = jnp.where(
                in_window, out_ref[device], turned[place * width : (place + 1) * width]
            )


def smooth_kernel(in_ref, out_ref, *, params, tiles, rows_x, rows_y):
    depth, width, _ = in_ref.shape
    groups = LANES // depth
    halves = rows_x // groups
    rows = 3 * width
    side = rows
    lane = lane_ids((width, LANES))
    low = lane % depth < depth // 2
    in_tile = (lane % (depth // 2)).astype(jnp.float32)
    zero = jnp.zeros((width, LANES), jnp.float32)
    stays = [zero] * rows_x
    moves = [zero] * rows_x
    for source in range(depth):
        message = in_ref[source]
        at = [
            jnp.broadcast_to(message[:, side + tile : side + tile + 1], (width, LANES))
            for tile in range(tiles)
        ]
        at = jnp.where(low, at[0], at[1])
        at_x = jnp.floor(at * (1.0 / depth))
        below_first = in_tile < at - at_x * depth
        stay = jnp.logical_xor(low, below_first)
        at_stay = jnp.where(stay, at_x, -1.0)
        at_move = jnp.where(stay, -1.0, at_x)
        for x in range(rows_x):
            stays[x] = stays[x] + jnp.where(at_stay == float(x), message, 0.0)
            moves[x] = moves[x] + jnp.where(at_move == float(x), message, 0.0)
    field = [
        stay + jnp.where(low, roll_lanes(move, -(depth // 2)), roll_lanes(move, depth // 2))
        for stay, move in zip(stays, moves)
    ]

    block = lane // depth
    current = []
    for param in range(params):
        current.append([])
        for half in range(halves):
            centre = zero
            for group in range(groups):
                moved = roll_lanes(field[group * halves + half], depth * (group - param - 1))
                centre = jnp.where(block == group, moved, centre)
            current[param].append(jnp.concatenate([zero, centre, zero], axis=0))

    dip = []
    for half in range(halves):
        layers = [in_ref[:, group * halves + half, :] for group in range(groups)]
        dip.append(jnp.transpose(jnp.concatenate(layers, axis=0))[:rows])

    lanes = lane_ids((rows, LANES))
    z = lanes % depth
    block = lanes // depth
    first = block == 0
    last = block == groups - 1
    y = device_index() * width - width + lax.broadcasted_iota(jnp.int32, (rows, LANES), 0)
    in_grid = jnp.logical_and(y >= 0, y < rows_y)

    def factor(lane, q):
        at = side + tiles + lane
        return jnp.broadcast_to(in_ref[0, q : q + 1, at : at + 1], (rows, LANES))

    strengths = [factor(0, q) for q in range(params)]
    keeps = [1.0 - 4.0 * strength for strength in strengths]
    mixing = [
        [jnp.where(in_grid, factor(p + 1, q), 0.0) for q in range(params)] for p in range(params)
    ]

    def codes(tilt, inside=True):
        level = jnp.where(jnp.abs(tilt) < 0.5, 1.0, 0.0)
        above = jnp.where(jnp.logical_and(tilt < -0.5, z > 0), 1.0, 0.0)
        below = jnp.where(jnp.logical_and(tilt > 0.5, z < depth - 1), 1.0, 0.0)
        return [jnp.where(inside, weight, 0.0) for weight in (level, above, below)]

    def candidates(values, shift):
        return [roll_lanes(values, shift + step) for step in (0, 1, -1)]

    def chosen(values, weights):
        total = values[0] * weights[0]
        for value, weight in zip(values[1:], weights[1:]):
            total = total + value * weight
        return total

    def next_y(values):
        return pltpu.roll(values, rows - 1, 0)

    def prev_y(values):
        return pltpu.roll(values, 1, 0)

    east, west, north, south = [], [], [], []
    for half in range(halves):
        tilt_x = jnp.where(dip[half] < 2.5, -1.0, jnp.where(dip[half] > 5.5, 1.0, 0.0))
        tilt_y = dip[half] - 3.0 * tilt_x - 4.0
        east.append(codes(tilt_x, jnp.logical_or(half + 1 < halves, jnp.logical_not(last))))
        west.append(codes(-tilt_x, jnp.logical_or(half > 0, jnp.logical_not(first))))
        north.append(codes(prev_y(tilt_y)))
        south.append(codes(-next_y(tilt_y)))

    for _ in range(PASSES):
        smooth = []
        for q in range(params):
            u = current[q]
            near = [candidates(values, 0) for values in u]
            row = []
            for half in range(halves):
                ahead = near[half + 1] if half + 1 < halves else candidates(u[0], -depth)
                behind = near[half - 1] if half > 0 else candidates(u[-1], depth)
                total = (
                    chosen(ahead, east[half])
                    + chosen(behind, west[half])
                    + next_y(chosen(near[half], north[half]))
                    + prev_y(chosen(near[half], south[half]))
                )
                row.append(keeps[q] * u[half] + strengths[q] * total)
            smooth.append(row)
        current = []
        for p in range(params):
            mixed = []
            for half in range(halves):
                value = mixing[p][0] * smooth[0][half]
                for q in range(1, params):
                    value = value + mixing[p][q] * smooth[q][half]
                mixed.append(value)
            current.append(mixed)

    pieces = []
    for half in range(halves):
        for p in range(params):
            pieces.append(current[p][half][width - PASSES : 2 * width + PASSES])
    used = halves * params * (width + 2 * PASSES)
    pieces.append(jnp.zeros((LANES - used, LANES), jnp.float32))
    turned = jnp.transpose(jnp.concatenate(pieces, axis=0))
    for group in range(groups):
        out_ref[:, group, :] = turned[group * depth : (group + 1) * depth]


def collect_kernel(in_ref, out_ref, *, width):
    params, _, rows_x, rows_y = out_ref.shape
    sources, groups, _ = in_ref.shape
    span = width + 2 * PASSES
    halves = rows_x // groups
    lane = lane_ids((rows_x, LANES))
    totals = [[jnp.zeros((rows_x, LANES), jnp.float32) for _ in range(rows_y // LANES)] for _ in range(params)]
    for source in range(sources):
        message = in_ref[source]
        stacked = jnp.concatenate(
            [roll_lanes(message, -half * params * span) for half in range(halves)], axis=0
        )
        first = source * width - PASSES
        for param in range(params):
            placed = roll_lanes(stacked, first - param * span)
            for column in range(rows_y // LANES):
                low, high = first - column * LANES, first - column * LANES + span
                if high <= 0 or low >= LANES:
                    continue
                inside = jnp.logical_and(lane >= low, lane < high)
                totals[param][column] = totals[param][column] + jnp.where(inside, placed, 0.0)
    for param in range(params):
        for column in range(rows_y // LANES):
            for x in range(rows_x):
                row = (x % halves) * groups + x // halves
                out_ref[param, 0, x : x + 1, column * LANES : (column + 1) * LANES] = totals[param][
                    column
                ][row : row + 1]


def fits(sensitivity, dip_class, devices):
    tiles, rays, params, tile_depth, tile_columns = sensitivity.shape
    slab_depth, rows_x, rows_y = dip_class.shape
    depth = slab_depth * devices
    return (
        slab_depth == 1
        and rows_y == devices * SUBLANES
        and PASSES <= SUBLANES
        and rows_y % LANES == 0
        and tile_columns == LANES
        and rows_x == SUBLANES
        and tiles == 2
        and tiles * tile_depth == depth
        and (params + 1) * depth == LANES
        and 3 * SUBLANES + tiles + params + 1 <= depth
        and rays % RAY_CHUNKS == 0
        and rows_x * params * (SUBLANES + 2 * PASSES) <= 4 * LANES
    )


def shards_by_y(
    tile_bounds, tile_anchor, tile_picks, rmo_picks, sensitivity, dip_class, strength, couple
):
    tiles, rays, params, _, _ = sensitivity.shape
    _, rows_x, rows_y = dip_class.shape
    devices = lax.axis_size("cols") * lax.axis_size("par")
    width = rows_y // devices
    groups = LANES // devices
    hbm = pl.BlockSpec(memory_space=pltpu.HBM)
    vmem = pl.BlockSpec(memory_space=pltpu.VMEM)
    arguments = (
        tile_bounds, tile_anchor, tile_picks, rmo_picks, sensitivity, dip_class, strength, couple
    )
    homes = (
        pltpu.SMEM, pltpu.SMEM, pltpu.SMEM, pltpu.VMEM, pltpu.VMEM, pltpu.VMEM, pltpu.SMEM, pltpu.SMEM
    )
    sent = pl.pallas_call(
        source_kernel,
        out_shape=pltpu.VMEM((devices, width, LANES), jnp.float32),
        in_specs=[hbm] * len(arguments),
        out_specs=vmem,
        scratch_shapes=[home(array.shape, array.dtype) for home, array in zip(homes, arguments)]
        + [
            pltpu.VMEM((tiles, rays, LANES), jnp.float32),
            pltpu.SemaphoreType.DMA((len(arguments) - 1,)),
            pltpu.SemaphoreType.DMA((tiles, RAY_CHUNKS)),
        ],
        compiler_params=pltpu.CompilerParams(vmem_limit_bytes=32 << 20),
        name="sum_rays",
    )(*(pltpu.with_memory_space_constraint(array, pltpu.HBM) for array in arguments))
    received = lax.all_to_all(sent, ("cols", "par"), 0, 0)
    layers = pl.pallas_call(
        functools.partial(smooth_kernel, params=params, tiles=tiles, rows_x=rows_x, rows_y=rows_y),
        out_shape=jax.ShapeDtypeStruct((devices, groups, LANES), jnp.float32),
        in_specs=[vmem],
        out_specs=vmem,
        compiler_params=pltpu.CompilerParams(vmem_limit_bytes=32 << 20),
        name="smooth_block",
    )(received)
    windows = lax.all_to_all(layers, ("cols", "par"), 0, 0)
    return pl.pallas_call(
        functools.partial(collect_kernel, width=width),
        out_shape=jax.ShapeDtypeStruct((params, 1, rows_x, rows_y), jnp.float32),
        in_specs=[vmem],
        out_specs=vmem,
        compiler_params=pltpu.CompilerParams(vmem_limit_bytes=32 << 20),
        name="collect_windows",
    )(windows)


def shards(
    tile_bounds, tile_anchor, tile_picks, rmo_picks, sensitivity, dip_class, strength, couple
):
    devices = lax.axis_size("cols") * lax.axis_size("par")
    plan = shards_by_y if fits(sensitivity, dip_class, devices) else shards_any
    return plan(
        tile_bounds, tile_anchor, tile_picks, rmo_picks, sensitivity, dip_class, strength, couple
    )


def solution(mesh):
    return jax.shard_map(
        shards,
        mesh=mesh,
        in_specs=(
            P(),
            P(("cols", "par"), None),
            P(("cols", "par")),
            P(("cols", "par"), None),
            P(("cols", "par"), None, None, None, None),
            P(("cols", "par"), None, None),
            P(),
            P(),
        ),
        out_specs=P(None, ("cols", "par"), None, None),
        check_vma=False,
    )
```

```python
import functools

import jax
import jax.numpy as jnp
from jax import lax
from jax.experimental import pallas as pl
from jax.experimental.pallas import tpu as pltpu
from jax.sharding import PartitionSpec as P

CAP = 384
PASSES = 6


def extended(block, sides, width):
    for axis, dim in sides:
        count = lax.axis_size(axis)
        forward = [(i, i + 1) for i in range(count - 1)]
        backward = [(target, source) for source, target in forward]
        low = lax.ppermute(
            lax.slice_in_dim(block, block.shape[dim] - width, None, axis=dim), axis, forward
        )
        high = lax.ppermute(lax.slice_in_dim(block, 0, width, axis=dim), axis, backward)
        block = jnp.concatenate([low, block, high], axis=dim)
    return block


def next_cells(values, along_dim):
    count = values.shape[along_dim]
    kept = lax.slice_in_dim(values, 1, count, axis=along_dim)
    zeros = jnp.zeros_like(lax.slice_in_dim(values, 0, 1, axis=along_dim))
    return jnp.concatenate([kept, zeros], axis=along_dim)


def prev_cells(values, along_dim):
    count = values.shape[along_dim]
    kept = lax.slice_in_dim(values, 0, count - 1, axis=along_dim)
    zeros = jnp.zeros_like(lax.slice_in_dim(values, 0, 1, axis=along_dim))
    return jnp.concatenate([zeros, kept], axis=along_dim)


def at_depth(padded, tilt):
    return jnp.where(tilt < 0, padded[:, :-2], jnp.where(tilt > 0, padded[:, 2:], padded[:, 1:-1]))


def smooth_pass(padded, dip_class, strength, mixing):
    centre = padded[:, 1:-1]
    tilt_across = (dip_class // 3 - 1)[None]
    tilt_along = (dip_class % 3 - 1)[None]
    east_side = at_depth(next_cells(padded, 2), tilt_across)
    west_side = at_depth(prev_cells(padded, 2), -tilt_across)
    north_side = at_depth(next_cells(padded, 3), tilt_along)
    south_side = at_depth(prev_cells(padded, 3), -tilt_along)
    laplace = east_side + west_side + north_side + south_side - 4.0 * centre
    smooth = centre + strength[:, None, None, None] * laplace
    return jnp.tensordot(mixing, smooth, axes=1, precision=lax.Precision.HIGHEST)


def shards_any(
    tile_bounds, tile_anchor, tile_picks, rmo_picks, sensitivity, dip_class, strength, couple
):
    tile_count, ray_count, param_count, depth_cells, tile_columns = sensitivity.shape
    col_devices = lax.axis_size("cols")
    par_devices = lax.axis_size("par")
    slab_depth, rows_x, rows_y = dip_class.shape
    total_depth = slab_depth * col_devices * par_devices
    live = jnp.arange(ray_count, dtype=jnp.int32)[None, :] < tile_picks[:, None]
    ray_weight = jnp.where(live, rmo_picks, jnp.zeros_like(rmo_picks))
    contribution = jnp.einsum(
        "tr,trk->tk",
        ray_weight,
        sensitivity.reshape(tile_count, ray_count, -1),
        preferred_element_type=jnp.float32,
    )
    contribution = contribution.reshape(tile_count, param_count, depth_cells, tile_columns)

    def add_tile(tile_number, gradient):
        anchor = (jnp.int32(0), tile_anchor[tile_number, 0], tile_anchor[tile_number, 1])
        current = lax.dynamic_slice(gradient, anchor, (param_count, depth_cells, tile_columns))
        return lax.dynamic_update_slice(gradient, current + contribution[tile_number], anchor)

    gradient = jnp.zeros((param_count, total_depth, CAP), jnp.float32)
    gradient = lax.fori_loop(0, tile_count, add_tile, gradient)
    blocks = gradient.reshape(param_count, col_devices, par_devices, slab_depth, CAP)
    reduced = lax.psum_scatter(blocks, "par", scatter_dimension=2, tiled=True)
    summed = lax.all_to_all(reduced, "cols", split_axis=1, concat_axis=4, tiled=True)
    padded_slots = summed.reshape(param_count, slab_depth, col_devices * CAP)
    columns = rows_x * rows_y
    column_ids = jnp.arange(columns, dtype=jnp.int32)
    starts = tile_bounds[:-1]
    below = starts[None, :] <= column_ids[:, None]
    owner_tile = jnp.sum(below.astype(jnp.int32), axis=1) - 1
    tile_start = jnp.max(jnp.where(below, starts[None, :], jnp.zeros_like(starts)[None, :]), axis=1)
    slot_index = owner_tile * CAP + column_ids - tile_start
    field = jnp.take(padded_slots, slot_index, axis=2).reshape(
        param_count, slab_depth, rows_x, rows_y
    )
    mixing = couple / jnp.sum(couple, axis=1, keepdims=True)
    for _ in range(PASSES):
        padded = extended(field, ((("cols", "par"), 1),), 1)
        field = smooth_pass(padded, dip_class, strength, mixing)
    return field


LANES = 128
SUBLANES = 8
RAY_CHUNKS = 2


def device_index():
    return lax.axis_index("cols") * lax.axis_size("par") + lax.axis_index("par")


def lane_ids(shape):
    return lax.broadcasted_iota(jnp.int32, shape, len(shape) - 1)


def roll_lanes(values, shift):
    width = values.shape[-1]
    shift = shift % width
    return values if shift == 0 else pltpu.roll(values, shift, values.ndim - 1)


def source_kernel(
    bounds_hbm, anchor_hbm, picks_hbm, rmo_hbm, sens_hbm, dip_hbm, strength_hbm, couple_hbm,
    out_ref,
    bounds_ref, anchor_ref, picks_ref, rmo_ref, sens_ref, dip_ref, strength_ref, couple_ref,
    weight_ref, small_sems, sens_sems,
):
    tiles, rays, params, tile_depth, tile_columns = sens_ref.shape
    _, rows_x, rows_y = dip_ref.shape
    devices, width, _ = out_ref.shape
    halves = rows_y // LANES
    per_tile = sens_sems.shape[1]
    chunk = rays // per_tile
    small = [
        pltpu.make_async_copy(hbm, ref, small_sems.at[number])
        for number, (hbm, ref) in enumerate(
            [
                (picks_hbm, picks_ref),
                (rmo_hbm, rmo_ref),
                (bounds_hbm, bounds_ref),
                (anchor_hbm, anchor_ref),
                (dip_hbm, dip_ref),
                (strength_hbm, strength_ref),
                (couple_hbm, couple_ref),
            ]
        )
    ]
    large = [
        [
            pltpu.make_async_copy(
                sens_hbm.at[tile, pl.ds(part * chunk, chunk)],
                sens_ref.at[tile, pl.ds(part * chunk, chunk)],
                sens_sems.at[tile, part],
            )
            for part in range(per_tile)
        ]
        for tile in range(tiles)
    ]
    for copy in small[:2]:
        copy.start()
    for row in large:
        for copy in row:
            copy.start()
    for copy in small[2:]:
        copy.start()

    diagonal = lax.broadcasted_iota(jnp.int32, (rays, rays), 0) == lane_ids((rays, rays))
    for copy in small:
        copy.wait()
    residuals = rmo_ref[...].astype(jnp.float32)
    for tile in range(tiles):
        live = lane_ids((1, rays)) < picks_ref[tile]
        weight = jnp.where(live, residuals[tile : tile + 1], 0.0)
        column = jnp.sum(jnp.where(diagonal, weight, 0.0), axis=1, keepdims=True)
        weight_ref[tile] = jnp.broadcast_to(column, (rays, LANES))

    y_ids = lane_ids((1, rows_y))
    place_in_packet = lax.rem(y_ids, width)

    def packet_lane(values):
        lane = jnp.zeros((1, rows_y), jnp.float32)
        for q, value in enumerate(values):
            lane = jnp.where(place_in_packet == q, value, lane)
        return lane

    factor_rows = [packet_lane([strength_ref[q] for q in range(params)])]
    for p in range(params):
        weights = [jnp.full((1, rows_y), couple_ref[p, q], jnp.float32) for q in range(params)]
        whole = weights[0]
        for weight in weights[1:]:
            whole = whole + weight
        factor_rows.append(packet_lane([weight / whole for weight in weights]))

    first_depth, lane_first, place_rows, first_half = [], [], [], []
    for tile in range(tiles):
        first_depth.append(anchor_ref[tile, 0])
        first = bounds_ref[lax.axis_index("cols")] + anchor_ref[tile, 1]
        first_x = first // rows_y
        first_y = first - first_x * rows_y
        first_half.append(first_y // LANES)
        lane_first.append(first_y - first_half[tile] * LANES)
        at_x = first_x + (y_ids < first_y).astype(jnp.int32)
        place_rows.append((at_x * devices + first_depth[tile]).astype(jnp.float32))
    notes = jnp.concatenate(
        [jnp.zeros((3 * width, rows_y), jnp.float32)]
        + place_rows
        + factor_rows
        + [jnp.zeros((devices - 3 * width - tiles - params - 1, rows_y), jnp.float32)],
        axis=0,
    )
    dip = dip_ref[0].astype(jnp.float32)
    count = LANES // width
    for device in range(devices):
        out_ref[device] = roll_lanes(dip, width - device * width)[:, :LANES]

    parts = [[[None] * tiles for _ in range(params)] for _ in range(halves)]
    for tile in range(tiles):
        total = jnp.zeros((params, tile_depth, tile_columns), jnp.float32)
        for ray in range(rays):
            if ray % chunk == 0:
                large[tile][ray // chunk].wait()
            weight = weight_ref[tile, ray : ray + 1, :]
            total = total + weight[None] * sens_ref[tile, ray].astype(jnp.float32)
        past = lane_ids((1, LANES)) >= lane_first[tile]
        for param in range(params):
            turned = pltpu.roll(total[param], lax.rem(first_depth[tile], tile_depth), 0)
            turned = pltpu.roll(turned, lane_first[tile], 1)
            for half in range(halves):
                after = lax.rem(first_half[tile] + 1, halves)
                kept = jnp.logical_or(
                    jnp.logical_and(past, first_half[tile] == half),
                    jnp.logical_and(jnp.logical_not(past), after == half),
                )
                parts[half][param][tile] = jnp.where(kept, turned, 0.0)
    in_window = lane_ids((rows_x, LANES)) < 3 * width
    for half in range(halves):
        rows = [notes[:, half * LANES : (half + 1) * LANES]]
        for param in range(params):
            rows.extend(parts[half][param])
        turned = jnp.transpose(jnp.concatenate(rows, axis=0))
        for place in range(count):
            device = half * count + place
            out_ref[device] = jnp.where(
                in_window, out_ref[device], turned[place * width : (place + 1) * width]
            )


def smooth_kernel(in_ref, out_ref, *, params, tiles, rows_x, rows_y):
    depth, width, _ = in_ref.shape
    groups = LANES // depth
    halves = rows_x // groups
    rows = 3 * width
    side = rows
    lane = lane_ids((width, LANES))
    low = lane % depth < depth // 2
    in_tile = (lane % (depth // 2)).astype(jnp.float32)
    zero = jnp.zeros((width, LANES), jnp.float32)
    stays = [zero] * rows_x
    moves = [zero] * rows_x
    for source in range(depth):
        message = in_ref[source]
        at = [
            jnp.broadcast_to(message[:, side + tile : side + tile + 1], (width, LANES))
            for tile in range(tiles)
        ]
        at = jnp.where(low, at[0], at[1])
        at_x = jnp.floor(at * (1.0 / depth))
        below_first = in_tile < at - at_x * depth
        stay = jnp.logical_xor(low, below_first)
        at_stay = jnp.where(stay, at_x, -1.0)
        at_move = jnp.where(stay, -1.0, at_x)
        for x in range(rows_x):
            stays[x] = stays[x] + jnp.where(at_stay == float(x), message, 0.0)
            moves[x] = moves[x] + jnp.where(at_move == float(x), message, 0.0)
    block = lane // depth
    current = []
    for param in range(params):
        current.append([])
        for half in range(halves):
            centre = zero
            for group in range(groups):
                x = group * halves + half
                shift = depth * (group - param - 1)
                moved = jnp.where(
                    low,
                    roll_lanes(moves[x], shift - depth // 2),
                    roll_lanes(moves[x], shift + depth // 2),
                )
                centre = jnp.where(block == group, roll_lanes(stays[x], shift) + moved, centre)
            current[param].append([None, centre, None])

    dip = []
    for half in range(halves):
        layers = [in_ref[:, group * halves + half, :] for group in range(groups)]
        dip.append(jnp.transpose(jnp.concatenate(layers, axis=0))[:rows])

    lanes = lane_ids((rows, LANES))
    z = lanes % depth
    block = lanes // depth
    first = block == 0
    last = block == groups - 1
    bands = range(3)
    own = device_index()
    in_grid = [
        jnp.where(own > 0, 1.0, 0.0),
        1.0,
        jnp.where(own < rows_y // width - 1, 1.0, 0.0),
    ]

    def by_band(values):
        return [values[band * width : (band + 1) * width] for band in bands]

    def factor(lane, q):
        at = side + tiles + lane
        return jnp.broadcast_to(in_ref[0, q : q + 1, at : at + 1], (width, LANES))

    strengths = [factor(0, q) for q in range(params)]
    keeps = [1.0 / strength - 4.0 for strength in strengths]
    mixing = [
        [
            [factor(p + 1, q) * strengths[q] * in_grid[band] for band in bands]
            for q in range(params)
        ]
        for p in range(params)
    ]

    def codes(tilt, inside=True):
        level = jnp.where(jnp.abs(tilt) < 0.5, 1.0, 0.0)
        above = jnp.where(jnp.logical_and(tilt < -0.5, z > 0), 1.0, 0.0)
        below = jnp.where(jnp.logical_and(tilt > 0.5, z < depth - 1), 1.0, 0.0)
        weights = [by_band(jnp.where(inside, weight, 0.0)) for weight in (level, above, below)]
        return list(zip(*weights))

    def chosen(weights, many):
        results = []
        for values in many:
            if values is None:
                results.append(None)
                continue
            total = values[0] * weights[0]
            for value, weight in zip(values[1:], weights[1:]):
                total = total + value * weight
            results.append(total)
        return results

    def candidates(values, shift):
        if values is None:
            return None
        return [roll_lanes(values, shift + step) for step in (0, 1, -1)]

    row_ids = lax.broadcasted_iota(jnp.int32, (width, LANES), 0)

    def moved_y(here, there, step):
        if here is None and there is None:
            return None
        parts = [
            0.0 if values is None else pltpu.roll(values, step % width, 0) for values in (here, there)
        ]
        return jnp.where(row_ids == (width - 1 if step < 0 else 0), parts[1], parts[0])

    def added(terms):
        terms = [term for term in terms if term is not None]
        total = terms[0] if terms else None
        for term in terms[1:]:
            total = total + term
        return total

    east, west, north, south = [], [], [], []
    for half in range(halves):
        tilt_x = jnp.where(dip[half] < 2.5, -1.0, jnp.where(dip[half] > 5.5, 1.0, 0.0))
        tilt_y = dip[half] - 3.0 * tilt_x - 4.0
        east.append(codes(tilt_x, jnp.logical_or(half + 1 < halves, jnp.logical_not(last))))
        west.append(codes(-tilt_x, jnp.logical_or(half > 0, jnp.logical_not(first))))
        north.append(codes(pltpu.roll(tilt_y, 1, 0)))
        south.append(codes(-pltpu.roll(tilt_y, rows - 1, 0)))

    def prepare(u, half):
        return [
            (
                v,
                candidates(v, 0),
                candidates(v, -depth) if half == 0 else None,
                candidates(v, depth) if half == halves - 1 else None,
            )
            for v in u
        ]

    ready = {
        (half, band): prepare([current[p][half][band] for p in range(params)], half)
        for band in bands
        for half in range(halves)
    }
    def in_turn(weight, earlier):
        return weight if earlier is None else jnp.maximum(weight, jnp.minimum(earlier, -1e30))

    for step in range(PASSES):
        turned_south, turned_north = {}, {}
        following = {}
        done = None

        def to_south(half, band):
            if (half, band) not in turned_south:
                many = [item[1] for item in ready[half, band]]
                turned_south[half, band] = chosen(north[half][band], many)
            return turned_south[half, band]

        def to_north(half, band):
            if (half, band) not in turned_north:
                many = [item[1] for item in ready[half, band]]
                turned_north[half, band] = chosen(south[half][band], many)
            return turned_north[half, band]

        for band in bands:
            for half in range(halves):
                if half + 1 < halves:
                    ahead = [item[1] for item in ready[half + 1, band]]
                else:
                    ahead = [item[2] for item in ready[0, band]]
                if half > 0:
                    behind = [item[1] for item in ready[half - 1, band]]
                else:
                    behind = [item[3] for item in ready[halves - 1, band]]
                level, above, below = east[half][band]
                to_west = chosen((in_turn(level, done), above, below), ahead)
                to_east = chosen(west[half][band], behind)
                sums = []
                for q in range(params):
                    u = ready[half, band][q][0]
                    upper = to_south(half, band + 1)[q] if band + 1 < len(bands) else None
                    lower = to_north(half, band - 1)[q] if band > 0 else None
                    sums.append(
                        added(
                            [
                                to_west[q],
                                to_east[q],
                                None if u is None else keeps[q] * u,
                                moved_y(to_south(half, band)[q], upper, -1),
                                moved_y(to_north(half, band)[q], lower, 1),
                            ]
                        )
                    )
                new = [
                    added([mixing[p][q][band] * sums[q] for q in range(params)])
                    for p in range(params)
                ]
                done = new[0]
                if step + 1 < PASSES:
                    following[half, band] = prepare(new, half)
                else:
                    for p in range(params):
                        current[p][half][band] = new[p]
        ready = following
    current = [[jnp.concatenate(bands_of, axis=0) for bands_of in u] for u in current]

    pieces = []
    for half in range(halves):
        for p in range(params):
            pieces.append(current[p][half][width - PASSES : 2 * width + PASSES])
    used = halves * params * (width + 2 * PASSES)
    pieces.append(jnp.zeros((LANES - used, LANES), jnp.float32))
    turned = jnp.transpose(jnp.concatenate(pieces, axis=0))
    for group in range(groups):
        out_ref[:, group, :] = turned[group * depth : (group + 1) * depth]


def collect_kernel(in_ref, out_ref, *, width):
    params, _, rows_x, rows_y = out_ref.shape
    sources, groups, _ = in_ref.shape
    span = width + 2 * PASSES
    halves = rows_x // groups
    lane = lane_ids((rows_x, LANES))
    totals = [[jnp.zeros((rows_x, LANES), jnp.float32) for _ in range(rows_y // LANES)] for _ in range(params)]
    for source in range(sources):
        message = in_ref[source]
        stacked = jnp.concatenate(
            [roll_lanes(message, -half * params * span) for half in range(halves)], axis=0
        )
        first = source * width - PASSES
        for param in range(params):
            placed = roll_lanes(stacked, first - param * span)
            for column in range(rows_y // LANES):
                low, high = first - column * LANES, first - column * LANES + span
                if high <= 0 or low >= LANES:
                    continue
                inside = jnp.logical_and(lane >= low, lane < high)
                totals[param][column] = totals[param][column] + jnp.where(inside, placed, 0.0)
    for param in range(params):
        for column in range(rows_y // LANES):
            for x in range(rows_x):
                row = (x % halves) * groups + x // halves
                out_ref[param, 0, x : x + 1, column * LANES : (column + 1) * LANES] = totals[param][
                    column
                ][row : row + 1]


def fits(sensitivity, dip_class, devices):
    tiles, rays, params, tile_depth, tile_columns = sensitivity.shape
    slab_depth, rows_x, rows_y = dip_class.shape
    depth = slab_depth * devices
    return (
        slab_depth == 1
        and rows_y == devices * SUBLANES
        and PASSES <= SUBLANES
        and rows_y % LANES == 0
        and tile_columns == LANES
        and rows_x == SUBLANES
        and tiles == 2
        and tiles * tile_depth == depth
        and (params + 1) * depth == LANES
        and 3 * SUBLANES + tiles + params + 1 <= depth
        and rays % RAY_CHUNKS == 0
        and rows_x * params * (SUBLANES + 2 * PASSES) <= 4 * LANES
    )


def shards_by_y(
    tile_bounds, tile_anchor, tile_picks, rmo_picks, sensitivity, dip_class, strength, couple
):
    tiles, rays, params, _, _ = sensitivity.shape
    _, rows_x, rows_y = dip_class.shape
    devices = lax.axis_size("cols") * lax.axis_size("par")
    width = rows_y // devices
    groups = LANES // devices
    hbm = pl.BlockSpec(memory_space=pltpu.HBM)
    vmem = pl.BlockSpec(memory_space=pltpu.VMEM)
    arguments = (
        tile_bounds, tile_anchor, tile_picks, rmo_picks, sensitivity, dip_class, strength, couple
    )
    homes = (
        pltpu.SMEM, pltpu.SMEM, pltpu.SMEM, pltpu.VMEM, pltpu.VMEM, pltpu.VMEM, pltpu.SMEM, pltpu.SMEM
    )
    sent = pl.pallas_call(
        source_kernel,
        out_shape=pltpu.VMEM((devices, width, LANES), jnp.float32),
        in_specs=[hbm] * len(arguments),
        out_specs=vmem,
        scratch_shapes=[home(array.shape, array.dtype) for home, array in zip(homes, arguments)]
        + [
            pltpu.VMEM((tiles, rays, LANES), jnp.float32),
            pltpu.SemaphoreType.DMA((len(arguments) - 1,)),
            pltpu.SemaphoreType.DMA((tiles, RAY_CHUNKS)),
        ],
        compiler_params=pltpu.CompilerParams(vmem_limit_bytes=32 << 20),
        name="sum_rays",
    )(*(pltpu.with_memory_space_constraint(array, pltpu.HBM) for array in arguments))
    received = lax.all_to_all(sent, ("cols", "par"), 0, 0)
    layers = pl.pallas_call(
        functools.partial(smooth_kernel, params=params, tiles=tiles, rows_x=rows_x, rows_y=rows_y),
        out_shape=jax.ShapeDtypeStruct((devices, groups, LANES), jnp.float32),
        in_specs=[vmem],
        out_specs=vmem,
        compiler_params=pltpu.CompilerParams(vmem_limit_bytes=32 << 20),
        name="smooth_block",
    )(received)
    windows = lax.all_to_all(layers, ("cols", "par"), 0, 0)
    return pl.pallas_call(
        functools.partial(collect_kernel, width=width),
        out_shape=jax.ShapeDtypeStruct((params, 1, rows_x, rows_y), jnp.float32),
        in_specs=[vmem],
        out_specs=vmem,
        compiler_params=pltpu.CompilerParams(vmem_limit_bytes=32 << 20),
        name="collect_windows",
    )(windows)


def shards(
    tile_bounds, tile_anchor, tile_picks, rmo_picks, sensitivity, dip_class, strength, couple
):
    devices = lax.axis_size("cols") * lax.axis_size("par")
    plan = shards_by_y if fits(sensitivity, dip_class, devices) else shards_any
    return plan(
        tile_bounds, tile_anchor, tile_picks, rmo_picks, sensitivity, dip_class, strength, couple
    )


def solution(mesh):
    return jax.shard_map(
        shards,
        mesh=mesh,
        in_specs=(
            P(),
            P(("cols", "par"), None),
            P(("cols", "par")),
            P(("cols", "par"), None),
            P(("cols", "par"), None, None, None, None),
            P(("cols", "par"), None, None),
            P(),
            P(),
        ),
        out_specs=P(None, ("cols", "par"), None, None),
        check_vma=False,
    )
```

```python
import functools

import jax
import jax.numpy as jnp
from jax import lax
from jax.experimental import pallas as pl
from jax.experimental.pallas import tpu as pltpu
from jax.sharding import PartitionSpec as P

CAP = 384
PASSES = 6


def extended(block, sides, width):
    for axis, dim in sides:
        count = lax.axis_size(axis)
        forward = [(i, i + 1) for i in range(count - 1)]
        backward = [(target, source) for source, target in forward]
        low = lax.ppermute(
            lax.slice_in_dim(block, block.shape[dim] - width, None, axis=dim), axis, forward
        )
        high = lax.ppermute(lax.slice_in_dim(block, 0, width, axis=dim), axis, backward)
        block = jnp.concatenate([low, block, high], axis=dim)
    return block


def next_cells(values, along_dim):
    count = values.shape[along_dim]
    kept = lax.slice_in_dim(values, 1, count, axis=along_dim)
    zeros = jnp.zeros_like(lax.slice_in_dim(values, 0, 1, axis=along_dim))
    return jnp.concatenate([kept, zeros], axis=along_dim)


def prev_cells(values, along_dim):
    count = values.shape[along_dim]
    kept = lax.slice_in_dim(values, 0, count - 1, axis=along_dim)
    zeros = jnp.zeros_like(lax.slice_in_dim(values, 0, 1, axis=along_dim))
    return jnp.concatenate([zeros, kept], axis=along_dim)


def at_depth(padded, tilt):
    return jnp.where(tilt < 0, padded[:, :-2], jnp.where(tilt > 0, padded[:, 2:], padded[:, 1:-1]))


def smooth_pass(padded, dip_class, strength, mixing):
    centre = padded[:, 1:-1]
    tilt_across = (dip_class // 3 - 1)[None]
    tilt_along = (dip_class % 3 - 1)[None]
    east_side = at_depth(next_cells(padded, 2), tilt_across)
    west_side = at_depth(prev_cells(padded, 2), -tilt_across)
    north_side = at_depth(next_cells(padded, 3), tilt_along)
    south_side = at_depth(prev_cells(padded, 3), -tilt_along)
    laplace = east_side + west_side + north_side + south_side - 4.0 * centre
    smooth = centre + strength[:, None, None, None] * laplace
    return jnp.tensordot(mixing, smooth, axes=1, precision=lax.Precision.HIGHEST)


def shards_any(
    tile_bounds, tile_anchor, tile_picks, rmo_picks, sensitivity, dip_class, strength, couple
):
    tile_count, ray_count, param_count, depth_cells, tile_columns = sensitivity.shape
    col_devices = lax.axis_size("cols")
    par_devices = lax.axis_size("par")
    slab_depth, rows_x, rows_y = dip_class.shape
    total_depth = slab_depth * col_devices * par_devices
    live = jnp.arange(ray_count, dtype=jnp.int32)[None, :] < tile_picks[:, None]
    ray_weight = jnp.where(live, rmo_picks, jnp.zeros_like(rmo_picks))
    contribution = jnp.einsum(
        "tr,trk->tk",
        ray_weight,
        sensitivity.reshape(tile_count, ray_count, -1),
        preferred_element_type=jnp.float32,
    )
    contribution = contribution.reshape(tile_count, param_count, depth_cells, tile_columns)

    def add_tile(tile_number, gradient):
        anchor = (jnp.int32(0), tile_anchor[tile_number, 0], tile_anchor[tile_number, 1])
        current = lax.dynamic_slice(gradient, anchor, (param_count, depth_cells, tile_columns))
        return lax.dynamic_update_slice(gradient, current + contribution[tile_number], anchor)

    gradient = jnp.zeros((param_count, total_depth, CAP), jnp.float32)
    gradient = lax.fori_loop(0, tile_count, add_tile, gradient)
    blocks = gradient.reshape(param_count, col_devices, par_devices, slab_depth, CAP)
    reduced = lax.psum_scatter(blocks, "par", scatter_dimension=2, tiled=True)
    summed = lax.all_to_all(reduced, "cols", split_axis=1, concat_axis=4, tiled=True)
    padded_slots = summed.reshape(param_count, slab_depth, col_devices * CAP)
    columns = rows_x * rows_y
    column_ids = jnp.arange(columns, dtype=jnp.int32)
    starts = tile_bounds[:-1]
    below = starts[None, :] <= column_ids[:, None]
    owner_tile = jnp.sum(below.astype(jnp.int32), axis=1) - 1
    tile_start = jnp.max(jnp.where(below, starts[None, :], jnp.zeros_like(starts)[None, :]), axis=1)
    slot_index = owner_tile * CAP + column_ids - tile_start
    field = jnp.take(padded_slots, slot_index, axis=2).reshape(
        param_count, slab_depth, rows_x, rows_y
    )
    mixing = couple / jnp.sum(couple, axis=1, keepdims=True)
    for _ in range(PASSES):
        padded = extended(field, ((("cols", "par"), 1),), 1)
        field = smooth_pass(padded, dip_class, strength, mixing)
    return field


LANES = 128
SUBLANES = 8
RAY_CHUNKS = 2


def block_index():
    return lax.axis_index("par") * lax.axis_size("cols") + lax.axis_index("cols")


def lane_ids(shape):
    return lax.broadcasted_iota(jnp.int32, shape, len(shape) - 1)


def roll_lanes(values, shift):
    width = values.shape[-1]
    shift = shift % width
    return values if shift == 0 else pltpu.roll(values, shift, values.ndim - 1)


def source_kernel(
    bounds_hbm, anchor_hbm, picks_hbm, rmo_hbm, sens_hbm, dip_hbm, strength_hbm, couple_hbm,
    out_ref,
    bounds_ref, anchor_ref, picks_ref, rmo_ref, sens_ref, dip_ref, strength_ref, couple_ref,
    weight_ref, small_sems, sens_sems,
):
    tiles, rays, params, tile_depth, tile_columns = sens_ref.shape
    _, rows_x, rows_y = dip_ref.shape
    devices, width, _ = out_ref.shape
    halves = rows_y // LANES
    per_tile = sens_sems.shape[1]
    chunk = rays // per_tile
    small = [
        pltpu.make_async_copy(hbm, ref, small_sems.at[number])
        for number, (hbm, ref) in enumerate(
            [
                (picks_hbm, picks_ref),
                (rmo_hbm, rmo_ref),
                (bounds_hbm, bounds_ref),
                (anchor_hbm, anchor_ref),
                (dip_hbm, dip_ref),
                (strength_hbm, strength_ref),
                (couple_hbm, couple_ref),
            ]
        )
    ]
    large = [
        [
            pltpu.make_async_copy(
                sens_hbm.at[tile, pl.ds(part * chunk, chunk)],
                sens_ref.at[tile, pl.ds(part * chunk, chunk)],
                sens_sems.at[tile, part],
            )
            for part in range(per_tile)
        ]
        for tile in range(tiles)
    ]
    for copy in small[:2]:
        copy.start()
    for row in large:
        for copy in row:
            copy.start()
    for copy in small[2:]:
        copy.start()

    diagonal = lax.broadcasted_iota(jnp.int32, (rays, rays), 0) == lane_ids((rays, rays))
    for copy in small:
        copy.wait()
    residuals = rmo_ref[...].astype(jnp.float32)
    for tile in range(tiles):
        live = lane_ids((1, rays)) < picks_ref[tile]
        weight = jnp.where(live, residuals[tile : tile + 1], 0.0)
        column = jnp.sum(jnp.where(diagonal, weight, 0.0), axis=1, keepdims=True)
        weight_ref[tile] = jnp.broadcast_to(column, (rays, LANES))

    y_ids = lane_ids((1, rows_y))
    place_in_packet = lax.rem(y_ids, width)

    def packet_lane(values):
        lane = jnp.zeros((1, rows_y), jnp.float32)
        for q, value in enumerate(values):
            lane = jnp.where(place_in_packet == q, value, lane)
        return lane

    factor_rows = [packet_lane([strength_ref[q] for q in range(params)])]
    for p in range(params):
        weights = [jnp.full((1, rows_y), couple_ref[p, q], jnp.float32) for q in range(params)]
        whole = weights[0]
        for weight in weights[1:]:
            whole = whole + weight
        factor_rows.append(packet_lane([weight / whole for weight in weights]))

    first_depth, lane_first, place_rows, first_half = [], [], [], []
    for tile in range(tiles):
        first_depth.append(anchor_ref[tile, 0])
        first = bounds_ref[lax.axis_index("cols")] + anchor_ref[tile, 1]
        first_x = first // rows_y
        first_y = first - first_x * rows_y
        first_half.append(first_y // LANES)
        lane_first.append(first_y - first_half[tile] * LANES)
        at_x = first_x + (y_ids < first_y).astype(jnp.int32)
        place_rows.append((at_x * devices + first_depth[tile]).astype(jnp.float32))
    notes = jnp.concatenate(
        [jnp.zeros((3 * width, rows_y), jnp.float32)]
        + place_rows
        + factor_rows
        + [jnp.zeros((devices - 3 * width - tiles - params - 1, rows_y), jnp.float32)],
        axis=0,
    )
    dip = dip_ref[0].astype(jnp.float32)
    count = LANES // width
    for device in range(devices):
        out_ref[device] = roll_lanes(dip, width - device * width)[:, :LANES]

    parts = [[[None] * tiles for _ in range(params)] for _ in range(halves)]
    for tile in range(tiles):
        total = jnp.zeros((params, tile_depth, tile_columns), jnp.float32)
        for ray in range(rays):
            if ray % chunk == 0:
                large[tile][ray // chunk].wait()
            weight = weight_ref[tile, ray : ray + 1, :]
            total = total + weight[None] * sens_ref[tile, ray].astype(jnp.float32)
        past = lane_ids((1, LANES)) >= lane_first[tile]
        for param in range(params):
            turned = pltpu.roll(total[param], lax.rem(first_depth[tile], tile_depth), 0)
            turned = pltpu.roll(turned, lane_first[tile], 1)
            for half in range(halves):
                after = lax.rem(first_half[tile] + 1, halves)
                kept = jnp.logical_or(
                    jnp.logical_and(past, first_half[tile] == half),
                    jnp.logical_and(jnp.logical_not(past), after == half),
                )
                parts[half][param][tile] = jnp.where(kept, turned, 0.0)
    in_window = lane_ids((rows_x, LANES)) < 3 * width
    for half in range(halves):
        rows = [notes[:, half * LANES : (half + 1) * LANES]]
        for param in range(params):
            rows.extend(parts[half][param])
        turned = jnp.transpose(jnp.concatenate(rows, axis=0))
        for place in range(count):
            device = half * count + place
            out_ref[device] = jnp.where(
                in_window, out_ref[device], turned[place * width : (place + 1) * width]
            )


def smooth_kernel(in_ref, out_ref, layer_ref, *, params, tiles, replicas, rows_x, rows_y):
    depth, width, _ = in_ref.shape
    groups = LANES // depth
    halves = rows_x // groups
    rows = 3 * width
    side = rows
    lane = lane_ids((width, LANES))
    low = lane % depth < depth // 2
    in_tile = (lane % (depth // 2)).astype(jnp.float32)
    zero = jnp.zeros((width, LANES), jnp.float32)
    stays = [zero] * rows_x
    moves = [zero] * rows_x
    for source in range(depth):
        message = in_ref[source]
        at = [
            jnp.broadcast_to(message[:, side + tile : side + tile + 1], (width, LANES))
            for tile in range(tiles)
        ]
        at = jnp.where(low, at[0], at[1])
        at_x = jnp.floor(at * (1.0 / depth))
        below_first = in_tile < at - at_x * depth
        stay = jnp.logical_xor(low, below_first)
        at_stay = jnp.where(stay, at_x, -1.0)
        at_move = jnp.where(stay, -1.0, at_x)
        for x in range(rows_x):
            stays[x] = stays[x] + jnp.where(at_stay == float(x), message, 0.0)
            moves[x] = moves[x] + jnp.where(at_move == float(x), message, 0.0)
    block = lane // depth
    current = []
    for param in range(params):
        current.append([])
        for half in range(halves):
            centre = zero
            for group in range(groups):
                x = group * halves + half
                shift = depth * (group - param - 1)
                moved = jnp.where(
                    low,
                    roll_lanes(moves[x], shift - depth // 2),
                    roll_lanes(moves[x], shift + depth // 2),
                )
                centre = jnp.where(block == group, roll_lanes(stays[x], shift) + moved, centre)
            current[param].append([None, centre, None])

    dip = []
    for half in range(halves):
        columns = depth // replicas
        for group in range(groups):
            for replica in range(replicas):
                layer_ref[half, pl.ds(group * depth + replica, columns, replicas), :] = in_ref[
                    replica * columns : (replica + 1) * columns, group * halves + half, :
                ]
        dip.append(jnp.transpose(layer_ref[half])[:rows])

    lanes = lane_ids((rows, LANES))
    z = lanes % depth
    block = lanes // depth
    first = block == 0
    last = block == groups - 1
    bands = range(3)
    own = block_index()
    in_grid = [
        jnp.where(own > 0, 1.0, 0.0),
        1.0,
        jnp.where(own < rows_y // width - 1, 1.0, 0.0),
    ]

    def by_band(values):
        return [values[band * width : (band + 1) * width] for band in bands]

    def factor(lane, q):
        at = side + tiles + lane
        return jnp.broadcast_to(in_ref[0, q : q + 1, at : at + 1], (width, LANES))

    strengths = [factor(0, q) for q in range(params)]
    keeps = [1.0 / strength - 4.0 for strength in strengths]
    mixing = [
        [
            [factor(p + 1, q) * strengths[q] * in_grid[band] for band in bands]
            for q in range(params)
        ]
        for p in range(params)
    ]

    def codes(tilt, inside=True):
        level = jnp.where(jnp.abs(tilt) < 0.5, 1.0, 0.0)
        above = jnp.where(jnp.logical_and(tilt < -0.5, z > 0), 1.0, 0.0)
        below = jnp.where(jnp.logical_and(tilt > 0.5, z < depth - 1), 1.0, 0.0)
        weights = [by_band(jnp.where(inside, weight, 0.0)) for weight in (level, above, below)]
        return list(zip(*weights))

    def chosen(weights, many):
        results = []
        for values in many:
            if values is None:
                results.append(None)
                continue
            total = values[0] * weights[0]
            for value, weight in zip(values[1:], weights[1:]):
                total = total + value * weight
            results.append(total)
        return results

    def candidates(values, shift):
        if values is None:
            return None
        return [roll_lanes(values, shift + step) for step in (0, 1, -1)]

    row_ids = lax.broadcasted_iota(jnp.int32, (width, LANES), 0)

    def moved_y(here, there, step):
        if here is None and there is None:
            return None
        parts = [
            0.0 if values is None else pltpu.roll(values, step % width, 0) for values in (here, there)
        ]
        return jnp.where(row_ids == (width - 1 if step < 0 else 0), parts[1], parts[0])

    def added(terms):
        terms = [term for term in terms if term is not None]
        total = terms[0] if terms else None
        for term in terms[1:]:
            total = total + term
        return total

    east, west, north, south = [], [], [], []
    for half in range(halves):
        tilt_x = jnp.where(dip[half] < 2.5, -1.0, jnp.where(dip[half] > 5.5, 1.0, 0.0))
        tilt_y = dip[half] - 3.0 * tilt_x - 4.0
        east.append(codes(tilt_x, jnp.logical_or(half + 1 < halves, jnp.logical_not(last))))
        west.append(codes(-tilt_x, jnp.logical_or(half > 0, jnp.logical_not(first))))
        north.append(codes(pltpu.roll(tilt_y, 1, 0)))
        south.append(codes(-pltpu.roll(tilt_y, rows - 1, 0)))

    def prepare(u, half):
        return [
            (
                v,
                candidates(v, 0),
                candidates(v, -depth) if half == 0 else None,
                candidates(v, depth) if half == halves - 1 else None,
            )
            for v in u
        ]

    ready = {
        (half, band): prepare([current[p][half][band] for p in range(params)], half)
        for band in bands
        for half in range(halves)
    }
    def in_turn(weight, earlier):
        return weight if earlier is None else jnp.maximum(weight, jnp.minimum(earlier, -1e30))

    for step in range(PASSES):
        turned_south, turned_north = {}, {}
        following = {}
        done = None

        def to_south(half, band):
            if (half, band) not in turned_south:
                many = [item[1] for item in ready[half, band]]
                turned_south[half, band] = chosen(north[half][band], many)
            return turned_south[half, band]

        def to_north(half, band):
            if (half, band) not in turned_north:
                many = [item[1] for item in ready[half, band]]
                turned_north[half, band] = chosen(south[half][band], many)
            return turned_north[half, band]

        for band in bands:
            for half in range(halves):
                if half + 1 < halves:
                    ahead = [item[1] for item in ready[half + 1, band]]
                else:
                    ahead = [item[2] for item in ready[0, band]]
                if half > 0:
                    behind = [item[1] for item in ready[half - 1, band]]
                else:
                    behind = [item[3] for item in ready[halves - 1, band]]
                level, above, below = east[half][band]
                to_west = chosen((in_turn(level, done), above, below), ahead)
                to_east = chosen(west[half][band], behind)
                sums = []
                for q in range(params):
                    u = ready[half, band][q][0]
                    upper = to_south(half, band + 1)[q] if band + 1 < len(bands) else None
                    lower = to_north(half, band - 1)[q] if band > 0 else None
                    sums.append(
                        added(
                            [
                                to_west[q],
                                to_east[q],
                                None if u is None else keeps[q] * u,
                                moved_y(to_south(half, band)[q], upper, -1),
                                moved_y(to_north(half, band)[q], lower, 1),
                            ]
                        )
                    )
                new = [
                    added([mixing[p][q][band] * sums[q] for q in range(params)])
                    for p in range(params)
                ]
                done = new[0]
                if step + 1 < PASSES:
                    following[half, band] = prepare(new, half)
                else:
                    for p in range(params):
                        current[p][half][band] = new[p]
        ready = following
    current = [[jnp.concatenate(bands_of, axis=0) for bands_of in u] for u in current]

    pieces = []
    for half in range(halves):
        for p in range(params):
            pieces.append(current[p][half][width - PASSES : 2 * width + PASSES])
    used = halves * params * (width + 2 * PASSES)
    pieces.append(jnp.zeros((LANES - used, LANES), jnp.float32))
    layer_ref[0] = jnp.transpose(jnp.concatenate(pieces, axis=0))
    for group in range(groups):
        for replica in range(replicas):
            out_ref[replica * columns : (replica + 1) * columns, group, :] = layer_ref[
                0, pl.ds(group * depth + replica, columns, replicas), :
            ]


def collect_kernel(in_ref, out_ref, *, width):
    params, _, rows_x, rows_y = out_ref.shape
    sources, groups, _ = in_ref.shape
    span = width + 2 * PASSES
    halves = rows_x // groups
    lane = lane_ids((rows_x, LANES))
    totals = [[jnp.zeros((rows_x, LANES), jnp.float32) for _ in range(rows_y // LANES)] for _ in range(params)]
    for source in range(sources):
        message = in_ref[source]
        stacked = jnp.concatenate(
            [roll_lanes(message, -half * params * span) for half in range(halves)], axis=0
        )
        first = source * width - PASSES
        for param in range(params):
            placed = roll_lanes(stacked, first - param * span)
            for column in range(rows_y // LANES):
                low, high = first - column * LANES, first - column * LANES + span
                if high <= 0 or low >= LANES:
                    continue
                inside = jnp.logical_and(lane >= low, lane < high)
                totals[param][column] = totals[param][column] + jnp.where(inside, placed, 0.0)
    for param in range(params):
        for column in range(rows_y // LANES):
            for x in range(rows_x):
                row = (x % halves) * groups + x // halves
                out_ref[param, 0, x : x + 1, column * LANES : (column + 1) * LANES] = totals[param][
                    column
                ][row : row + 1]


def fits(sensitivity, dip_class, devices):
    tiles, rays, params, tile_depth, tile_columns = sensitivity.shape
    slab_depth, rows_x, rows_y = dip_class.shape
    depth = slab_depth * devices
    return (
        slab_depth == 1
        and rows_y == devices * SUBLANES
        and PASSES <= SUBLANES
        and rows_y % LANES == 0
        and tile_columns == LANES
        and rows_x == SUBLANES
        and tiles == 2
        and tiles * tile_depth == depth
        and (params + 1) * depth == LANES
        and 3 * SUBLANES + tiles + params + 1 <= depth
        and rays % RAY_CHUNKS == 0
        and rows_x * params * (SUBLANES + 2 * PASSES) <= 4 * LANES
    )


def shards_by_y(
    tile_bounds, tile_anchor, tile_picks, rmo_picks, sensitivity, dip_class, strength, couple
):
    tiles, rays, params, _, _ = sensitivity.shape
    _, rows_x, rows_y = dip_class.shape
    replicas = lax.axis_size("par")
    devices = lax.axis_size("cols") * replicas
    width = rows_y // devices
    groups = LANES // devices
    hbm = pl.BlockSpec(memory_space=pltpu.HBM)
    vmem = pl.BlockSpec(memory_space=pltpu.VMEM)
    arguments = (
        tile_bounds, tile_anchor, tile_picks, rmo_picks, sensitivity, dip_class, strength, couple
    )
    homes = (
        pltpu.SMEM, pltpu.SMEM, pltpu.SMEM, pltpu.VMEM, pltpu.VMEM, pltpu.VMEM, pltpu.SMEM, pltpu.SMEM
    )
    sent = pl.pallas_call(
        source_kernel,
        out_shape=pltpu.VMEM((devices, width, LANES), jnp.float32),
        in_specs=[hbm] * len(arguments),
        out_specs=vmem,
        scratch_shapes=[home(array.shape, array.dtype) for home, array in zip(homes, arguments)]
        + [
            pltpu.VMEM((tiles, rays, LANES), jnp.float32),
            pltpu.SemaphoreType.DMA((len(arguments) - 1,)),
            pltpu.SemaphoreType.DMA((tiles, RAY_CHUNKS)),
        ],
        compiler_params=pltpu.CompilerParams(vmem_limit_bytes=32 << 20),
        name="sum_rays",
    )(*(pltpu.with_memory_space_constraint(array, pltpu.HBM) for array in arguments))
    received = lax.all_to_all(sent, ("par", "cols"), 0, 0)
    layers = pl.pallas_call(
        functools.partial(
            smooth_kernel,
            params=params,
            tiles=tiles,
            replicas=replicas,
            rows_x=rows_x,
            rows_y=rows_y,
        ),
        out_shape=jax.ShapeDtypeStruct((devices, groups, LANES), jnp.float32),
        in_specs=[vmem],
        out_specs=vmem,
        scratch_shapes=[pltpu.VMEM((rows_x // groups, LANES, LANES), jnp.float32)],
        compiler_params=pltpu.CompilerParams(vmem_limit_bytes=32 << 20),
        name="smooth_block",
    )(received)
    windows = lax.all_to_all(layers, ("par", "cols"), 0, 0)
    return pl.pallas_call(
        functools.partial(collect_kernel, width=width),
        out_shape=jax.ShapeDtypeStruct((params, 1, rows_x, rows_y), jnp.float32),
        in_specs=[vmem],
        out_specs=vmem,
        compiler_params=pltpu.CompilerParams(vmem_limit_bytes=32 << 20),
        name="collect_windows",
    )(windows)


def shards(
    tile_bounds, tile_anchor, tile_picks, rmo_picks, sensitivity, dip_class, strength, couple
):
    devices = lax.axis_size("cols") * lax.axis_size("par")
    plan = shards_by_y if fits(sensitivity, dip_class, devices) else shards_any
    return plan(
        tile_bounds, tile_anchor, tile_picks, rmo_picks, sensitivity, dip_class, strength, couple
    )


def solution(mesh):
    return jax.shard_map(
        shards,
        mesh=mesh,
        in_specs=(
            P(),
            P(("cols", "par"), None),
            P(("cols", "par")),
            P(("cols", "par"), None),
            P(("cols", "par"), None, None, None, None),
            P(("cols", "par"), None, None),
            P(),
            P(),
        ),
        out_specs=P(None, ("cols", "par"), None, None),
        check_vma=False,
    )
```

```python
import functools

import jax
import jax.numpy as jnp
from jax import lax
from jax.experimental import pallas as pl
from jax.experimental.pallas import tpu as pltpu
from jax.sharding import PartitionSpec as P

CAP = 384
PASSES = 6


def extended(block, sides, width):
    for axis, dim in sides:
        count = lax.axis_size(axis)
        forward = [(i, i + 1) for i in range(count - 1)]
        backward = [(target, source) for source, target in forward]
        low = lax.ppermute(
            lax.slice_in_dim(block, block.shape[dim] - width, None, axis=dim), axis, forward
        )
        high = lax.ppermute(lax.slice_in_dim(block, 0, width, axis=dim), axis, backward)
        block = jnp.concatenate([low, block, high], axis=dim)
    return block


def next_cells(values, along_dim):
    count = values.shape[along_dim]
    kept = lax.slice_in_dim(values, 1, count, axis=along_dim)
    zeros = jnp.zeros_like(lax.slice_in_dim(values, 0, 1, axis=along_dim))
    return jnp.concatenate([kept, zeros], axis=along_dim)


def prev_cells(values, along_dim):
    count = values.shape[along_dim]
    kept = lax.slice_in_dim(values, 0, count - 1, axis=along_dim)
    zeros = jnp.zeros_like(lax.slice_in_dim(values, 0, 1, axis=along_dim))
    return jnp.concatenate([zeros, kept], axis=along_dim)


def at_depth(padded, tilt):
    return jnp.where(tilt < 0, padded[:, :-2], jnp.where(tilt > 0, padded[:, 2:], padded[:, 1:-1]))


def smooth_pass(padded, dip_class, strength, mixing):
    centre = padded[:, 1:-1]
    tilt_across = (dip_class // 3 - 1)[None]
    tilt_along = (dip_class % 3 - 1)[None]
    east_side = at_depth(next_cells(padded, 2), tilt_across)
    west_side = at_depth(prev_cells(padded, 2), -tilt_across)
    north_side = at_depth(next_cells(padded, 3), tilt_along)
    south_side = at_depth(prev_cells(padded, 3), -tilt_along)
    laplace = east_side + west_side + north_side + south_side - 4.0 * centre
    smooth = centre + strength[:, None, None, None] * laplace
    return jnp.tensordot(mixing, smooth, axes=1, precision=lax.Precision.HIGHEST)


def shards_any(
    tile_bounds, tile_anchor, tile_picks, rmo_picks, sensitivity, dip_class, strength, couple
):
    tile_count, ray_count, param_count, depth_cells, tile_columns = sensitivity.shape
    col_devices = lax.axis_size("cols")
    par_devices = lax.axis_size("par")
    slab_depth, rows_x, rows_y = dip_class.shape
    total_depth = slab_depth * col_devices * par_devices
    live = jnp.arange(ray_count, dtype=jnp.int32)[None, :] < tile_picks[:, None]
    ray_weight = jnp.where(live, rmo_picks, jnp.zeros_like(rmo_picks))
    contribution = jnp.einsum(
        "tr,trk->tk",
        ray_weight,
        sensitivity.reshape(tile_count, ray_count, -1),
        preferred_element_type=jnp.float32,
    )
    contribution = contribution.reshape(tile_count, param_count, depth_cells, tile_columns)

    def add_tile(tile_number, gradient):
        anchor = (jnp.int32(0), tile_anchor[tile_number, 0], tile_anchor[tile_number, 1])
        current = lax.dynamic_slice(gradient, anchor, (param_count, depth_cells, tile_columns))
        return lax.dynamic_update_slice(gradient, current + contribution[tile_number], anchor)

    gradient = jnp.zeros((param_count, total_depth, CAP), jnp.float32)
    gradient = lax.fori_loop(0, tile_count, add_tile, gradient)
    blocks = gradient.reshape(param_count, col_devices, par_devices, slab_depth, CAP)
    reduced = lax.psum_scatter(blocks, "par", scatter_dimension=2, tiled=True)
    summed = lax.all_to_all(reduced, "cols", split_axis=1, concat_axis=4, tiled=True)
    padded_slots = summed.reshape(param_count, slab_depth, col_devices * CAP)
    columns = rows_x * rows_y
    column_ids = jnp.arange(columns, dtype=jnp.int32)
    starts = tile_bounds[:-1]
    below = starts[None, :] <= column_ids[:, None]
    owner_tile = jnp.sum(below.astype(jnp.int32), axis=1) - 1
    tile_start = jnp.max(jnp.where(below, starts[None, :], jnp.zeros_like(starts)[None, :]), axis=1)
    slot_index = owner_tile * CAP + column_ids - tile_start
    field = jnp.take(padded_slots, slot_index, axis=2).reshape(
        param_count, slab_depth, rows_x, rows_y
    )
    mixing = couple / jnp.sum(couple, axis=1, keepdims=True)
    for _ in range(PASSES):
        padded = extended(field, ((("cols", "par"), 1),), 1)
        field = smooth_pass(padded, dip_class, strength, mixing)
    return field


LANES = 128
SUBLANES = 8
RAY_CHUNKS = 2


def block_index():
    return lax.axis_index("par") * lax.axis_size("cols") + lax.axis_index("cols")


def lane_ids(shape):
    return lax.broadcasted_iota(jnp.int32, shape, len(shape) - 1)


def roll_lanes(values, shift):
    width = values.shape[-1]
    shift = shift % width
    return values if shift == 0 else pltpu.roll(values, shift, values.ndim - 1)


def source_kernel(
    bounds_hbm, anchor_hbm, picks_hbm, rmo_hbm, sens_hbm, dip_hbm, strength_hbm, couple_hbm,
    out_ref,
    bounds_ref, anchor_ref, picks_ref, rmo_ref, sens_ref, dip_ref, strength_ref, couple_ref,
    weight_ref, small_sems, sens_sems,
):
    tiles, rays, params, tile_depth, tile_columns = sens_ref.shape
    _, rows_x, rows_y = dip_ref.shape
    devices, width, _ = out_ref.shape
    halves = rows_y // LANES
    per_tile = sens_sems.shape[1]
    chunk = rays // per_tile
    small = [
        pltpu.make_async_copy(hbm, ref, small_sems.at[number])
        for number, (hbm, ref) in enumerate(
            [
                (picks_hbm, picks_ref),
                (rmo_hbm, rmo_ref),
                (bounds_hbm, bounds_ref),
                (anchor_hbm, anchor_ref),
                (dip_hbm, dip_ref),
                (strength_hbm, strength_ref),
                (couple_hbm, couple_ref),
            ]
        )
    ]
    large = [
        [
            pltpu.make_async_copy(
                sens_hbm.at[tile, pl.ds(part * chunk, chunk)],
                sens_ref.at[tile, pl.ds(part * chunk, chunk)],
                sens_sems.at[tile, part],
            )
            for part in range(per_tile)
        ]
        for tile in range(tiles)
    ]
    for copy in small[:2]:
        copy.start()
    for row in large:
        for copy in row:
            copy.start()
    for copy in small[2:]:
        copy.start()

    diagonal = lax.broadcasted_iota(jnp.int32, (rays, rays), 0) == lane_ids((rays, rays))
    for copy in small:
        copy.wait()
    residuals = rmo_ref[...].astype(jnp.float32)
    for tile in range(tiles):
        live = lane_ids((1, rays)) < picks_ref[tile]
        weight = jnp.where(live, residuals[tile : tile + 1], 0.0)
        column = jnp.sum(jnp.where(diagonal, weight, 0.0), axis=1, keepdims=True)
        weight_ref[tile] = jnp.broadcast_to(column, (rays, LANES))

    y_ids = lane_ids((1, rows_y))
    place_in_packet = lax.rem(y_ids, width)

    def packet_lane(values):
        lane = jnp.zeros((1, rows_y), jnp.float32)
        for q, value in enumerate(values):
            lane = jnp.where(place_in_packet == q, value, lane)
        return lane

    factor_rows = [packet_lane([strength_ref[q] for q in range(params)])]
    for p in range(params):
        weights = [jnp.full((1, rows_y), couple_ref[p, q], jnp.float32) for q in range(params)]
        whole = weights[0]
        for weight in weights[1:]:
            whole = whole + weight
        factor_rows.append(packet_lane([weight / whole for weight in weights]))

    first_depth, lane_first, first_half, x_rows, depth_rows = [], [], [], [], []
    for tile in range(tiles):
        first_depth.append(anchor_ref[tile, 0])
        first = bounds_ref[lax.axis_index("cols")] + anchor_ref[tile, 1]
        first_x = first // rows_y
        first_y = first - first_x * rows_y
        first_half.append(first_y // LANES)
        lane_first.append(first_y - first_half[tile] * LANES)
        at_x = first_x + (y_ids < first_y).astype(jnp.int32)
        x_rows.append(at_x.astype(jnp.float32))
        depth_rows.append(jnp.full((1, rows_y), first_depth[tile], jnp.int32).astype(jnp.float32))
    notes = jnp.concatenate(
        [jnp.zeros((3 * width, rows_y), jnp.float32)]
        + x_rows
        + depth_rows
        + factor_rows,
        axis=0,
    )
    dip = dip_ref[0].astype(jnp.float32)
    count = LANES // width
    for device in range(devices):
        out_ref[device] = roll_lanes(dip, width - device * width)[:, :LANES]

    parts = [[[None] * tiles for _ in range(params)] for _ in range(halves)]
    for tile in range(tiles):
        total = jnp.zeros((params, tile_depth, tile_columns), jnp.float32)
        for ray in range(rays):
            if ray % chunk == 0:
                large[tile][ray // chunk].wait()
            weight = weight_ref[tile, ray : ray + 1, :]
            total = total + weight[None] * sens_ref[tile, ray].astype(jnp.float32)
        past = lane_ids((1, LANES)) >= lane_first[tile]
        for param in range(params):
            turned = pltpu.roll(total[param], lax.rem(first_depth[tile], tile_depth), 0)
            turned = pltpu.roll(turned, lane_first[tile], 1)
            for half in range(halves):
                after = lax.rem(first_half[tile] + 1, halves)
                kept = jnp.logical_or(
                    jnp.logical_and(past, first_half[tile] == half),
                    jnp.logical_and(jnp.logical_not(past), after == half),
                )
                parts[half][param][tile] = jnp.where(kept, turned, 0.0)
    in_window = lane_ids((rows_x, LANES)) < 3 * width
    for half in range(halves):
        rows = [notes[:, half * LANES : (half + 1) * LANES]]
        for param in range(params):
            rows.extend(parts[half][param])
        turned = jnp.transpose(jnp.concatenate(rows, axis=0))
        for place in range(count):
            device = half * count + place
            out_ref[device] = jnp.where(
                in_window, out_ref[device], turned[place * width : (place + 1) * width]
            )


def smooth_kernel(in_ref, out_ref, layer_ref, *, params, tiles, replicas, rows_x, rows_y):
    depth, width, _ = in_ref.shape
    groups = LANES // depth
    halves = rows_x // groups
    rows = 3 * width
    side = rows
    lane = lane_ids((width, LANES))
    low = lane % depth < depth // 2
    in_tile = (lane % (depth // 2)).astype(jnp.float32)
    zero = jnp.zeros((width, LANES), jnp.float32)
    stays = [zero] * rows_x
    moves = [zero] * rows_x
    for source in range(depth):
        message = in_ref[source]
        notes = [
            jnp.broadcast_to(message[:, side + number : side + number + 1], (width, LANES))
            for number in range(2 * tiles)
        ]
        at_x = jnp.where(low, notes[0], notes[1])
        below_first = in_tile < jnp.where(low, notes[2], notes[3])
        stay = jnp.logical_xor(low, below_first)
        at_stay = jnp.where(stay, at_x, -1.0)
        at_move = jnp.where(stay, -1.0, at_x)
        for x in range(rows_x):
            stays[x] = stays[x] + jnp.where(at_stay == float(x), message, 0.0)
            moves[x] = moves[x] + jnp.where(at_move == float(x), message, 0.0)
    block = lane // depth
    current = []
    for param in range(params):
        current.append([])
        for half in range(halves):
            centre = zero
            for group in range(groups):
                x = group * halves + half
                shift = depth * (group - param - 1)
                moved = jnp.where(
                    low,
                    roll_lanes(moves[x], shift - depth // 2),
                    roll_lanes(moves[x], shift + depth // 2),
                )
                centre = jnp.where(block == group, roll_lanes(stays[x], shift) + moved, centre)
            current[param].append([None, centre, None])

    dip = []
    for half in range(halves):
        columns = depth // replicas
        for group in range(groups):
            for replica in range(replicas):
                layer_ref[half, pl.ds(group * depth + replica, columns, replicas), :] = in_ref[
                    replica * columns : (replica + 1) * columns, group * halves + half, :
                ]
        dip.append(jnp.transpose(layer_ref[half])[:rows])

    lanes = lane_ids((rows, LANES))
    z = lanes % depth
    block = lanes // depth
    first = block == 0
    last = block == groups - 1
    bands = range(3)
    own = block_index()
    in_grid = [
        jnp.where(own > 0, 1.0, 0.0),
        1.0,
        jnp.where(own < rows_y // width - 1, 1.0, 0.0),
    ]

    def by_band(values):
        return [values[band * width : (band + 1) * width] for band in bands]

    def factor(lane, q):
        at = side + 2 * tiles + lane
        return jnp.broadcast_to(in_ref[0, q : q + 1, at : at + 1], (width, LANES))

    strengths = [factor(0, q) for q in range(params)]
    keeps = [1.0 / strength - 4.0 for strength in strengths]
    mixing = [
        [
            [factor(p + 1, q) * strengths[q] * in_grid[band] for band in bands]
            for q in range(params)
        ]
        for p in range(params)
    ]

    def codes(tilt, inside=True):
        level = jnp.where(jnp.abs(tilt) < 0.5, 1.0, 0.0)
        above = jnp.where(jnp.logical_and(tilt < -0.5, z > 0), 1.0, 0.0)
        below = jnp.where(jnp.logical_and(tilt > 0.5, z < depth - 1), 1.0, 0.0)
        weights = [by_band(jnp.where(inside, weight, 0.0)) for weight in (level, above, below)]
        return list(zip(*weights))

    def chosen(weights, many):
        results = []
        for values in many:
            if values is None:
                results.append(None)
                continue
            total = values[0] * weights[0]
            for value, weight in zip(values[1:], weights[1:]):
                total = total + value * weight
            results.append(total)
        return results

    def candidates(values, shift):
        if values is None:
            return None
        return [roll_lanes(values, shift + step) for step in (0, 1, -1)]

    row_ids = lax.broadcasted_iota(jnp.int32, (width, LANES), 0)

    def moved_y(here, there, step):
        if here is None and there is None:
            return None
        parts = [
            0.0 if values is None else pltpu.roll(values, step % width, 0) for values in (here, there)
        ]
        return jnp.where(row_ids == (width - 1 if step < 0 else 0), parts[1], parts[0])

    def added(terms):
        terms = [term for term in terms if term is not None]
        total = terms[0] if terms else None
        for term in terms[1:]:
            total = total + term
        return total

    east, west, north, south = [], [], [], []
    for half in range(halves):
        tilt_x = jnp.where(dip[half] < 2.5, -1.0, jnp.where(dip[half] > 5.5, 1.0, 0.0))
        tilt_y = dip[half] - 3.0 * tilt_x - 4.0
        east.append(codes(tilt_x, jnp.logical_or(half + 1 < halves, jnp.logical_not(last))))
        west.append(codes(-tilt_x, jnp.logical_or(half > 0, jnp.logical_not(first))))
        north.append(codes(pltpu.roll(tilt_y, 1, 0)))
        south.append(codes(-pltpu.roll(tilt_y, rows - 1, 0)))

    def prepare(u, half):
        return [
            (
                v,
                candidates(v, 0),
                candidates(v, -depth) if half == 0 else None,
                candidates(v, depth) if half == halves - 1 else None,
            )
            for v in u
        ]

    ready = {
        (half, band): prepare([current[p][half][band] for p in range(params)], half)
        for band in bands
        for half in range(halves)
    }
    def in_turn(weight, earlier):
        return weight if earlier is None else jnp.maximum(weight, jnp.minimum(earlier, -1e30))

    for step in range(PASSES):
        turned_south, turned_north = {}, {}
        following = {}
        done = None

        def to_south(half, band):
            if (half, band) not in turned_south:
                many = [item[1] for item in ready[half, band]]
                turned_south[half, band] = chosen(north[half][band], many)
            return turned_south[half, band]

        def to_north(half, band):
            if (half, band) not in turned_north:
                many = [item[1] for item in ready[half, band]]
                turned_north[half, band] = chosen(south[half][band], many)
            return turned_north[half, band]

        for band in bands:
            for half in range(halves):
                if half + 1 < halves:
                    ahead = [item[1] for item in ready[half + 1, band]]
                else:
                    ahead = [item[2] for item in ready[0, band]]
                if half > 0:
                    behind = [item[1] for item in ready[half - 1, band]]
                else:
                    behind = [item[3] for item in ready[halves - 1, band]]
                level, above, below = east[half][band]
                to_west = chosen((in_turn(level, done), above, below), ahead)
                to_east = chosen(west[half][band], behind)
                sums = []
                for q in range(params):
                    u = ready[half, band][q][0]
                    upper = to_south(half, band + 1)[q] if band + 1 < len(bands) else None
                    lower = to_north(half, band - 1)[q] if band > 0 else None
                    sums.append(
                        added(
                            [
                                to_west[q],
                                to_east[q],
                                None if u is None else keeps[q] * u,
                                moved_y(to_south(half, band)[q], upper, -1),
                                moved_y(to_north(half, band)[q], lower, 1),
                            ]
                        )
                    )
                new = [
                    added([mixing[p][q][band] * sums[q] for q in range(params)])
                    for p in range(params)
                ]
                done = new[0]
                if step + 1 < PASSES:
                    following[half, band] = prepare(new, half)
                else:
                    for p in range(params):
                        current[p][half][band] = new[p]
        ready = following
    current = [[jnp.concatenate(bands_of, axis=0) for bands_of in u] for u in current]

    pieces = []
    for half in range(halves):
        for p in range(params):
            pieces.append(current[p][half][width - PASSES : 2 * width + PASSES])
    used = halves * params * (width + 2 * PASSES)
    pieces.append(jnp.zeros((LANES - used, LANES), jnp.float32))
    layer_ref[0] = jnp.transpose(jnp.concatenate(pieces, axis=0))
    for group in range(groups):
        for replica in range(replicas):
            out_ref[replica * columns : (replica + 1) * columns, group, :] = layer_ref[
                0, pl.ds(group * depth + replica, columns, replicas), :
            ]


def collect_kernel(in_ref, out_ref, *, width):
    params, _, rows_x, rows_y = out_ref.shape
    sources, groups, _ = in_ref.shape
    span = width + 2 * PASSES
    halves = rows_x // groups
    lane = lane_ids((rows_x, LANES))
    totals = [[jnp.zeros((rows_x, LANES), jnp.float32) for _ in range(rows_y // LANES)] for _ in range(params)]
    for source in range(sources):
        message = in_ref[source]
        stacked = jnp.concatenate(
            [roll_lanes(message, -half * params * span) for half in range(halves)], axis=0
        )
        first = source * width - PASSES
        for param in range(params):
            placed = roll_lanes(stacked, first - param * span)
            for column in range(rows_y // LANES):
                low, high = first - column * LANES, first - column * LANES + span
                if high <= 0 or low >= LANES:
                    continue
                inside = jnp.logical_and(lane >= low, lane < high)
                totals[param][column] = totals[param][column] + jnp.where(inside, placed, 0.0)
    for param in range(params):
        for column in range(rows_y // LANES):
            for x in range(rows_x):
                row = (x % halves) * groups + x // halves
                out_ref[param, 0, x : x + 1, column * LANES : (column + 1) * LANES] = totals[param][
                    column
                ][row : row + 1]


def fits(sensitivity, dip_class, devices):
    tiles, rays, params, tile_depth, tile_columns = sensitivity.shape
    slab_depth, rows_x, rows_y = dip_class.shape
    depth = slab_depth * devices
    return (
        slab_depth == 1
        and rows_y == devices * SUBLANES
        and PASSES <= SUBLANES
        and rows_y % LANES == 0
        and tile_columns == LANES
        and rows_x == SUBLANES
        and tiles == 2
        and tiles * tile_depth == depth
        and (params + 1) * depth == LANES
        and 3 * SUBLANES + 2 * tiles + params + 1 == depth
        and rays % RAY_CHUNKS == 0
        and rows_x * params * (SUBLANES + 2 * PASSES) <= 4 * LANES
    )


def shards_by_y(
    tile_bounds, tile_anchor, tile_picks, rmo_picks, sensitivity, dip_class, strength, couple
):
    tiles, rays, params, _, _ = sensitivity.shape
    _, rows_x, rows_y = dip_class.shape
    replicas = lax.axis_size("par")
    devices = lax.axis_size("cols") * replicas
    width = rows_y // devices
    groups = LANES // devices
    hbm = pl.BlockSpec(memory_space=pltpu.HBM)
    vmem = pl.BlockSpec(memory_space=pltpu.VMEM)
    arguments = (
        tile_bounds, tile_anchor, tile_picks, rmo_picks, sensitivity, dip_class, strength, couple
    )
    homes = (
        pltpu.SMEM, pltpu.SMEM, pltpu.SMEM, pltpu.VMEM, pltpu.VMEM, pltpu.VMEM, pltpu.SMEM, pltpu.SMEM
    )
    sent = pl.pallas_call(
        source_kernel,
        out_shape=pltpu.VMEM((devices, width, LANES), jnp.float32),
        in_specs=[hbm] * len(arguments),
        out_specs=vmem,
        scratch_shapes=[home(array.shape, array.dtype) for home, array in zip(homes, arguments)]
        + [
            pltpu.VMEM((tiles, rays, LANES), jnp.float32),
            pltpu.SemaphoreType.DMA((len(arguments) - 1,)),
            pltpu.SemaphoreType.DMA((tiles, RAY_CHUNKS)),
        ],
        compiler_params=pltpu.CompilerParams(vmem_limit_bytes=32 << 20),
        name="sum_rays",
    )(*(pltpu.with_memory_space_constraint(array, pltpu.HBM) for array in arguments))
    received = lax.all_to_all(sent, ("par", "cols"), 0, 0)
    layers = pl.pallas_call(
        functools.partial(
            smooth_kernel,
            params=params,
            tiles=tiles,
            replicas=replicas,
            rows_x=rows_x,
            rows_y=rows_y,
        ),
        out_shape=jax.ShapeDtypeStruct((devices, groups, LANES), jnp.float32),
        in_specs=[vmem],
        out_specs=vmem,
        scratch_shapes=[pltpu.VMEM((rows_x // groups, LANES, LANES), jnp.float32)],
        compiler_params=pltpu.CompilerParams(vmem_limit_bytes=32 << 20),
        name="smooth_block",
    )(received)
    windows = lax.all_to_all(layers, ("par", "cols"), 0, 0)
    return pl.pallas_call(
        functools.partial(collect_kernel, width=width),
        out_shape=jax.ShapeDtypeStruct((params, 1, rows_x, rows_y), jnp.float32),
        in_specs=[vmem],
        out_specs=vmem,
        compiler_params=pltpu.CompilerParams(vmem_limit_bytes=32 << 20),
        name="collect_windows",
    )(windows)


def shards(
    tile_bounds, tile_anchor, tile_picks, rmo_picks, sensitivity, dip_class, strength, couple
):
    devices = lax.axis_size("cols") * lax.axis_size("par")
    plan = shards_by_y if fits(sensitivity, dip_class, devices) else shards_any
    return plan(
        tile_bounds, tile_anchor, tile_picks, rmo_picks, sensitivity, dip_class, strength, couple
    )


def solution(mesh):
    return jax.shard_map(
        shards,
        mesh=mesh,
        in_specs=(
            P(),
            P(("cols", "par"), None),
            P(("cols", "par")),
            P(("cols", "par"), None),
            P(("cols", "par"), None, None, None, None),
            P(("cols", "par"), None, None),
            P(),
            P(),
        ),
        out_specs=P(None, ("cols", "par"), None, None),
        check_vma=False,
    )
```

```python
import functools

import jax
import jax.numpy as jnp
from jax import lax
from jax.experimental import pallas as pl
from jax.experimental.pallas import tpu as pltpu
from jax.sharding import PartitionSpec as P

CAP = 384
PASSES = 6


def extended(block, sides, width):
    for axis, dim in sides:
        count = lax.axis_size(axis)
        forward = [(i, i + 1) for i in range(count - 1)]
        backward = [(target, source) for source, target in forward]
        low = lax.ppermute(
            lax.slice_in_dim(block, block.shape[dim] - width, None, axis=dim), axis, forward
        )
        high = lax.ppermute(lax.slice_in_dim(block, 0, width, axis=dim), axis, backward)
        block = jnp.concatenate([low, block, high], axis=dim)
    return block


def next_cells(values, along_dim):
    count = values.shape[along_dim]
    kept = lax.slice_in_dim(values, 1, count, axis=along_dim)
    zeros = jnp.zeros_like(lax.slice_in_dim(values, 0, 1, axis=along_dim))
    return jnp.concatenate([kept, zeros], axis=along_dim)


def prev_cells(values, along_dim):
    count = values.shape[along_dim]
    kept = lax.slice_in_dim(values, 0, count - 1, axis=along_dim)
    zeros = jnp.zeros_like(lax.slice_in_dim(values, 0, 1, axis=along_dim))
    return jnp.concatenate([zeros, kept], axis=along_dim)


def at_depth(padded, tilt):
    return jnp.where(tilt < 0, padded[:, :-2], jnp.where(tilt > 0, padded[:, 2:], padded[:, 1:-1]))


def smooth_pass(padded, dip_class, strength, mixing):
    centre = padded[:, 1:-1]
    tilt_across = (dip_class // 3 - 1)[None]
    tilt_along = (dip_class % 3 - 1)[None]
    east_side = at_depth(next_cells(padded, 2), tilt_across)
    west_side = at_depth(prev_cells(padded, 2), -tilt_across)
    north_side = at_depth(next_cells(padded, 3), tilt_along)
    south_side = at_depth(prev_cells(padded, 3), -tilt_along)
    laplace = east_side + west_side + north_side + south_side - 4.0 * centre
    smooth = centre + strength[:, None, None, None] * laplace
    return jnp.tensordot(mixing, smooth, axes=1, precision=lax.Precision.HIGHEST)


def shards_any(
    tile_bounds, tile_anchor, tile_picks, rmo_picks, sensitivity, dip_class, strength, couple
):
    tile_count, ray_count, param_count, depth_cells, tile_columns = sensitivity.shape
    col_devices = lax.axis_size("cols")
    par_devices = lax.axis_size("par")
    slab_depth, rows_x, rows_y = dip_class.shape
    total_depth = slab_depth * col_devices * par_devices
    live = jnp.arange(ray_count, dtype=jnp.int32)[None, :] < tile_picks[:, None]
    ray_weight = jnp.where(live, rmo_picks, jnp.zeros_like(rmo_picks))
    contribution = jnp.einsum(
        "tr,trk->tk",
        ray_weight,
        sensitivity.reshape(tile_count, ray_count, -1),
        preferred_element_type=jnp.float32,
    )
    contribution = contribution.reshape(tile_count, param_count, depth_cells, tile_columns)

    def add_tile(tile_number, gradient):
        anchor = (jnp.int32(0), tile_anchor[tile_number, 0], tile_anchor[tile_number, 1])
        current = lax.dynamic_slice(gradient, anchor, (param_count, depth_cells, tile_columns))
        return lax.dynamic_update_slice(gradient, current + contribution[tile_number], anchor)

    gradient = jnp.zeros((param_count, total_depth, CAP), jnp.float32)
    gradient = lax.fori_loop(0, tile_count, add_tile, gradient)
    blocks = gradient.reshape(param_count, col_devices, par_devices, slab_depth, CAP)
    reduced = lax.psum_scatter(blocks, "par", scatter_dimension=2, tiled=True)
    summed = lax.all_to_all(reduced, "cols", split_axis=1, concat_axis=4, tiled=True)
    padded_slots = summed.reshape(param_count, slab_depth, col_devices * CAP)
    columns = rows_x * rows_y
    column_ids = jnp.arange(columns, dtype=jnp.int32)
    starts = tile_bounds[:-1]
    below = starts[None, :] <= column_ids[:, None]
    owner_tile = jnp.sum(below.astype(jnp.int32), axis=1) - 1
    tile_start = jnp.max(jnp.where(below, starts[None, :], jnp.zeros_like(starts)[None, :]), axis=1)
    slot_index = owner_tile * CAP + column_ids - tile_start
    field = jnp.take(padded_slots, slot_index, axis=2).reshape(
        param_count, slab_depth, rows_x, rows_y
    )
    mixing = couple / jnp.sum(couple, axis=1, keepdims=True)
    for _ in range(PASSES):
        padded = extended(field, ((("cols", "par"), 1),), 1)
        field = smooth_pass(padded, dip_class, strength, mixing)
    return field


LANES = 128
SUBLANES = 8
RAY_CHUNKS = 2


def exchange_order(cols, par):
    return sorted(range(cols * par), key=lambda i: (i // par % 2, i % par % 2, i % par // 2, i // par // 2))


def block_index():
    col, replica = lax.axis_index("cols"), lax.axis_index("par")
    odd = lax.rem(col, 2) * 2 + lax.rem(replica, 2)
    return (odd * (lax.axis_size("par") // 2) + replica // 2) * (lax.axis_size("cols") // 2) + col // 2


def lane_ids(shape):
    return lax.broadcasted_iota(jnp.int32, shape, len(shape) - 1)


def roll_lanes(values, shift):
    width = values.shape[-1]
    shift = shift % width
    return values if shift == 0 else pltpu.roll(values, shift, values.ndim - 1)


def source_kernel(
    bounds_hbm, anchor_hbm, picks_hbm, rmo_hbm, sens_hbm, dip_hbm, strength_hbm, couple_hbm,
    out_ref,
    bounds_ref, anchor_ref, picks_ref, rmo_ref, sens_ref, dip_ref, strength_ref, couple_ref,
    weight_ref, small_sems, sens_sems,
):
    tiles, rays, params, tile_depth, tile_columns = sens_ref.shape
    _, rows_x, rows_y = dip_ref.shape
    devices, width, _ = out_ref.shape
    halves = rows_y // LANES
    per_tile = sens_sems.shape[1]
    chunk = rays // per_tile
    small = [
        pltpu.make_async_copy(hbm, ref, small_sems.at[number])
        for number, (hbm, ref) in enumerate(
            [
                (picks_hbm, picks_ref),
                (rmo_hbm, rmo_ref),
                (bounds_hbm, bounds_ref),
                (anchor_hbm, anchor_ref),
                (dip_hbm, dip_ref),
                (strength_hbm, strength_ref),
                (couple_hbm, couple_ref),
            ]
        )
    ]
    large = [
        [
            pltpu.make_async_copy(
                sens_hbm.at[tile, pl.ds(part * chunk, chunk)],
                sens_ref.at[tile, pl.ds(part * chunk, chunk)],
                sens_sems.at[tile, part],
            )
            for part in range(per_tile)
        ]
        for tile in range(tiles)
    ]
    for copy in small[:2]:
        copy.start()
    for row in large:
        for copy in row:
            copy.start()
    for copy in small[2:]:
        copy.start()

    diagonal = lax.broadcasted_iota(jnp.int32, (rays, rays), 0) == lane_ids((rays, rays))
    for copy in small:
        copy.wait()
    residuals = rmo_ref[...].astype(jnp.float32)
    for tile in range(tiles):
        live = lane_ids((1, rays)) < picks_ref[tile]
        weight = jnp.where(live, residuals[tile : tile + 1], 0.0)
        column = jnp.sum(jnp.where(diagonal, weight, 0.0), axis=1, keepdims=True)
        weight_ref[tile] = jnp.broadcast_to(column, (rays, LANES))

    y_ids = lane_ids((1, rows_y))
    place_in_packet = lax.rem(y_ids, width)

    def packet_lane(values):
        lane = jnp.zeros((1, rows_y), jnp.float32)
        for q, value in enumerate(values):
            lane = jnp.where(place_in_packet == q, value, lane)
        return lane

    factor_rows = [packet_lane([strength_ref[q] for q in range(params)])]
    for p in range(params):
        weights = [jnp.full((1, rows_y), couple_ref[p, q], jnp.float32) for q in range(params)]
        whole = weights[0]
        for weight in weights[1:]:
            whole = whole + weight
        factor_rows.append(packet_lane([weight / whole for weight in weights]))

    first_depth, lane_first, first_half, x_rows, depth_rows = [], [], [], [], []
    for tile in range(tiles):
        first_depth.append(anchor_ref[tile, 0])
        first = bounds_ref[lax.axis_index("cols")] + anchor_ref[tile, 1]
        first_x = first // rows_y
        first_y = first - first_x * rows_y
        first_half.append(first_y // LANES)
        lane_first.append(first_y - first_half[tile] * LANES)
        at_x = first_x + (y_ids < first_y).astype(jnp.int32)
        x_rows.append(at_x.astype(jnp.float32))
        depth_rows.append(jnp.full((1, rows_y), first_depth[tile], jnp.int32).astype(jnp.float32))
    notes = jnp.concatenate(
        [jnp.zeros((3 * width, rows_y), jnp.float32)]
        + x_rows
        + depth_rows
        + factor_rows,
        axis=0,
    )
    dip = dip_ref[0].astype(jnp.float32)
    count = LANES // width
    for device in range(devices):
        out_ref[device] = roll_lanes(dip, width - device * width)[:, :LANES]

    parts = [[[None] * tiles for _ in range(params)] for _ in range(halves)]
    for tile in range(tiles):
        total = jnp.zeros((params, tile_depth, tile_columns), jnp.float32)
        for ray in range(rays):
            if ray % chunk == 0:
                large[tile][ray // chunk].wait()
            weight = weight_ref[tile, ray : ray + 1, :]
            total = total + weight[None] * sens_ref[tile, ray].astype(jnp.float32)
        past = lane_ids((1, LANES)) >= lane_first[tile]
        for param in range(params):
            turned = pltpu.roll(total[param], lax.rem(first_depth[tile], tile_depth), 0)
            turned = pltpu.roll(turned, lane_first[tile], 1)
            for half in range(halves):
                after = lax.rem(first_half[tile] + 1, halves)
                kept = jnp.logical_or(
                    jnp.logical_and(past, first_half[tile] == half),
                    jnp.logical_and(jnp.logical_not(past), after == half),
                )
                parts[half][param][tile] = jnp.where(kept, turned, 0.0)
    in_window = lane_ids((rows_x, LANES)) < 3 * width
    for half in range(halves):
        rows = [notes[:, half * LANES : (half + 1) * LANES]]
        for param in range(params):
            rows.extend(parts[half][param])
        turned = jnp.transpose(jnp.concatenate(rows, axis=0))
        for place in range(count):
            device = half * count + place
            out_ref[device] = jnp.where(
                in_window, out_ref[device], turned[place * width : (place + 1) * width]
            )


def smooth_kernel(in_ref, out_ref, layer_ref, skip_ref, *, params, tiles, replicas, rows_x, rows_y):
    depth, width, _ = in_ref.shape
    groups = LANES // depth
    halves = rows_x // groups
    rows = 3 * width
    side = rows
    lane = lane_ids((width, LANES))
    low = lane % depth < depth // 2
    zero = jnp.zeros((width, LANES), jnp.float32)
    all_lanes = lane_ids((depth, LANES))
    all_low = all_lanes % depth < depth // 2
    first_z = [
        jnp.broadcast_to(in_ref[:, 0, side + tiles + tile : side + tiles + tile + 1], (depth, LANES))
        for tile in range(tiles)
    ]
    behind = (all_lanes % (depth // 2)).astype(jnp.float32) < jnp.where(all_low, *first_z)
    stay = jnp.logical_xor(all_low, behind)
    out_of_grid = -2.0 * rows_x
    skip_ref[0] = jnp.where(stay, 0.0, out_of_grid)
    skip_ref[1] = jnp.where(stay, out_of_grid, 0.0)
    stays = [zero] * rows_x
    moves = [zero] * rows_x
    for source in range(depth):
        message = in_ref[source]
        at_x = [
            jnp.broadcast_to(message[:, side + tile : side + tile + 1], (width, LANES))
            for tile in range(tiles)
        ]
        at_x = jnp.where(low, *at_x)
        at_stay = at_x + skip_ref[0, source : source + 1, :]
        at_move = at_x + skip_ref[1, source : source + 1, :]
        for x in range(rows_x):
            stays[x] = stays[x] + jnp.where(at_stay == float(x), message, 0.0)
            moves[x] = moves[x] + jnp.where(at_move == float(x), message, 0.0)
    block = lane // depth
    current = []
    for param in range(params):
        current.append([])
        for half in range(halves):
            centre = zero
            for group in range(groups):
                x = group * halves + half
                shift = depth * (group - param - 1)
                moved = jnp.where(
                    low,
                    roll_lanes(moves[x], shift - depth // 2),
                    roll_lanes(moves[x], shift + depth // 2),
                )
                centre = jnp.where(block == group, roll_lanes(stays[x], shift) + moved, centre)
            current[param].append([None, centre, None])

    run = depth // replicas // 2
    stride = 2 * replicas
    order = exchange_order(depth // replicas, replicas)
    dip = []
    for half in range(halves):
        for group in range(groups):
            for place in range(0, depth, run):
                layer_ref[half, pl.ds(group * depth + order[place], run, stride), :] = in_ref[
                    place : place + run, group * halves + half, :
                ]
        dip.append(jnp.transpose(layer_ref[half])[:rows])

    lanes = lane_ids((rows, LANES))
    z = lanes % depth
    block = lanes // depth
    first = block == 0
    last = block == groups - 1
    bands = range(3)
    own = block_index()
    in_grid = [
        jnp.where(own > 0, 1.0, 0.0),
        1.0,
        jnp.where(own < rows_y // width - 1, 1.0, 0.0),
    ]

    def by_band(values):
        return [values[band * width : (band + 1) * width] for band in bands]

    def factor(lane, q):
        at = side + 2 * tiles + lane
        return jnp.broadcast_to(in_ref[0, q : q + 1, at : at + 1], (width, LANES))

    strengths = [factor(0, q) for q in range(params)]
    keeps = [1.0 / strength - 4.0 for strength in strengths]
    mixing = [
        [
            [factor(p + 1, q) * strengths[q] * in_grid[band] for band in bands]
            for q in range(params)
        ]
        for p in range(params)
    ]

    def codes(tilt, inside=True):
        level = jnp.where(jnp.abs(tilt) < 0.5, 1.0, 0.0)
        above = jnp.where(jnp.logical_and(tilt < -0.5, z > 0), 1.0, 0.0)
        below = jnp.where(jnp.logical_and(tilt > 0.5, z < depth - 1), 1.0, 0.0)
        weights = [by_band(jnp.where(inside, weight, 0.0)) for weight in (level, above, below)]
        return list(zip(*weights))

    def chosen(weights, many):
        results = []
        for values in many:
            if values is None:
                results.append(None)
                continue
            total = values[0] * weights[0]
            for value, weight in zip(values[1:], weights[1:]):
                total = total + value * weight
            results.append(total)
        return results

    def candidates(values, shift):
        if values is None:
            return None
        return [roll_lanes(values, shift + step) for step in (0, 1, -1)]

    row_ids = lax.broadcasted_iota(jnp.int32, (width, LANES), 0)

    def moved_y(here, there, step):
        if here is None and there is None:
            return None
        parts = [
            0.0 if values is None else pltpu.roll(values, step % width, 0) for values in (here, there)
        ]
        return jnp.where(row_ids == (width - 1 if step < 0 else 0), parts[1], parts[0])

    def added(terms):
        terms = [term for term in terms if term is not None]
        total = terms[0] if terms else None
        for term in terms[1:]:
            total = total + term
        return total

    east, west, north, south = [], [], [], []
    for half in range(halves):
        tilt_x = jnp.where(dip[half] < 2.5, -1.0, jnp.where(dip[half] > 5.5, 1.0, 0.0))
        tilt_y = dip[half] - 3.0 * tilt_x - 4.0
        east.append(codes(tilt_x, jnp.logical_or(half + 1 < halves, jnp.logical_not(last))))
        west.append(codes(-tilt_x, jnp.logical_or(half > 0, jnp.logical_not(first))))
        north.append(codes(pltpu.roll(tilt_y, 1, 0)))
        south.append(codes(-pltpu.roll(tilt_y, rows - 1, 0)))

    def prepare(u, half):
        return [
            (
                v,
                candidates(v, 0),
                candidates(v, -depth) if half == 0 else None,
                candidates(v, depth) if half == halves - 1 else None,
            )
            for v in u
        ]

    ready = {
        (half, band): prepare([current[p][half][band] for p in range(params)], half)
        for band in bands
        for half in range(halves)
    }
    def in_turn(weight, earlier):
        return weight if earlier is None else jnp.maximum(weight, jnp.minimum(earlier, -1e30))

    for step in range(PASSES):
        turned_south, turned_north = {}, {}
        following = {}
        done = None

        def to_south(half, band):
            if (half, band) not in turned_south:
                many = [item[1] for item in ready[half, band]]
                turned_south[half, band] = chosen(north[half][band], many)
            return turned_south[half, band]

        def to_north(half, band):
            if (half, band) not in turned_north:
                many = [item[1] for item in ready[half, band]]
                turned_north[half, band] = chosen(south[half][band], many)
            return turned_north[half, band]

        for band in bands:
            for half in range(halves):
                if half + 1 < halves:
                    ahead = [item[1] for item in ready[half + 1, band]]
                else:
                    ahead = [item[2] for item in ready[0, band]]
                if half > 0:
                    behind = [item[1] for item in ready[half - 1, band]]
                else:
                    behind = [item[3] for item in ready[halves - 1, band]]
                level, above, below = east[half][band]
                to_west = chosen((in_turn(level, done), above, below), ahead)
                to_east = chosen(west[half][band], behind)
                sums = []
                for q in range(params):
                    u = ready[half, band][q][0]
                    upper = to_south(half, band + 1)[q] if band + 1 < len(bands) else None
                    lower = to_north(half, band - 1)[q] if band > 0 else None
                    sums.append(
                        added(
                            [
                                to_west[q],
                                to_east[q],
                                None if u is None else keeps[q] * u,
                                moved_y(to_south(half, band)[q], upper, -1),
                                moved_y(to_north(half, band)[q], lower, 1),
                            ]
                        )
                    )
                new = [
                    added([mixing[p][q][band] * sums[q] for q in range(params)])
                    for p in range(params)
                ]
                done = new[0]
                if step + 1 < PASSES:
                    following[half, band] = prepare(new, half)
                else:
                    for p in range(params):
                        current[p][half][band] = new[p]
        ready = following
    current = [[jnp.concatenate(bands_of, axis=0) for bands_of in u] for u in current]

    pieces = []
    for half in range(halves):
        for p in range(params):
            pieces.append(current[p][half][width - PASSES : 2 * width + PASSES])
    used = halves * params * (width + 2 * PASSES)
    pieces.append(jnp.zeros((LANES - used, LANES), jnp.float32))
    layer_ref[0] = jnp.transpose(jnp.concatenate(pieces, axis=0))
    for group in range(groups):
        for place in range(0, depth, run):
            out_ref[place : place + run, group, :] = layer_ref[
                0, pl.ds(group * depth + order[place], run, stride), :
            ]


def collect_kernel(in_ref, out_ref, *, width):
    params, _, rows_x, rows_y = out_ref.shape
    sources, groups, _ = in_ref.shape
    span = width + 2 * PASSES
    halves = rows_x // groups
    lane = lane_ids((rows_x, LANES))
    totals = [[jnp.zeros((rows_x, LANES), jnp.float32) for _ in range(rows_y // LANES)] for _ in range(params)]
    for source in range(sources):
        message = in_ref[source]
        stacked = jnp.concatenate(
            [roll_lanes(message, -half * params * span) for half in range(halves)], axis=0
        )
        first = source * width - PASSES
        for param in range(params):
            placed = roll_lanes(stacked, first - param * span)
            for column in range(rows_y // LANES):
                low, high = first - column * LANES, first - column * LANES + span
                if high <= 0 or low >= LANES:
                    continue
                inside = jnp.logical_and(lane >= low, lane < high)
                totals[param][column] = totals[param][column] + jnp.where(inside, placed, 0.0)
    for param in range(params):
        for column in range(rows_y // LANES):
            for x in range(rows_x):
                row = (x % halves) * groups + x // halves
                out_ref[param, 0, x : x + 1, column * LANES : (column + 1) * LANES] = totals[param][
                    column
                ][row : row + 1]


def fits(sensitivity, dip_class, devices):
    tiles, rays, params, tile_depth, tile_columns = sensitivity.shape
    slab_depth, rows_x, rows_y = dip_class.shape
    depth = slab_depth * devices
    return (
        slab_depth == 1
        and rows_y == devices * SUBLANES
        and PASSES <= SUBLANES
        and rows_y % LANES == 0
        and tile_columns == LANES
        and rows_x == SUBLANES
        and tiles == 2
        and tiles * tile_depth == depth
        and (params + 1) * depth == LANES
        and 3 * SUBLANES + 2 * tiles + params + 1 == depth
        and rays % RAY_CHUNKS == 0
        and lax.axis_size("cols") % 2 == 0
        and lax.axis_size("par") % 2 == 0
        and rows_x * params * (SUBLANES + 2 * PASSES) <= 4 * LANES
    )


def shards_by_y(
    tile_bounds, tile_anchor, tile_picks, rmo_picks, sensitivity, dip_class, strength, couple
):
    tiles, rays, params, _, _ = sensitivity.shape
    _, rows_x, rows_y = dip_class.shape
    replicas = lax.axis_size("par")
    devices = lax.axis_size("cols") * replicas
    exchange = [exchange_order(devices // replicas, replicas)]
    width = rows_y // devices
    groups = LANES // devices
    hbm = pl.BlockSpec(memory_space=pltpu.HBM)
    vmem = pl.BlockSpec(memory_space=pltpu.VMEM)
    arguments = (
        tile_bounds, tile_anchor, tile_picks, rmo_picks, sensitivity, dip_class, strength, couple
    )
    homes = (
        pltpu.SMEM, pltpu.SMEM, pltpu.SMEM, pltpu.VMEM, pltpu.VMEM, pltpu.VMEM, pltpu.SMEM, pltpu.SMEM
    )
    sent = pl.pallas_call(
        source_kernel,
        out_shape=pltpu.VMEM((devices, width, LANES), jnp.float32),
        in_specs=[hbm] * len(arguments),
        out_specs=vmem,
        scratch_shapes=[home(array.shape, array.dtype) for home, array in zip(homes, arguments)]
        + [
            pltpu.VMEM((tiles, rays, LANES), jnp.float32),
            pltpu.SemaphoreType.DMA((len(arguments) - 1,)),
            pltpu.SemaphoreType.DMA((tiles, RAY_CHUNKS)),
        ],
        compiler_params=pltpu.CompilerParams(vmem_limit_bytes=32 << 20),
        name="sum_rays",
    )(*(pltpu.with_memory_space_constraint(array, pltpu.HBM) for array in arguments))
    received = lax.all_to_all(sent, ("cols", "par"), 0, 0, axis_index_groups=exchange)
    layers = pl.pallas_call(
        functools.partial(
            smooth_kernel,
            params=params,
            tiles=tiles,
            replicas=replicas,
            rows_x=rows_x,
            rows_y=rows_y,
        ),
        out_shape=jax.ShapeDtypeStruct((devices, groups, LANES), jnp.float32),
        in_specs=[vmem],
        out_specs=vmem,
        scratch_shapes=[
            pltpu.VMEM((rows_x // groups, LANES, LANES), jnp.float32),
            pltpu.VMEM((2, devices, LANES), jnp.float32),
        ],
        compiler_params=pltpu.CompilerParams(vmem_limit_bytes=32 << 20),
        name="smooth_block",
    )(received)
    windows = lax.all_to_all(layers, ("cols", "par"), 0, 0, axis_index_groups=exchange)
    return pl.pallas_call(
        functools.partial(collect_kernel, width=width),
        out_shape=jax.ShapeDtypeStruct((params, 1, rows_x, rows_y), jnp.float32),
        in_specs=[vmem],
        out_specs=vmem,
        compiler_params=pltpu.CompilerParams(vmem_limit_bytes=32 << 20),
        name="collect_windows",
    )(windows)


def shards(
    tile_bounds, tile_anchor, tile_picks, rmo_picks, sensitivity, dip_class, strength, couple
):
    devices = lax.axis_size("cols") * lax.axis_size("par")
    plan = shards_by_y if fits(sensitivity, dip_class, devices) else shards_any
    return plan(
        tile_bounds, tile_anchor, tile_picks, rmo_picks, sensitivity, dip_class, strength, couple
    )


def solution(mesh):
    return jax.shard_map(
        shards,
        mesh=mesh,
        in_specs=(
            P(),
            P(("cols", "par"), None),
            P(("cols", "par")),
            P(("cols", "par"), None),
            P(("cols", "par"), None, None, None, None),
            P(("cols", "par"), None, None),
            P(),
            P(),
        ),
        out_specs=P(None, ("cols", "par"), None, None),
        check_vma=False,
    )
```

```python
import functools

import jax
import jax.numpy as jnp
from jax import lax
from jax.experimental import pallas as pl
from jax.experimental.pallas import tpu as pltpu
from jax.sharding import PartitionSpec as P

CAP = 384
PASSES = 6


def extended(block, sides, width):
    for axis, dim in sides:
        count = lax.axis_size(axis)
        forward = [(i, i + 1) for i in range(count - 1)]
        backward = [(target, source) for source, target in forward]
        low = lax.ppermute(
            lax.slice_in_dim(block, block.shape[dim] - width, None, axis=dim), axis, forward
        )
        high = lax.ppermute(lax.slice_in_dim(block, 0, width, axis=dim), axis, backward)
        block = jnp.concatenate([low, block, high], axis=dim)
    return block


def next_cells(values, along_dim):
    count = values.shape[along_dim]
    kept = lax.slice_in_dim(values, 1, count, axis=along_dim)
    zeros = jnp.zeros_like(lax.slice_in_dim(values, 0, 1, axis=along_dim))
    return jnp.concatenate([kept, zeros], axis=along_dim)


def prev_cells(values, along_dim):
    count = values.shape[along_dim]
    kept = lax.slice_in_dim(values, 0, count - 1, axis=along_dim)
    zeros = jnp.zeros_like(lax.slice_in_dim(values, 0, 1, axis=along_dim))
    return jnp.concatenate([zeros, kept], axis=along_dim)


def at_depth(padded, tilt):
    return jnp.where(tilt < 0, padded[:, :-2], jnp.where(tilt > 0, padded[:, 2:], padded[:, 1:-1]))


def smooth_pass(padded, dip_class, strength, mixing):
    centre = padded[:, 1:-1]
    tilt_across = (dip_class // 3 - 1)[None]
    tilt_along = (dip_class % 3 - 1)[None]
    east_side = at_depth(next_cells(padded, 2), tilt_across)
    west_side = at_depth(prev_cells(padded, 2), -tilt_across)
    north_side = at_depth(next_cells(padded, 3), tilt_along)
    south_side = at_depth(prev_cells(padded, 3), -tilt_along)
    laplace = east_side + west_side + north_side + south_side - 4.0 * centre
    smooth = centre + strength[:, None, None, None] * laplace
    return jnp.tensordot(mixing, smooth, axes=1, precision=lax.Precision.HIGHEST)


def shards_any(
    tile_bounds, tile_anchor, tile_picks, rmo_picks, sensitivity, dip_class, strength, couple
):
    tile_count, ray_count, param_count, depth_cells, tile_columns = sensitivity.shape
    col_devices = lax.axis_size("cols")
    par_devices = lax.axis_size("par")
    slab_depth, rows_x, rows_y = dip_class.shape
    total_depth = slab_depth * col_devices * par_devices
    live = jnp.arange(ray_count, dtype=jnp.int32)[None, :] < tile_picks[:, None]
    ray_weight = jnp.where(live, rmo_picks, jnp.zeros_like(rmo_picks))
    contribution = jnp.einsum(
        "tr,trk->tk",
        ray_weight,
        sensitivity.reshape(tile_count, ray_count, -1),
        preferred_element_type=jnp.float32,
    )
    contribution = contribution.reshape(tile_count, param_count, depth_cells, tile_columns)

    def add_tile(tile_number, gradient):
        anchor = (jnp.int32(0), tile_anchor[tile_number, 0], tile_anchor[tile_number, 1])
        current = lax.dynamic_slice(gradient, anchor, (param_count, depth_cells, tile_columns))
        return lax.dynamic_update_slice(gradient, current + contribution[tile_number], anchor)

    gradient = jnp.zeros((param_count, total_depth, CAP), jnp.float32)
    gradient = lax.fori_loop(0, tile_count, add_tile, gradient)
    blocks = gradient.reshape(param_count, col_devices, par_devices, slab_depth, CAP)
    reduced = lax.psum_scatter(blocks, "par", scatter_dimension=2, tiled=True)
    summed = lax.all_to_all(reduced, "cols", split_axis=1, concat_axis=4, tiled=True)
    padded_slots = summed.reshape(param_count, slab_depth, col_devices * CAP)
    columns = rows_x * rows_y
    column_ids = jnp.arange(columns, dtype=jnp.int32)
    starts = tile_bounds[:-1]
    below = starts[None, :] <= column_ids[:, None]
    owner_tile = jnp.sum(below.astype(jnp.int32), axis=1) - 1
    tile_start = jnp.max(jnp.where(below, starts[None, :], jnp.zeros_like(starts)[None, :]), axis=1)
    slot_index = owner_tile * CAP + column_ids - tile_start
    field = jnp.take(padded_slots, slot_index, axis=2).reshape(
        param_count, slab_depth, rows_x, rows_y
    )
    mixing = couple / jnp.sum(couple, axis=1, keepdims=True)
    for _ in range(PASSES):
        padded = extended(field, ((("cols", "par"), 1),), 1)
        field = smooth_pass(padded, dip_class, strength, mixing)
    return field


LANES = 128
SUBLANES = 8
RAY_CHUNKS = 2


def exchange_order(cols, par):
    return sorted(range(cols * par), key=lambda i: (i // par % 2, i % par % 2, i % par // 2, i // par // 2))


def block_index():
    col, replica = lax.axis_index("cols"), lax.axis_index("par")
    odd = lax.rem(col, 2) * 2 + lax.rem(replica, 2)
    return (odd * (lax.axis_size("par") // 2) + replica // 2) * (lax.axis_size("cols") // 2) + col // 2


def lane_ids(shape):
    return lax.broadcasted_iota(jnp.int32, shape, len(shape) - 1)


def roll_lanes(values, shift):
    width = values.shape[-1]
    shift = shift % width
    return values if shift == 0 else pltpu.roll(values, shift, values.ndim - 1)


def source_kernel(
    bounds_hbm, anchor_hbm, picks_hbm, rmo_hbm, sens_hbm, dip_hbm, strength_hbm, couple_hbm,
    out_ref,
    bounds_ref, anchor_ref, picks_ref, rmo_ref, sens_ref, dip_ref, strength_ref, couple_ref,
    weight_ref, small_sems, sens_sems,
):
    tiles, rays, params, tile_depth, tile_columns = sens_ref.shape
    _, rows_x, rows_y = dip_ref.shape
    devices, width, _ = out_ref.shape
    halves = rows_y // LANES
    per_tile = sens_sems.shape[1]
    chunk = rays // per_tile
    small = [
        pltpu.make_async_copy(hbm, ref, small_sems.at[number])
        for number, (hbm, ref) in enumerate(
            [
                (picks_hbm, picks_ref),
                (rmo_hbm, rmo_ref),
                (bounds_hbm, bounds_ref),
                (anchor_hbm, anchor_ref),
                (dip_hbm, dip_ref),
                (strength_hbm, strength_ref),
                (couple_hbm, couple_ref),
            ]
        )
    ]
    large = [
        [
            pltpu.make_async_copy(
                sens_hbm.at[tile, pl.ds(part * chunk, chunk)],
                sens_ref.at[tile, pl.ds(part * chunk, chunk)],
                sens_sems.at[tile, part],
            )
            for part in range(per_tile)
        ]
        for tile in range(tiles)
    ]
    for copy in small[:2]:
        copy.start()
    for row in large:
        for copy in row:
            copy.start()
    for copy in small[2:]:
        copy.start()

    diagonal = lax.broadcasted_iota(jnp.int32, (rays, rays), 0) == lane_ids((rays, rays))
    for copy in small:
        copy.wait()
    residuals = rmo_ref[...].astype(jnp.float32)
    for tile in range(tiles):
        live = lane_ids((1, rays)) < picks_ref[tile]
        weight = jnp.where(live, residuals[tile : tile + 1], 0.0)
        column = jnp.sum(jnp.where(diagonal, weight, 0.0), axis=1, keepdims=True)
        weight_ref[tile] = jnp.broadcast_to(column, (rays, LANES))

    y_ids = lane_ids((1, rows_y))
    place_in_packet = lax.rem(y_ids, width)

    def packet_lane(values):
        lane = jnp.zeros((1, rows_y), jnp.float32)
        for q, value in enumerate(values):
            lane = jnp.where(place_in_packet == q, value, lane)
        return lane

    factor_rows = [packet_lane([strength_ref[q] for q in range(params)])]
    for p in range(params):
        weights = [jnp.full((1, rows_y), couple_ref[p, q], jnp.float32) for q in range(params)]
        whole = weights[0]
        for weight in weights[1:]:
            whole = whole + weight
        factor_rows.append(packet_lane([weight / whole for weight in weights]))

    first_depth, lane_first, first_half, x_rows, depth_rows = [], [], [], [], []
    for tile in range(tiles):
        first_depth.append(anchor_ref[tile, 0])
        first = bounds_ref[lax.axis_index("cols")] + anchor_ref[tile, 1]
        first_x = first // rows_y
        first_y = first - first_x * rows_y
        first_half.append(first_y // LANES)
        lane_first.append(first_y - first_half[tile] * LANES)
        at_x = first_x + (y_ids < first_y).astype(jnp.int32)
        x_rows.append(at_x.astype(jnp.float32))
        depth_rows.append(jnp.full((1, rows_y), first_depth[tile], jnp.int32).astype(jnp.float32))
    notes = jnp.concatenate(
        [jnp.zeros((3 * width, rows_y), jnp.float32)]
        + x_rows
        + depth_rows
        + factor_rows,
        axis=0,
    )
    dip = dip_ref[0].astype(jnp.float32)
    count = LANES // width
    for device in range(devices):
        out_ref[device] = roll_lanes(dip, width - device * width)[:, :LANES]

    parts = [[[None] * tiles for _ in range(params)] for _ in range(halves)]
    for tile in range(tiles):
        total = jnp.zeros((params, tile_depth, tile_columns), jnp.float32)
        for ray in range(rays):
            if ray % chunk == 0:
                large[tile][ray // chunk].wait()
            weight = weight_ref[tile, ray : ray + 1, :]
            total = total + weight[None] * sens_ref[tile, ray].astype(jnp.float32)
        past = lane_ids((1, LANES)) >= lane_first[tile]
        for param in range(params):
            turned = pltpu.roll(total[param], lax.rem(first_depth[tile], tile_depth), 0)
            turned = pltpu.roll(turned, lane_first[tile], 1)
            for half in range(halves):
                after = lax.rem(first_half[tile] + 1, halves)
                kept = jnp.logical_or(
                    jnp.logical_and(past, first_half[tile] == half),
                    jnp.logical_and(jnp.logical_not(past), after == half),
                )
                parts[half][param][tile] = jnp.where(kept, turned, 0.0)
    in_window = lane_ids((rows_x, LANES)) < 3 * width
    for half in range(halves):
        rows = [notes[:, half * LANES : (half + 1) * LANES]]
        for param in range(params):
            rows.extend(parts[half][param])
        turned = jnp.transpose(jnp.concatenate(rows, axis=0))
        for place in range(count):
            device = half * count + place
            out_ref[device] = jnp.where(
                in_window, out_ref[device], turned[place * width : (place + 1) * width]
            )


def smooth_kernel(in_ref, out_ref, layer_ref, *, params, tiles, replicas, rows_x, rows_y):
    depth, width, _ = in_ref.shape
    groups = LANES // depth
    halves = rows_x // groups
    rows = 3 * width
    side = rows
    lane = lane_ids((width, LANES))
    low = lane % depth < depth // 2
    in_tile = (lane % (depth // 2)).astype(jnp.float32)
    zero = jnp.zeros((width, LANES), jnp.float32)
    stays = [zero] * rows_x
    moves = [zero] * rows_x
    from_lane = lax.broadcasted_iota(jnp.int32, (LANES, 2 * LANES), 0)
    to_lane = lane_ids((LANES, 2 * LANES))
    tile_of = (to_lane % depth) // (depth // 2)
    spread = from_lane == side + tile_of + jnp.where(to_lane < LANES, 0, tiles)
    packets = in_ref[...].reshape(depth * width, LANES)
    packet_lanes = lane_ids(packets.shape)
    is_note = jnp.logical_and(packet_lanes >= side, packet_lanes < side + 2 * tiles)
    notes = jnp.dot(
        jnp.where(is_note, packets, 0.0).astype(jnp.bfloat16),
        jnp.where(spread, 1.0, 0.0).astype(jnp.bfloat16),
        preferred_element_type=jnp.float32,
    )
    for source in range(depth):
        message = in_ref[source]
        at_x = notes[source * width : (source + 1) * width, :LANES]
        below_first = in_tile < notes[source * width : (source + 1) * width, LANES:]
        stay = jnp.logical_xor(low, below_first)
        at_stay = jnp.where(stay, at_x, -1.0)
        at_move = jnp.where(stay, -1.0, at_x)
        for x in range(rows_x):
            stays[x] = stays[x] + jnp.where(at_stay == float(x), message, 0.0)
            moves[x] = moves[x] + jnp.where(at_move == float(x), message, 0.0)
    block = lane // depth
    current = []
    for param in range(params):
        current.append([])
        for half in range(halves):
            centre = zero
            for group in range(groups):
                x = group * halves + half
                shift = depth * (group - param - 1)
                moved = jnp.where(
                    low,
                    roll_lanes(moves[x], shift - depth // 2),
                    roll_lanes(moves[x], shift + depth // 2),
                )
                centre = jnp.where(block == group, roll_lanes(stays[x], shift) + moved, centre)
            current[param].append([None, centre, None])

    run = depth // replicas // 2
    stride = 2 * replicas
    order = exchange_order(depth // replicas, replicas)
    dip = []
    for half in range(halves):
        for group in range(groups):
            for place in range(0, depth, run):
                layer_ref[half, pl.ds(group * depth + order[place], run, stride), :] = in_ref[
                    place : place + run, group * halves + half, :
                ]
        dip.append(jnp.transpose(layer_ref[half])[:rows])

    lanes = lane_ids((rows, LANES))
    z = lanes % depth
    block = lanes // depth
    first = block == 0
    last = block == groups - 1
    bands = range(3)
    own = block_index()
    in_grid = [
        jnp.where(own > 0, 1.0, 0.0),
        1.0,
        jnp.where(own < rows_y // width - 1, 1.0, 0.0),
    ]

    def by_band(values):
        return [values[band * width : (band + 1) * width] for band in bands]

    def factor(lane, q):
        at = side + 2 * tiles + lane
        return jnp.broadcast_to(in_ref[0, q : q + 1, at : at + 1], (width, LANES))

    strengths = [factor(0, q) for q in range(params)]
    keeps = [1.0 / strength - 4.0 for strength in strengths]
    mixing = [
        [
            [factor(p + 1, q) * strengths[q] * in_grid[band] for band in bands]
            for q in range(params)
        ]
        for p in range(params)
    ]

    def codes(tilt, inside=True):
        level = jnp.where(jnp.abs(tilt) < 0.5, 1.0, 0.0)
        above = jnp.where(jnp.logical_and(tilt < -0.5, z > 0), 1.0, 0.0)
        below = jnp.where(jnp.logical_and(tilt > 0.5, z < depth - 1), 1.0, 0.0)
        weights = [by_band(jnp.where(inside, weight, 0.0)) for weight in (level, above, below)]
        return list(zip(*weights))

    def chosen(weights, many):
        results = []
        for values in many:
            if values is None:
                results.append(None)
                continue
            total = values[0] * weights[0]
            for value, weight in zip(values[1:], weights[1:]):
                total = total + value * weight
            results.append(total)
        return results

    def candidates(values, shift):
        if values is None:
            return None
        return [roll_lanes(values, shift + step) for step in (0, 1, -1)]

    row_ids = lax.broadcasted_iota(jnp.int32, (width, LANES), 0)

    def moved_y(here, there, step):
        if here is None and there is None:
            return None
        parts = [
            0.0 if values is None else pltpu.roll(values, step % width, 0) for values in (here, there)
        ]
        return jnp.where(row_ids == (width - 1 if step < 0 else 0), parts[1], parts[0])

    def added(terms):
        terms = [term for term in terms if term is not None]
        total = terms[0] if terms else None
        for term in terms[1:]:
            total = total + term
        return total

    east, west, north, south = [], [], [], []
    for half in range(halves):
        tilt_x = jnp.where(dip[half] < 2.5, -1.0, jnp.where(dip[half] > 5.5, 1.0, 0.0))
        tilt_y = dip[half] - 3.0 * tilt_x - 4.0
        east.append(codes(tilt_x, jnp.logical_or(half + 1 < halves, jnp.logical_not(last))))
        west.append(codes(-tilt_x, jnp.logical_or(half > 0, jnp.logical_not(first))))
        north.append(codes(pltpu.roll(tilt_y, 1, 0)))
        south.append(codes(-pltpu.roll(tilt_y, rows - 1, 0)))

    def prepare(u, half):
        return [
            (
                v,
                candidates(v, 0),
                candidates(v, -depth) if half == 0 else None,
                candidates(v, depth) if half == halves - 1 else None,
            )
            for v in u
        ]

    ready = {
        (half, band): prepare([current[p][half][band] for p in range(params)], half)
        for band in bands
        for half in range(halves)
    }
    def in_turn(weight, earlier):
        return weight if earlier is None else jnp.maximum(weight, jnp.minimum(earlier, -1e30))

    for step in range(PASSES):
        turned_south, turned_north = {}, {}
        following = {}
        done = None

        def to_south(half, band):
            if (half, band) not in turned_south:
                many = [item[1] for item in ready[half, band]]
                turned_south[half, band] = chosen(north[half][band], many)
            return turned_south[half, band]

        def to_north(half, band):
            if (half, band) not in turned_north:
                many = [item[1] for item in ready[half, band]]
                turned_north[half, band] = chosen(south[half][band], many)
            return turned_north[half, band]

        for band in bands:
            for half in range(halves):
                if half + 1 < halves:
                    ahead = [item[1] for item in ready[half + 1, band]]
                else:
                    ahead = [item[2] for item in ready[0, band]]
                if half > 0:
                    behind = [item[1] for item in ready[half - 1, band]]
                else:
                    behind = [item[3] for item in ready[halves - 1, band]]
                level, above, below = east[half][band]
                to_west = chosen((in_turn(level, done), above, below), ahead)
                to_east = chosen(west[half][band], behind)
                sums = []
                for q in range(params):
                    u = ready[half, band][q][0]
                    upper = to_south(half, band + 1)[q] if band + 1 < len(bands) else None
                    lower = to_north(half, band - 1)[q] if band > 0 else None
                    sums.append(
                        added(
                            [
                                to_west[q],
                                to_east[q],
                                None if u is None else keeps[q] * u,
                                moved_y(to_south(half, band)[q], upper, -1),
                                moved_y(to_north(half, band)[q], lower, 1),
                            ]
                        )
                    )
                new = [
                    added([mixing[p][q][band] * sums[q] for q in range(params)])
                    for p in range(params)
                ]
                done = new[0]
                if step + 1 < PASSES:
                    following[half, band] = prepare(new, half)
                else:
                    for p in range(params):
                        current[p][half][band] = new[p]
        ready = following
    current = [[jnp.concatenate(bands_of, axis=0) for bands_of in u] for u in current]

    pieces = []
    for half in range(halves):
        for p in range(params):
            pieces.append(current[p][half][width - PASSES : 2 * width + PASSES])
    used = halves * params * (width + 2 * PASSES)
    pieces.append(jnp.zeros((LANES - used, LANES), jnp.float32))
    layer_ref[0] = jnp.transpose(jnp.concatenate(pieces, axis=0))
    for group in range(groups):
        for place in range(0, depth, run):
            out_ref[place : place + run, group, :] = layer_ref[
                0, pl.ds(group * depth + order[place], run, stride), :
            ]


def collect_kernel(in_ref, out_ref, *, width):
    params, _, rows_x, rows_y = out_ref.shape
    sources, groups, _ = in_ref.shape
    span = width + 2 * PASSES
    halves = rows_x // groups
    lane = lane_ids((rows_x, LANES))
    totals = [[jnp.zeros((rows_x, LANES), jnp.float32) for _ in range(rows_y // LANES)] for _ in range(params)]
    for source in range(sources):
        message = in_ref[source]
        stacked = jnp.concatenate(
            [roll_lanes(message, -half * params * span) for half in range(halves)], axis=0
        )
        first = source * width - PASSES
        for param in range(params):
            placed = roll_lanes(stacked, first - param * span)
            for column in range(rows_y // LANES):
                low, high = first - column * LANES, first - column * LANES + span
                if high <= 0 or low >= LANES:
                    continue
                inside = jnp.logical_and(lane >= low, lane < high)
                totals[param][column] = totals[param][column] + jnp.where(inside, placed, 0.0)
    for param in range(params):
        for column in range(rows_y // LANES):
            for x in range(rows_x):
                row = (x % halves) * groups + x // halves
                out_ref[param, 0, x : x + 1, column * LANES : (column + 1) * LANES] = totals[param][
                    column
                ][row : row + 1]


def fits(sensitivity, dip_class, devices):
    tiles, rays, params, tile_depth, tile_columns = sensitivity.shape
    slab_depth, rows_x, rows_y = dip_class.shape
    depth = slab_depth * devices
    return (
        slab_depth == 1
        and rows_y == devices * SUBLANES
        and PASSES <= SUBLANES
        and rows_y % LANES == 0
        and tile_columns == LANES
        and rows_x == SUBLANES
        and tiles == 2
        and tiles * tile_depth == depth
        and (params + 1) * depth == LANES
        and 3 * SUBLANES + 2 * tiles + params + 1 == depth
        and rays % RAY_CHUNKS == 0
        and lax.axis_size("cols") % 2 == 0
        and lax.axis_size("par") % 2 == 0
        and rows_x * params * (SUBLANES + 2 * PASSES) <= 4 * LANES
    )


def shards_by_y(
    tile_bounds, tile_anchor, tile_picks, rmo_picks, sensitivity, dip_class, strength, couple
):
    tiles, rays, params, _, _ = sensitivity.shape
    _, rows_x, rows_y = dip_class.shape
    replicas = lax.axis_size("par")
    devices = lax.axis_size("cols") * replicas
    exchange = [exchange_order(devices // replicas, replicas)]
    width = rows_y // devices
    groups = LANES // devices
    hbm = pl.BlockSpec(memory_space=pltpu.HBM)
    vmem = pl.BlockSpec(memory_space=pltpu.VMEM)
    arguments = (
        tile_bounds, tile_anchor, tile_picks, rmo_picks, sensitivity, dip_class, strength, couple
    )
    homes = (
        pltpu.SMEM, pltpu.SMEM, pltpu.SMEM, pltpu.VMEM, pltpu.VMEM, pltpu.VMEM, pltpu.SMEM, pltpu.SMEM
    )
    sent = pl.pallas_call(
        source_kernel,
        out_shape=pltpu.VMEM((devices, width, LANES), jnp.float32),
        in_specs=[hbm] * len(arguments),
        out_specs=vmem,
        scratch_shapes=[home(array.shape, array.dtype) for home, array in zip(homes, arguments)]
        + [
            pltpu.VMEM((tiles, rays, LANES), jnp.float32),
            pltpu.SemaphoreType.DMA((len(arguments) - 1,)),
            pltpu.SemaphoreType.DMA((tiles, RAY_CHUNKS)),
        ],
        compiler_params=pltpu.CompilerParams(vmem_limit_bytes=32 << 20),
        name="sum_rays",
    )(*(pltpu.with_memory_space_constraint(array, pltpu.HBM) for array in arguments))
    received = lax.all_to_all(sent, ("cols", "par"), 0, 0, axis_index_groups=exchange)
    layers = pl.pallas_call(
        functools.partial(
            smooth_kernel,
            params=params,
            tiles=tiles,
            replicas=replicas,
            rows_x=rows_x,
            rows_y=rows_y,
        ),
        out_shape=jax.ShapeDtypeStruct((devices, groups, LANES), jnp.float32),
        in_specs=[vmem],
        out_specs=vmem,
        scratch_shapes=[pltpu.VMEM((rows_x // groups, LANES, LANES), jnp.float32)],
        compiler_params=pltpu.CompilerParams(vmem_limit_bytes=32 << 20),
        name="smooth_block",
    )(received)
    windows = lax.all_to_all(layers, ("cols", "par"), 0, 0, axis_index_groups=exchange)
    return pl.pallas_call(
        functools.partial(collect_kernel, width=width),
        out_shape=jax.ShapeDtypeStruct((params, 1, rows_x, rows_y), jnp.float32),
        in_specs=[vmem],
        out_specs=vmem,
        compiler_params=pltpu.CompilerParams(vmem_limit_bytes=32 << 20),
        name="collect_windows",
    )(windows)


def shards(
    tile_bounds, tile_anchor, tile_picks, rmo_picks, sensitivity, dip_class, strength, couple
):
    devices = lax.axis_size("cols") * lax.axis_size("par")
    plan = shards_by_y if fits(sensitivity, dip_class, devices) else shards_any
    return plan(
        tile_bounds, tile_anchor, tile_picks, rmo_picks, sensitivity, dip_class, strength, couple
    )


def solution(mesh):
    return jax.shard_map(
        shards,
        mesh=mesh,
        in_specs=(
            P(),
            P(("cols", "par"), None),
            P(("cols", "par")),
            P(("cols", "par"), None),
            P(("cols", "par"), None, None, None, None),
            P(("cols", "par"), None, None),
            P(),
            P(),
        ),
        out_specs=P(None, ("cols", "par"), None, None),
        check_vma=False,
    )
```

```python
import functools

import jax
import jax.numpy as jnp
from jax import lax
from jax.experimental import pallas as pl
from jax.experimental.pallas import tpu as pltpu
from jax.sharding import PartitionSpec as P

CAP = 384
PASSES = 6


def extended(block, sides, width):
    for axis, dim in sides:
        count = lax.axis_size(axis)
        forward = [(i, i + 1) for i in range(count - 1)]
        backward = [(target, source) for source, target in forward]
        low = lax.ppermute(
            lax.slice_in_dim(block, block.shape[dim] - width, None, axis=dim), axis, forward
        )
        high = lax.ppermute(lax.slice_in_dim(block, 0, width, axis=dim), axis, backward)
        block = jnp.concatenate([low, block, high], axis=dim)
    return block


def next_cells(values, along_dim):
    count = values.shape[along_dim]
    kept = lax.slice_in_dim(values, 1, count, axis=along_dim)
    zeros = jnp.zeros_like(lax.slice_in_dim(values, 0, 1, axis=along_dim))
    return jnp.concatenate([kept, zeros], axis=along_dim)


def prev_cells(values, along_dim):
    count = values.shape[along_dim]
    kept = lax.slice_in_dim(values, 0, count - 1, axis=along_dim)
    zeros = jnp.zeros_like(lax.slice_in_dim(values, 0, 1, axis=along_dim))
    return jnp.concatenate([zeros, kept], axis=along_dim)


def at_depth(padded, tilt):
    return jnp.where(tilt < 0, padded[:, :-2], jnp.where(tilt > 0, padded[:, 2:], padded[:, 1:-1]))


def smooth_pass(padded, dip_class, strength, mixing):
    centre = padded[:, 1:-1]
    tilt_across = (dip_class // 3 - 1)[None]
    tilt_along = (dip_class % 3 - 1)[None]
    east_side = at_depth(next_cells(padded, 2), tilt_across)
    west_side = at_depth(prev_cells(padded, 2), -tilt_across)
    north_side = at_depth(next_cells(padded, 3), tilt_along)
    south_side = at_depth(prev_cells(padded, 3), -tilt_along)
    laplace = east_side + west_side + north_side + south_side - 4.0 * centre
    smooth = centre + strength[:, None, None, None] * laplace
    return jnp.tensordot(mixing, smooth, axes=1, precision=lax.Precision.HIGHEST)


def shards_any(
    tile_bounds, tile_anchor, tile_picks, rmo_picks, sensitivity, dip_class, strength, couple
):
    tile_count, ray_count, param_count, depth_cells, tile_columns = sensitivity.shape
    col_devices = lax.axis_size("cols")
    par_devices = lax.axis_size("par")
    slab_depth, rows_x, rows_y = dip_class.shape
    total_depth = slab_depth * col_devices * par_devices
    live = jnp.arange(ray_count, dtype=jnp.int32)[None, :] < tile_picks[:, None]
    ray_weight = jnp.where(live, rmo_picks, jnp.zeros_like(rmo_picks))
    contribution = jnp.einsum(
        "tr,trk->tk",
        ray_weight,
        sensitivity.reshape(tile_count, ray_count, -1),
        preferred_element_type=jnp.float32,
    )
    contribution = contribution.reshape(tile_count, param_count, depth_cells, tile_columns)

    def add_tile(tile_number, gradient):
        anchor = (jnp.int32(0), tile_anchor[tile_number, 0], tile_anchor[tile_number, 1])
        current = lax.dynamic_slice(gradient, anchor, (param_count, depth_cells, tile_columns))
        return lax.dynamic_update_slice(gradient, current + contribution[tile_number], anchor)

    gradient = jnp.zeros((param_count, total_depth, CAP), jnp.float32)
    gradient = lax.fori_loop(0, tile_count, add_tile, gradient)
    blocks = gradient.reshape(param_count, col_devices, par_devices, slab_depth, CAP)
    reduced = lax.psum_scatter(blocks, "par", scatter_dimension=2, tiled=True)
    summed = lax.all_to_all(reduced, "cols", split_axis=1, concat_axis=4, tiled=True)
    padded_slots = summed.reshape(param_count, slab_depth, col_devices * CAP)
    columns = rows_x * rows_y
    column_ids = jnp.arange(columns, dtype=jnp.int32)
    starts = tile_bounds[:-1]
    below = starts[None, :] <= column_ids[:, None]
    owner_tile = jnp.sum(below.astype(jnp.int32), axis=1) - 1
    tile_start = jnp.max(jnp.where(below, starts[None, :], jnp.zeros_like(starts)[None, :]), axis=1)
    slot_index = owner_tile * CAP + column_ids - tile_start
    field = jnp.take(padded_slots, slot_index, axis=2).reshape(
        param_count, slab_depth, rows_x, rows_y
    )
    mixing = couple / jnp.sum(couple, axis=1, keepdims=True)
    for _ in range(PASSES):
        padded = extended(field, ((("cols", "par"), 1),), 1)
        field = smooth_pass(padded, dip_class, strength, mixing)
    return field


LANES = 128
SUBLANES = 8
RAY_CHUNKS = 2


def exchange_order(cols, par):
    return sorted(range(cols * par), key=lambda i: (i // par % 2, i % par % 2, i % par // 2, i // par // 2))


def block_index():
    col, replica = lax.axis_index("cols"), lax.axis_index("par")
    odd = lax.rem(col, 2) * 2 + lax.rem(replica, 2)
    return (odd * (lax.axis_size("par") // 2) + replica // 2) * (lax.axis_size("cols") // 2) + col // 2


def lane_ids(shape):
    return lax.broadcasted_iota(jnp.int32, shape, len(shape) - 1)


def roll_lanes(values, shift):
    width = values.shape[-1]
    shift = shift % width
    return values if shift == 0 else pltpu.roll(values, shift, values.ndim - 1)


def source_kernel(
    bounds_hbm, anchor_hbm, picks_hbm, rmo_hbm, sens_hbm, dip_hbm, strength_hbm, couple_hbm,
    out_ref,
    bounds_ref, anchor_ref, picks_ref, rmo_ref, sens_ref, dip_ref, strength_ref, couple_ref,
    weight_ref, small_sems, sens_sems,
):
    tiles, rays, params, tile_depth, tile_columns = sens_ref.shape
    _, rows_x, rows_y = dip_ref.shape
    devices, width, _ = out_ref.shape
    halves = rows_y // LANES
    per_tile = sens_sems.shape[1]
    chunk = rays // per_tile
    small = [
        pltpu.make_async_copy(hbm, ref, small_sems.at[number])
        for number, (hbm, ref) in enumerate(
            [
                (picks_hbm, picks_ref),
                (rmo_hbm, rmo_ref),
                (bounds_hbm, bounds_ref),
                (anchor_hbm, anchor_ref),
                (dip_hbm, dip_ref),
                (strength_hbm, strength_ref),
                (couple_hbm, couple_ref),
            ]
        )
    ]
    large = [
        [
            pltpu.make_async_copy(
                sens_hbm.at[tile, pl.ds(part * chunk, chunk)],
                sens_ref.at[tile, pl.ds(part * chunk, chunk)],
                sens_sems.at[tile, part],
            )
            for part in range(per_tile)
        ]
        for tile in range(tiles)
    ]
    for copy in small[:2]:
        copy.start()
    for row in large:
        for copy in row:
            copy.start()
    for copy in small[2:]:
        copy.start()

    diagonal = lax.broadcasted_iota(jnp.int32, (rays, rays), 0) == lane_ids((rays, rays))
    for copy in small:
        copy.wait()
    residuals = rmo_ref[...].astype(jnp.float32)
    for tile in range(tiles):
        live = lane_ids((1, rays)) < picks_ref[tile]
        weight = jnp.where(live, residuals[tile : tile + 1], 0.0)
        column = jnp.sum(jnp.where(diagonal, weight, 0.0), axis=1, keepdims=True)
        weight_ref[tile] = jnp.broadcast_to(column, (rays, LANES))

    y_ids = lane_ids((1, rows_y))
    place_in_packet = lax.rem(y_ids, width)

    def packet_lane(values):
        lane = jnp.zeros((1, rows_y), jnp.float32)
        for q, value in enumerate(values):
            lane = jnp.where(place_in_packet == q, value, lane)
        return lane

    factors = [jnp.full((1, rows_y), strength_ref[q], jnp.float32) for q in range(params)]
    for p in range(params):
        weights = [jnp.full((1, rows_y), couple_ref[p, q], jnp.float32) for q in range(params)]
        whole = weights[0]
        for weight in weights[1:]:
            whole = whole + weight
        factors.extend(weight / whole for weight in weights)

    factor_rows = [
        packet_lane(factors[first : first + 2 * params]) for first in range(0, len(factors), 2 * params)
    ]
    column_first = bounds_ref[lax.axis_index("cols")]
    column_x = column_first // rows_y
    from_x = column_x + (y_ids < column_first - column_x * rows_y).astype(jnp.int32)
    first_depth, lane_first, first_half, x_rows, depth_rows = [], [], [], [], []
    for tile in range(tiles):
        first_depth.append(anchor_ref[tile, 0])
        first = column_first + anchor_ref[tile, 1]
        first_x = first // rows_y
        first_y = first - first_x * rows_y
        first_half.append(first_y // LANES)
        lane_first.append(first_y - first_half[tile] * LANES)
        at_x = first_x + (y_ids < first_y).astype(jnp.int32)
        x_rows.append((at_x - from_x).astype(jnp.float32))
        depth_rows.append(jnp.full((1, rows_y), first_depth[tile], jnp.int32).astype(jnp.float32))
    notes = jnp.concatenate(
        [jnp.zeros((3 * width, rows_y), jnp.float32)]
        + x_rows
        + depth_rows
        + [from_x.astype(jnp.float32)]
        + factor_rows
        + [jnp.zeros((devices - 3 * width - 2 * tiles - 1 - len(factor_rows), rows_y), jnp.float32)],
        axis=0,
    )
    dip = dip_ref[0].astype(jnp.float32)
    count = LANES // width
    for device in range(devices):
        out_ref[device] = roll_lanes(dip, width - device * width)[:, :LANES]

    parts = [[[None] * tiles for _ in range(params)] for _ in range(halves)]
    for tile in range(tiles):
        total = jnp.zeros((params, tile_depth, tile_columns), jnp.float32)
        for ray in range(rays):
            if ray % chunk == 0:
                large[tile][ray // chunk].wait()
            weight = weight_ref[tile, ray : ray + 1, :]
            total = total + weight[None] * sens_ref[tile, ray].astype(jnp.float32)
        past = lane_ids((1, LANES)) >= lane_first[tile]
        for param in range(params):
            turned = pltpu.roll(total[param], lax.rem(first_depth[tile], tile_depth), 0)
            turned = pltpu.roll(turned, lane_first[tile], 1)
            for half in range(halves):
                after = lax.rem(first_half[tile] + 1, halves)
                kept = jnp.logical_or(
                    jnp.logical_and(past, first_half[tile] == half),
                    jnp.logical_and(jnp.logical_not(past), after == half),
                )
                parts[half][param][tile] = jnp.where(kept, turned, 0.0)
    in_window = lane_ids((rows_x, LANES)) < 3 * width
    for half in range(halves):
        rows = [notes[:, half * LANES : (half + 1) * LANES]]
        for param in range(params):
            rows.extend(parts[half][param])
        turned = jnp.transpose(jnp.concatenate(rows, axis=0))
        for place in range(count):
            device = half * count + place
            out_ref[device] = jnp.where(
                in_window, out_ref[device], turned[place * width : (place + 1) * width]
            )


def smooth_kernel(in_ref, out_ref, layer_ref, *, params, tiles, replicas, rows_x, rows_y):
    depth, width, _ = in_ref.shape
    groups = LANES // depth
    halves = rows_x // groups
    rows = 3 * width
    side = rows
    lane = lane_ids((width, LANES))
    low = lane % depth < depth // 2
    in_tile = (lane % (depth // 2)).astype(jnp.float32)
    zero = jnp.zeros((width, LANES), jnp.float32)
    stays = [zero] * rows_x
    moves = [zero] * rows_x
    from_lane = lax.broadcasted_iota(jnp.int32, (LANES, 3 * LANES), 0)
    to_lane = lane_ids((LANES, 3 * LANES))
    tile_of = (to_lane % depth) // (depth // 2)
    spread = from_lane == side + jnp.where(
        to_lane < 2 * LANES, tile_of + jnp.where(to_lane < LANES, 0, tiles), 2 * tiles
    )
    packets = in_ref[...].reshape(depth * width, LANES)
    packet_lanes = lane_ids(packets.shape)
    is_note = jnp.logical_and(packet_lanes >= side, packet_lanes <= side + 2 * tiles)
    notes = jnp.dot(
        jnp.where(is_note, packets, 0.0).astype(jnp.bfloat16),
        jnp.where(spread, 1.0, 0.0).astype(jnp.bfloat16),
        preferred_element_type=jnp.float32,
    )
    columns = depth // replicas
    places = {device: place for place, device in enumerate(exchange_order(columns, replicas))}
    for column in range(columns):
        near = [[zero, zero], [zero, zero]]
        for replica in range(replicas):
            place = places[column * replicas + replica]
            message = in_ref[place]
            rows_of = slice(place * width, (place + 1) * width)
            second = notes[rows_of, :LANES] > 0.5
            stay = jnp.logical_xor(low, in_tile < notes[rows_of, LANES : 2 * LANES])
            for sums, values in zip(near, (jnp.where(stay, message, 0.0), jnp.where(stay, 0.0, message))):
                sums[0] = sums[0] + jnp.where(second, 0.0, values)
                sums[1] = sums[1] + jnp.where(second, values, 0.0)
        from_x = notes[rows_of, 2 * LANES :]
        for x in range(rows_x):
            here = from_x == float(x)
            for field, sums in zip((stays, moves), near):
                field[x] = field[x] + jnp.where(here, sums[0], 0.0)
                if x + 1 < rows_x:
                    field[x + 1] = field[x + 1] + jnp.where(here, sums[1], 0.0)

    block = lane // depth
    current = []
    for param in range(params):
        current.append([])
        for half in range(halves):
            centre = zero
            for group in range(groups):
                x = group * halves + half
                shift = depth * (group - param - 1)
                moved = jnp.where(
                    low,
                    roll_lanes(moves[x], shift - depth // 2),
                    roll_lanes(moves[x], shift + depth // 2),
                )
                centre = jnp.where(block == group, roll_lanes(stays[x], shift) + moved, centre)
            current[param].append([None, centre, None])

    run = depth // replicas // 2
    stride = 2 * replicas
    order = exchange_order(depth // replicas, replicas)
    dip = []
    for half in range(halves):
        for group in range(groups):
            for place in range(0, depth, run):
                layer_ref[half, pl.ds(group * depth + order[place], run, stride), :] = in_ref[
                    place : place + run, group * halves + half, :
                ]
        dip.append(jnp.transpose(layer_ref[half])[:rows])

    lanes = lane_ids((rows, LANES))
    z = lanes % depth
    block = lanes // depth
    first = block == 0
    last = block == groups - 1
    bands = range(3)
    own = block_index()
    in_grid = [
        jnp.where(own > 0, 1.0, 0.0),
        1.0,
        jnp.where(own < rows_y // width - 1, 1.0, 0.0),
    ]

    def by_band(values):
        return [values[band * width : (band + 1) * width] for band in bands]

    def factor(lane, q):
        number = lane * params + q
        at = side + 2 * tiles + 1 + number // (2 * params)
        row = number % (2 * params)
        return jnp.broadcast_to(in_ref[0, row : row + 1, at : at + 1], (width, LANES))

    strengths = [factor(0, q) for q in range(params)]
    keeps = [1.0 / strength - 4.0 for strength in strengths]
    mixing = [
        [
            [factor(p + 1, q) * strengths[q] * in_grid[band] for band in bands]
            for q in range(params)
        ]
        for p in range(params)
    ]

    def codes(tilt, inside=True):
        level = jnp.where(jnp.abs(tilt) < 0.5, 1.0, 0.0)
        above = jnp.where(jnp.logical_and(tilt < -0.5, z > 0), 1.0, 0.0)
        below = jnp.where(jnp.logical_and(tilt > 0.5, z < depth - 1), 1.0, 0.0)
        weights = [by_band(jnp.where(inside, weight, 0.0)) for weight in (level, above, below)]
        return list(zip(*weights))

    def chosen(weights, many):
        results = []
        for values in many:
            if values is None:
                results.append(None)
                continue
            total = values[0] * weights[0]
            for value, weight in zip(values[1:], weights[1:]):
                total = total + value * weight
            results.append(total)
        return results

    def candidates(values, shift):
        if values is None:
            return None
        return [roll_lanes(values, shift + step) for step in (0, 1, -1)]

    row_ids = lax.broadcasted_iota(jnp.int32, (width, LANES), 0)

    def moved_y(here, there, step):
        if here is None and there is None:
            return None
        parts = [
            0.0 if values is None else pltpu.roll(values, step % width, 0) for values in (here, there)
        ]
        return jnp.where(row_ids == (width - 1 if step < 0 else 0), parts[1], parts[0])

    def added(terms):
        terms = [term for term in terms if term is not None]
        total = terms[0] if terms else None
        for term in terms[1:]:
            total = total + term
        return total

    east, west, north, south = [], [], [], []
    for half in range(halves):
        tilt_x = jnp.where(dip[half] < 2.5, -1.0, jnp.where(dip[half] > 5.5, 1.0, 0.0))
        tilt_y = dip[half] - 3.0 * tilt_x - 4.0
        east.append(codes(tilt_x, jnp.logical_or(half + 1 < halves, jnp.logical_not(last))))
        west.append(codes(-tilt_x, jnp.logical_or(half > 0, jnp.logical_not(first))))
        north.append(codes(pltpu.roll(tilt_y, 1, 0)))
        south.append(codes(-pltpu.roll(tilt_y, rows - 1, 0)))

    def prepare(u, half):
        return [
            (
                v,
                candidates(v, 0),
                candidates(v, -depth) if half == 0 else None,
                candidates(v, depth) if half == halves - 1 else None,
            )
            for v in u
        ]

    ready = {
        (half, band): prepare([current[p][half][band] for p in range(params)], half)
        for band in bands
        for half in range(halves)
    }
    def in_turn(weight, earlier):
        return weight if earlier is None else jnp.maximum(weight, jnp.minimum(earlier, -1e30))

    for step in range(PASSES):
        turned_south, turned_north = {}, {}
        following = {}
        done = None

        def to_south(half, band):
            if (half, band) not in turned_south:
                many = [item[1] for item in ready[half, band]]
                turned_south[half, band] = chosen(north[half][band], many)
            return turned_south[half, band]

        def to_north(half, band):
            if (half, band) not in turned_north:
                many = [item[1] for item in ready[half, band]]
                turned_north[half, band] = chosen(south[half][band], many)
            return turned_north[half, band]

        for band in bands:
            for half in range(halves):
                if half + 1 < halves:
                    ahead = [item[1] for item in ready[half + 1, band]]
                else:
                    ahead = [item[2] for item in ready[0, band]]
                if half > 0:
                    behind = [item[1] for item in ready[half - 1, band]]
                else:
                    behind = [item[3] for item in ready[halves - 1, band]]
                level, above, below = east[half][band]
                to_west = chosen((in_turn(level, done), above, below), ahead)
                to_east = chosen(west[half][band], behind)
                sums = []
                for q in range(params):
                    u = ready[half, band][q][0]
                    upper = to_south(half, band + 1)[q] if band + 1 < len(bands) else None
                    lower = to_north(half, band - 1)[q] if band > 0 else None
                    sums.append(
                        added(
                            [
                                to_west[q],
                                to_east[q],
                                None if u is None else keeps[q] * u,
                                moved_y(to_south(half, band)[q], upper, -1),
                                moved_y(to_north(half, band)[q], lower, 1),
                            ]
                        )
                    )
                new = [
                    added([mixing[p][q][band] * sums[q] for q in range(params)])
                    for p in range(params)
                ]
                done = new[0]
                if step + 1 < PASSES:
                    following[half, band] = prepare(new, half)
                else:
                    for p in range(params):
                        current[p][half][band] = new[p]
        ready = following
    current = [[jnp.concatenate(bands_of, axis=0) for bands_of in u] for u in current]

    pieces = []
    for half in range(halves):
        for p in range(params):
            pieces.append(current[p][half][width - PASSES : 2 * width + PASSES])
    used = halves * params * (width + 2 * PASSES)
    pieces.append(jnp.zeros((LANES - used, LANES), jnp.float32))
    layer_ref[0] = jnp.transpose(jnp.concatenate(pieces, axis=0))
    for group in range(groups):
        for place in range(0, depth, run):
            out_ref[place : place + run, group, :] = layer_ref[
                0, pl.ds(group * depth + order[place], run, stride), :
            ]


def collect_kernel(in_ref, out_ref, *, width):
    params, _, rows_x, rows_y = out_ref.shape
    sources, groups, _ = in_ref.shape
    span = width + 2 * PASSES
    halves = rows_x // groups
    lane = lane_ids((rows_x, LANES))
    totals = [[jnp.zeros((rows_x, LANES), jnp.float32) for _ in range(rows_y // LANES)] for _ in range(params)]
    for source in range(sources):
        message = in_ref[source]
        stacked = jnp.concatenate(
            [roll_lanes(message, -half * params * span) for half in range(halves)], axis=0
        )
        first = source * width - PASSES
        for param in range(params):
            placed = roll_lanes(stacked, first - param * span)
            for column in range(rows_y // LANES):
                low, high = first - column * LANES, first - column * LANES + span
                if high <= 0 or low >= LANES:
                    continue
                inside = jnp.logical_and(lane >= low, lane < high)
                totals[param][column] = totals[param][column] + jnp.where(inside, placed, 0.0)
    for param in range(params):
        for column in range(rows_y // LANES):
            for x in range(rows_x):
                row = (x % halves) * groups + x // halves
                out_ref[param, 0, x : x + 1, column * LANES : (column + 1) * LANES] = totals[param][
                    column
                ][row : row + 1]


def fits(sensitivity, dip_class, devices):
    tiles, rays, params, tile_depth, tile_columns = sensitivity.shape
    slab_depth, rows_x, rows_y = dip_class.shape
    depth = slab_depth * devices
    return (
        slab_depth == 1
        and rows_y == devices * SUBLANES
        and PASSES <= SUBLANES
        and rows_y % LANES == 0
        and tile_columns == LANES
        and rows_x == SUBLANES
        and tiles == 2
        and tiles * tile_depth == depth
        and (params + 1) * depth == LANES
        and 2 * params <= SUBLANES
        and 3 * SUBLANES + 2 * tiles + 1 + (params + 2) // 2 < depth
        and CAP <= 2 * rows_y
        and rays % RAY_CHUNKS == 0
        and lax.axis_size("cols") % 2 == 0
        and lax.axis_size("par") % 2 == 0
        and rows_x * params * (SUBLANES + 2 * PASSES) <= 4 * LANES
    )


def shards_by_y(
    tile_bounds, tile_anchor, tile_picks, rmo_picks, sensitivity, dip_class, strength, couple
):
    tiles, rays, params, _, _ = sensitivity.shape
    _, rows_x, rows_y = dip_class.shape
    replicas = lax.axis_size("par")
    devices = lax.axis_size("cols") * replicas
    exchange = [exchange_order(devices // replicas, replicas)]
    width = rows_y // devices
    groups = LANES // devices
    hbm = pl.BlockSpec(memory_space=pltpu.HBM)
    vmem = pl.BlockSpec(memory_space=pltpu.VMEM)
    arguments = (
        tile_bounds, tile_anchor, tile_picks, rmo_picks, sensitivity, dip_class, strength, couple
    )
    homes = (
        pltpu.SMEM, pltpu.SMEM, pltpu.SMEM, pltpu.VMEM, pltpu.VMEM, pltpu.VMEM, pltpu.SMEM, pltpu.SMEM
    )
    sent = pl.pallas_call(
        source_kernel,
        out_shape=pltpu.VMEM((devices, width, LANES), jnp.float32),
        in_specs=[hbm] * len(arguments),
        out_specs=vmem,
        scratch_shapes=[home(array.shape, array.dtype) for home, array in zip(homes, arguments)]
        + [
            pltpu.VMEM((tiles, rays, LANES), jnp.float32),
            pltpu.SemaphoreType.DMA((len(arguments) - 1,)),
            pltpu.SemaphoreType.DMA((tiles, RAY_CHUNKS)),
        ],
        compiler_params=pltpu.CompilerParams(vmem_limit_bytes=32 << 20),
        name="sum_rays",
    )(*(pltpu.with_memory_space_constraint(array, pltpu.HBM) for array in arguments))
    received = lax.all_to_all(sent, ("cols", "par"), 0, 0, axis_index_groups=exchange)
    layers = pl.pallas_call(
        functools.partial(
            smooth_kernel,
            params=params,
            tiles=tiles,
            replicas=replicas,
            rows_x=rows_x,
            rows_y=rows_y,
        ),
        out_shape=jax.ShapeDtypeStruct((devices, groups, LANES), jnp.float32),
        in_specs=[vmem],
        out_specs=vmem,
        scratch_shapes=[pltpu.VMEM((rows_x // groups, LANES, LANES), jnp.float32)],
        compiler_params=pltpu.CompilerParams(vmem_limit_bytes=32 << 20),
        name="smooth_block",
    )(received)
    windows = lax.all_to_all(layers, ("cols", "par"), 0, 0, axis_index_groups=exchange)
    return pl.pallas_call(
        functools.partial(collect_kernel, width=width),
        out_shape=jax.ShapeDtypeStruct((params, 1, rows_x, rows_y), jnp.float32),
        in_specs=[vmem],
        out_specs=vmem,
        compiler_params=pltpu.CompilerParams(vmem_limit_bytes=32 << 20),
        name="collect_windows",
    )(windows)


def shards(
    tile_bounds, tile_anchor, tile_picks, rmo_picks, sensitivity, dip_class, strength, couple
):
    devices = lax.axis_size("cols") * lax.axis_size("par")
    plan = shards_by_y if fits(sensitivity, dip_class, devices) else shards_any
    return plan(
        tile_bounds, tile_anchor, tile_picks, rmo_picks, sensitivity, dip_class, strength, couple
    )


def solution(mesh):
    return jax.shard_map(
        shards,
        mesh=mesh,
        in_specs=(
            P(),
            P(("cols", "par"), None),
            P(("cols", "par")),
            P(("cols", "par"), None),
            P(("cols", "par"), None, None, None, None),
            P(("cols", "par"), None, None),
            P(),
            P(),
        ),
        out_specs=P(None, ("cols", "par"), None, None),
        check_vma=False,
    )
```

```python
import functools

import jax
import jax.numpy as jnp
from jax import lax
from jax.experimental import pallas as pl
from jax.experimental.pallas import tpu as pltpu
from jax.sharding import PartitionSpec as P

CAP = 384
PASSES = 6


def extended(block, sides, width):
    for axis, dim in sides:
        count = lax.axis_size(axis)
        forward = [(i, i + 1) for i in range(count - 1)]
        backward = [(target, source) for source, target in forward]
        low = lax.ppermute(
            lax.slice_in_dim(block, block.shape[dim] - width, None, axis=dim), axis, forward
        )
        high = lax.ppermute(lax.slice_in_dim(block, 0, width, axis=dim), axis, backward)
        block = jnp.concatenate([low, block, high], axis=dim)
    return block


def next_cells(values, along_dim):
    count = values.shape[along_dim]
    kept = lax.slice_in_dim(values, 1, count, axis=along_dim)
    zeros = jnp.zeros_like(lax.slice_in_dim(values, 0, 1, axis=along_dim))
    return jnp.concatenate([kept, zeros], axis=along_dim)


def prev_cells(values, along_dim):
    count = values.shape[along_dim]
    kept = lax.slice_in_dim(values, 0, count - 1, axis=along_dim)
    zeros = jnp.zeros_like(lax.slice_in_dim(values, 0, 1, axis=along_dim))
    return jnp.concatenate([zeros, kept], axis=along_dim)


def at_depth(padded, tilt):
    return jnp.where(tilt < 0, padded[:, :-2], jnp.where(tilt > 0, padded[:, 2:], padded[:, 1:-1]))


def smooth_pass(padded, dip_class, strength, mixing):
    centre = padded[:, 1:-1]
    tilt_across = (dip_class // 3 - 1)[None]
    tilt_along = (dip_class % 3 - 1)[None]
    east_side = at_depth(next_cells(padded, 2), tilt_across)
    west_side = at_depth(prev_cells(padded, 2), -tilt_across)
    north_side = at_depth(next_cells(padded, 3), tilt_along)
    south_side = at_depth(prev_cells(padded, 3), -tilt_along)
    laplace = east_side + west_side + north_side + south_side - 4.0 * centre
    smooth = centre + strength[:, None, None, None] * laplace
    return jnp.tensordot(mixing, smooth, axes=1, precision=lax.Precision.HIGHEST)


def shards_any(
    tile_bounds, tile_anchor, tile_picks, rmo_picks, sensitivity, dip_class, strength, couple
):
    tile_count, ray_count, param_count, depth_cells, tile_columns = sensitivity.shape
    col_devices = lax.axis_size("cols")
    par_devices = lax.axis_size("par")
    slab_depth, rows_x, rows_y = dip_class.shape
    total_depth = slab_depth * col_devices * par_devices
    live = jnp.arange(ray_count, dtype=jnp.int32)[None, :] < tile_picks[:, None]
    ray_weight = jnp.where(live, rmo_picks, jnp.zeros_like(rmo_picks))
    contribution = jnp.einsum(
        "tr,trk->tk",
        ray_weight,
        sensitivity.reshape(tile_count, ray_count, -1),
        preferred_element_type=jnp.float32,
    )
    contribution = contribution.reshape(tile_count, param_count, depth_cells, tile_columns)

    def add_tile(tile_number, gradient):
        anchor = (jnp.int32(0), tile_anchor[tile_number, 0], tile_anchor[tile_number, 1])
        current = lax.dynamic_slice(gradient, anchor, (param_count, depth_cells, tile_columns))
        return lax.dynamic_update_slice(gradient, current + contribution[tile_number], anchor)

    gradient = jnp.zeros((param_count, total_depth, CAP), jnp.float32)
    gradient = lax.fori_loop(0, tile_count, add_tile, gradient)
    blocks = gradient.reshape(param_count, col_devices, par_devices, slab_depth, CAP)
    reduced = lax.psum_scatter(blocks, "par", scatter_dimension=2, tiled=True)
    summed = lax.all_to_all(reduced, "cols", split_axis=1, concat_axis=4, tiled=True)
    padded_slots = summed.reshape(param_count, slab_depth, col_devices * CAP)
    columns = rows_x * rows_y
    column_ids = jnp.arange(columns, dtype=jnp.int32)
    starts = tile_bounds[:-1]
    below = starts[None, :] <= column_ids[:, None]
    owner_tile = jnp.sum(below.astype(jnp.int32), axis=1) - 1
    tile_start = jnp.max(jnp.where(below, starts[None, :], jnp.zeros_like(starts)[None, :]), axis=1)
    slot_index = owner_tile * CAP + column_ids - tile_start
    field = jnp.take(padded_slots, slot_index, axis=2).reshape(
        param_count, slab_depth, rows_x, rows_y
    )
    mixing = couple / jnp.sum(couple, axis=1, keepdims=True)
    for _ in range(PASSES):
        padded = extended(field, ((("cols", "par"), 1),), 1)
        field = smooth_pass(padded, dip_class, strength, mixing)
    return field


LANES = 128
SUBLANES = 8
RAY_CHUNKS = 2


def exchange_order(cols, par):
    return sorted(range(cols * par), key=lambda i: (i // par % 2, i % par % 2, i % par // 2, i // par // 2))


def block_index():
    col, replica = lax.axis_index("cols"), lax.axis_index("par")
    odd = lax.rem(col, 2) * 2 + lax.rem(replica, 2)
    return (odd * (lax.axis_size("par") // 2) + replica // 2) * (lax.axis_size("cols") // 2) + col // 2


def lane_ids(shape):
    return lax.broadcasted_iota(jnp.int32, shape, len(shape) - 1)


def roll_lanes(values, shift):
    width = values.shape[-1]
    shift = shift % width
    return values if shift == 0 else pltpu.roll(values, shift, values.ndim - 1)


def source_kernel(
    bounds_hbm, anchor_hbm, picks_hbm, rmo_hbm, sens_hbm, dip_hbm, strength_hbm, couple_hbm,
    out_ref,
    bounds_ref, anchor_ref, picks_ref, rmo_ref, sens_ref, dip_ref, strength_ref, couple_ref,
    weight_ref, small_sems, sens_sems,
):
    tiles, rays, params, tile_depth, tile_columns = sens_ref.shape
    _, rows_x, rows_y = dip_ref.shape
    devices, width, _ = out_ref.shape
    halves = rows_y // LANES
    per_tile = sens_sems.shape[1]
    chunk = rays // per_tile
    small = [
        pltpu.make_async_copy(hbm, ref, small_sems.at[number])
        for number, (hbm, ref) in enumerate(
            [
                (picks_hbm, picks_ref),
                (rmo_hbm, rmo_ref),
                (bounds_hbm, bounds_ref),
                (anchor_hbm, anchor_ref),
                (dip_hbm, dip_ref),
                (strength_hbm, strength_ref),
                (couple_hbm, couple_ref),
            ]
        )
    ]
    large = [
        [
            pltpu.make_async_copy(
                sens_hbm.at[tile, pl.ds(part * chunk, chunk)],
                sens_ref.at[tile, pl.ds(part * chunk, chunk)],
                sens_sems.at[tile, part],
            )
            for part in range(per_tile)
        ]
        for tile in range(tiles)
    ]
    for copy in small[:2]:
        copy.start()
    for row in large:
        for copy in row:
            copy.start()
    for copy in small[2:]:
        copy.start()

    diagonal = lax.broadcasted_iota(jnp.int32, (rays, rays), 0) == lane_ids((rays, rays))
    for copy in small:
        copy.wait()
    residuals = rmo_ref[...].astype(jnp.float32)
    for tile in range(tiles):
        live = lane_ids((1, rays)) < picks_ref[tile]
        weight = jnp.where(live, residuals[tile : tile + 1], 0.0)
        column = jnp.sum(jnp.where(diagonal, weight, 0.0), axis=1, keepdims=True)
        weight_ref[tile] = jnp.broadcast_to(column, (rays, LANES))

    y_ids = lane_ids((1, rows_y))
    place_in_packet = lax.rem(y_ids, width)

    def packet_lane(values):
        lane = jnp.zeros((1, rows_y), jnp.float32)
        for q, value in enumerate(values):
            lane = jnp.where(place_in_packet == q, value, lane)
        return lane

    factors = [jnp.full((1, rows_y), strength_ref[q], jnp.float32) for q in range(params)]
    for p in range(params):
        weights = [jnp.full((1, rows_y), couple_ref[p, q], jnp.float32) for q in range(params)]
        whole = weights[0]
        for weight in weights[1:]:
            whole = whole + weight
        factors.extend(weight / whole for weight in weights)

    factor_rows = [
        packet_lane(factors[first : first + 2 * params]) for first in range(0, len(factors), 2 * params)
    ]
    column_first = bounds_ref[lax.axis_index("cols")]
    column_x = column_first // rows_y
    from_x = column_x + (y_ids < column_first - column_x * rows_y).astype(jnp.int32)
    first_depth, lane_first, first_half, x_rows, depth_rows = [], [], [], [], []
    for tile in range(tiles):
        first_depth.append(anchor_ref[tile, 0])
        first = column_first + anchor_ref[tile, 1]
        first_x = first // rows_y
        first_y = first - first_x * rows_y
        first_half.append(first_y // LANES)
        lane_first.append(first_y - first_half[tile] * LANES)
        at_x = first_x + (y_ids < first_y).astype(jnp.int32)
        x_rows.append((at_x - from_x).astype(jnp.float32))
        depth_rows.append(jnp.full((1, rows_y), first_depth[tile], jnp.int32).astype(jnp.float32))
    notes = jnp.concatenate(
        [jnp.zeros((3 * width, rows_y), jnp.float32)]
        + x_rows
        + depth_rows
        + [from_x.astype(jnp.float32)]
        + factor_rows
        + [jnp.zeros((devices - 3 * width - 2 * tiles - 1 - len(factor_rows), rows_y), jnp.float32)],
        axis=0,
    )
    dip = dip_ref[0].astype(jnp.float32)
    count = LANES // width
    for device in range(devices):
        out_ref[device] = roll_lanes(dip, width - device * width)[:, :LANES]

    parts = [[[None] * tiles for _ in range(params)] for _ in range(halves)]
    for tile in range(tiles):
        total = jnp.zeros((params, tile_depth, tile_columns), jnp.float32)
        for ray in range(rays):
            if ray % chunk == 0:
                large[tile][ray // chunk].wait()
            weight = weight_ref[tile, ray : ray + 1, :]
            total = total + weight[None] * sens_ref[tile, ray].astype(jnp.float32)
        past = lane_ids((1, LANES)) >= lane_first[tile]
        for param in range(params):
            turned = pltpu.roll(total[param], lax.rem(first_depth[tile], tile_depth), 0)
            turned = pltpu.roll(turned, lane_first[tile], 1)
            for half in range(halves):
                after = lax.rem(first_half[tile] + 1, halves)
                kept = jnp.logical_or(
                    jnp.logical_and(past, first_half[tile] == half),
                    jnp.logical_and(jnp.logical_not(past), after == half),
                )
                parts[half][param][tile] = jnp.where(kept, turned, 0.0)
    in_window = lane_ids((rows_x, LANES)) < 3 * width
    for half in range(halves):
        rows = [notes[:, half * LANES : (half + 1) * LANES]]
        for param in range(params):
            rows.extend(parts[half][param])
        turned = jnp.transpose(jnp.concatenate(rows, axis=0))
        for place in range(count):
            device = half * count + place
            out_ref[device] = jnp.where(
                in_window, out_ref[device], turned[place * width : (place + 1) * width]
            )


def smooth_kernel(in_ref, out_ref, layer_ref, *, params, tiles, replicas, rows_x, rows_y):
    depth, width, _ = in_ref.shape
    groups = LANES // depth
    halves = rows_x // groups
    rows = 3 * width
    side = rows
    lane = lane_ids((width, LANES))
    low = lane % depth < depth // 2
    in_tile = (lane % (depth // 2)).astype(jnp.float32)
    zero = jnp.zeros((width, LANES), jnp.float32)
    run = depth // replicas // 2
    stride = 2 * replicas
    order = exchange_order(depth // replicas, replicas)
    dip = []
    for half in range(halves):
        for group in range(groups):
            for place in range(0, depth, run):
                layer_ref[half, pl.ds(group * depth + order[place], run, stride), :] = in_ref[
                    place : place + run, group * halves + half, :
                ]
        dip.append(jnp.transpose(layer_ref[half])[:rows])

    stays = [zero] * rows_x
    moves = [zero] * rows_x
    from_lane = lax.broadcasted_iota(jnp.int32, (LANES, 3 * LANES), 0)
    to_lane = lane_ids((LANES, 3 * LANES))
    tile_of = (to_lane % depth) // (depth // 2)
    spread = from_lane == side + jnp.where(
        to_lane < 2 * LANES, tile_of + jnp.where(to_lane < LANES, 0, tiles), 2 * tiles
    )
    packets = in_ref[...].reshape(depth * width, LANES)
    packet_lanes = lane_ids(packets.shape)
    is_note = jnp.logical_and(packet_lanes >= side, packet_lanes <= side + 2 * tiles)
    notes = jnp.dot(
        jnp.where(is_note, packets, 0.0).astype(jnp.bfloat16),
        jnp.where(spread, 1.0, 0.0).astype(jnp.bfloat16),
        preferred_element_type=jnp.float32,
    )
    columns = depth // replicas
    places = {device: place for place, device in enumerate(exchange_order(columns, replicas))}
    for column in range(columns):
        near = [[zero, zero], [zero, zero]]
        for replica in range(replicas):
            place = places[column * replicas + replica]
            message = in_ref[place]
            rows_of = slice(place * width, (place + 1) * width)
            second = notes[rows_of, :LANES] > 0.5
            stay = jnp.logical_xor(low, in_tile < notes[rows_of, LANES : 2 * LANES])
            for sums, values in zip(near, (jnp.where(stay, message, 0.0), jnp.where(stay, 0.0, message))):
                sums[0] = sums[0] + jnp.where(second, 0.0, values)
                sums[1] = sums[1] + jnp.where(second, values, 0.0)
        from_x = notes[rows_of, 2 * LANES :]
        for x in range(rows_x):
            here = from_x == float(x)
            for field, sums in zip((stays, moves), near):
                field[x] = field[x] + jnp.where(here, sums[0], 0.0)
                if x + 1 < rows_x:
                    field[x + 1] = field[x + 1] + jnp.where(here, sums[1], 0.0)

    block = lane // depth
    current = []
    for param in range(params):
        current.append([])
        for half in range(halves):
            centre = zero
            for group in range(groups):
                x = group * halves + half
                shift = depth * (group - param - 1)
                moved = jnp.where(
                    low,
                    roll_lanes(moves[x], shift - depth // 2),
                    roll_lanes(moves[x], shift + depth // 2),
                )
                centre = jnp.where(block == group, roll_lanes(stays[x], shift) + moved, centre)
            current[param].append([None, centre, None])

    lanes = lane_ids((rows, LANES))
    z = lanes % depth
    block = lanes // depth
    first = block == 0
    last = block == groups - 1
    bands = range(3)
    own = block_index()
    in_grid = [
        jnp.where(own > 0, 1.0, 0.0),
        1.0,
        jnp.where(own < rows_y // width - 1, 1.0, 0.0),
    ]

    def by_band(values):
        return [values[band * width : (band + 1) * width] for band in bands]

    def factor(lane, q):
        number = lane * params + q
        at = side + 2 * tiles + 1 + number // (2 * params)
        row = number % (2 * params)
        return jnp.broadcast_to(in_ref[0, row : row + 1, at : at + 1], (width, LANES))

    strengths = [factor(0, q) for q in range(params)]
    keeps = [1.0 / strength - 4.0 for strength in strengths]
    mixing = [
        [
            [factor(p + 1, q) * strengths[q] * in_grid[band] for band in bands]
            for q in range(params)
        ]
        for p in range(params)
    ]

    def codes(tilt, inside=True):
        level = jnp.where(jnp.abs(tilt) < 0.5, 1.0, 0.0)
        above = jnp.where(jnp.logical_and(tilt < -0.5, z > 0), 1.0, 0.0)
        below = jnp.where(jnp.logical_and(tilt > 0.5, z < depth - 1), 1.0, 0.0)
        weights = [by_band(jnp.where(inside, weight, 0.0)) for weight in (level, above, below)]
        return list(zip(*weights))

    def chosen(weights, many):
        results = []
        for values in many:
            if values is None:
                results.append(None)
                continue
            total = values[0] * weights[0]
            for value, weight in zip(values[1:], weights[1:]):
                total = total + value * weight
            results.append(total)
        return results

    def candidates(values, shift):
        if values is None:
            return None
        return [roll_lanes(values, shift + step) for step in (0, 1, -1)]

    row_ids = lax.broadcasted_iota(jnp.int32, (width, LANES), 0)

    def moved_y(here, there, step):
        if here is None and there is None:
            return None
        parts = [
            0.0 if values is None else pltpu.roll(values, step % width, 0) for values in (here, there)
        ]
        return jnp.where(row_ids == (width - 1 if step < 0 else 0), parts[1], parts[0])

    def added(terms):
        terms = [term for term in terms if term is not None]
        total = terms[0] if terms else None
        for term in terms[1:]:
            total = total + term
        return total

    east, west, north, south = [], [], [], []
    for half in range(halves):
        tilt_x = jnp.where(dip[half] < 2.5, -1.0, jnp.where(dip[half] > 5.5, 1.0, 0.0))
        tilt_y = dip[half] - 3.0 * tilt_x - 4.0
        east.append(codes(tilt_x, jnp.logical_or(half + 1 < halves, jnp.logical_not(last))))
        west.append(codes(-tilt_x, jnp.logical_or(half > 0, jnp.logical_not(first))))
        north.append(codes(pltpu.roll(tilt_y, 1, 0)))
        south.append(codes(-pltpu.roll(tilt_y, rows - 1, 0)))

    def prepare(u, half):
        return [
            (
                v,
                candidates(v, 0),
                candidates(v, -depth) if half == 0 else None,
                candidates(v, depth) if half == halves - 1 else None,
            )
            for v in u
        ]

    ready = {
        (half, band): prepare([current[p][half][band] for p in range(params)], half)
        for band in bands
        for half in range(halves)
    }
    def in_turn(weight, earlier):
        return weight if earlier is None else jnp.maximum(weight, jnp.minimum(earlier, -1e30))

    for step in range(PASSES):
        turned_south, turned_north = {}, {}
        following = {}
        done = None

        def to_south(half, band):
            if (half, band) not in turned_south:
                many = [item[1] for item in ready[half, band]]
                turned_south[half, band] = chosen(north[half][band], many)
            return turned_south[half, band]

        def to_north(half, band):
            if (half, band) not in turned_north:
                many = [item[1] for item in ready[half, band]]
                turned_north[half, band] = chosen(south[half][band], many)
            return turned_north[half, band]

        for band in bands:
            for half in range(halves):
                if half + 1 < halves:
                    ahead = [item[1] for item in ready[half + 1, band]]
                else:
                    ahead = [item[2] for item in ready[0, band]]
                if half > 0:
                    behind = [item[1] for item in ready[half - 1, band]]
                else:
                    behind = [item[3] for item in ready[halves - 1, band]]
                level, above, below = east[half][band]
                to_west = chosen((in_turn(level, done), above, below), ahead)
                to_east = chosen(west[half][band], behind)
                sums = []
                for q in range(params):
                    u = ready[half, band][q][0]
                    upper = to_south(half, band + 1)[q] if band + 1 < len(bands) else None
                    lower = to_north(half, band - 1)[q] if band > 0 else None
                    sums.append(
                        added(
                            [
                                to_west[q],
                                to_east[q],
                                None if u is None else keeps[q] * u,
                                moved_y(to_south(half, band)[q], upper, -1),
                                moved_y(to_north(half, band)[q], lower, 1),
                            ]
                        )
                    )
                new = [
                    added([mixing[p][q][band] * sums[q] for q in range(params)])
                    for p in range(params)
                ]
                done = new[0]
                if step + 1 < PASSES:
                    following[half, band] = prepare(new, half)
                else:
                    for p in range(params):
                        current[p][half][band] = new[p]
        ready = following
    current = [[jnp.concatenate(bands_of, axis=0) for bands_of in u] for u in current]

    pieces = []
    for half in range(halves):
        for p in range(params):
            pieces.append(current[p][half][width - PASSES : 2 * width + PASSES])
    used = halves * params * (width + 2 * PASSES)
    pieces.append(jnp.zeros((LANES - used, LANES), jnp.float32))
    layer_ref[0] = jnp.transpose(jnp.concatenate(pieces, axis=0))
    for group in range(groups):
        for place in range(0, depth, run):
            out_ref[place : place + run, group, :] = layer_ref[
                0, pl.ds(group * depth + order[place], run, stride), :
            ]


def collect_kernel(in_ref, out_ref, *, width):
    params, _, rows_x, rows_y = out_ref.shape
    sources, groups, _ = in_ref.shape
    span = width + 2 * PASSES
    halves = rows_x // groups
    lane = lane_ids((rows_x, LANES))
    totals = [[jnp.zeros((rows_x, LANES), jnp.float32) for _ in range(rows_y // LANES)] for _ in range(params)]
    for source in range(sources):
        message = in_ref[source]
        stacked = jnp.concatenate(
            [roll_lanes(message, -half * params * span) for half in range(halves)], axis=0
        )
        first = source * width - PASSES
        for param in range(params):
            placed = roll_lanes(stacked, first - param * span)
            for column in range(rows_y // LANES):
                low, high = first - column * LANES, first - column * LANES + span
                if high <= 0 or low >= LANES:
                    continue
                inside = jnp.logical_and(lane >= low, lane < high)
                totals[param][column] = totals[param][column] + jnp.where(inside, placed, 0.0)
    for param in range(params):
        for column in range(rows_y // LANES):
            for x in range(rows_x):
                row = (x % halves) * groups + x // halves
                out_ref[param, 0, x : x + 1, column * LANES : (column + 1) * LANES] = totals[param][
                    column
                ][row : row + 1]


def fits(sensitivity, dip_class, devices):
    tiles, rays, params, tile_depth, tile_columns = sensitivity.shape
    slab_depth, rows_x, rows_y = dip_class.shape
    depth = slab_depth * devices
    return (
        slab_depth == 1
        and rows_y == devices * SUBLANES
        and PASSES <= SUBLANES
        and rows_y % LANES == 0
        and tile_columns == LANES
        and rows_x == SUBLANES
        and tiles == 2
        and tiles * tile_depth == depth
        and (params + 1) * depth == LANES
        and 2 * params <= SUBLANES
        and 3 * SUBLANES + 2 * tiles + 1 + (params + 2) // 2 < depth
        and CAP <= 2 * rows_y
        and rays % RAY_CHUNKS == 0
        and lax.axis_size("cols") % 2 == 0
        and lax.axis_size("par") % 2 == 0
        and rows_x * params * (SUBLANES + 2 * PASSES) <= 4 * LANES
    )


def shards_by_y(
    tile_bounds, tile_anchor, tile_picks, rmo_picks, sensitivity, dip_class, strength, couple
):
    tiles, rays, params, _, _ = sensitivity.shape
    _, rows_x, rows_y = dip_class.shape
    replicas = lax.axis_size("par")
    devices = lax.axis_size("cols") * replicas
    exchange = [exchange_order(devices // replicas, replicas)]
    width = rows_y // devices
    groups = LANES // devices
    hbm = pl.BlockSpec(memory_space=pltpu.HBM)
    vmem = pl.BlockSpec(memory_space=pltpu.VMEM)
    arguments = (
        tile_bounds, tile_anchor, tile_picks, rmo_picks, sensitivity, dip_class, strength, couple
    )
    homes = (
        pltpu.SMEM, pltpu.SMEM, pltpu.SMEM, pltpu.VMEM, pltpu.VMEM, pltpu.VMEM, pltpu.SMEM, pltpu.SMEM
    )
    sent = pl.pallas_call(
        source_kernel,
        out_shape=pltpu.VMEM((devices, width, LANES), jnp.float32),
        in_specs=[hbm] * len(arguments),
        out_specs=vmem,
        scratch_shapes=[home(array.shape, array.dtype) for home, array in zip(homes, arguments)]
        + [
            pltpu.VMEM((tiles, rays, LANES), jnp.float32),
            pltpu.SemaphoreType.DMA((len(arguments) - 1,)),
            pltpu.SemaphoreType.DMA((tiles, RAY_CHUNKS)),
        ],
        compiler_params=pltpu.CompilerParams(vmem_limit_bytes=32 << 20),
        name="sum_rays",
    )(*(pltpu.with_memory_space_constraint(array, pltpu.HBM) for array in arguments))
    received = lax.all_to_all(sent, ("cols", "par"), 0, 0, axis_index_groups=exchange)
    layers = pl.pallas_call(
        functools.partial(
            smooth_kernel,
            params=params,
            tiles=tiles,
            replicas=replicas,
            rows_x=rows_x,
            rows_y=rows_y,
        ),
        out_shape=jax.ShapeDtypeStruct((devices, groups, LANES), jnp.float32),
        in_specs=[vmem],
        out_specs=vmem,
        scratch_shapes=[pltpu.VMEM((rows_x // groups, LANES, LANES), jnp.float32)],
        compiler_params=pltpu.CompilerParams(vmem_limit_bytes=32 << 20),
        name="smooth_block",
    )(received)
    windows = lax.all_to_all(layers, ("cols", "par"), 0, 0, axis_index_groups=exchange)
    return pl.pallas_call(
        functools.partial(collect_kernel, width=width),
        out_shape=jax.ShapeDtypeStruct((params, 1, rows_x, rows_y), jnp.float32),
        in_specs=[vmem],
        out_specs=vmem,
        compiler_params=pltpu.CompilerParams(vmem_limit_bytes=32 << 20),
        name="collect_windows",
    )(windows)


def shards(
    tile_bounds, tile_anchor, tile_picks, rmo_picks, sensitivity, dip_class, strength, couple
):
    devices = lax.axis_size("cols") * lax.axis_size("par")
    plan = shards_by_y if fits(sensitivity, dip_class, devices) else shards_any
    return plan(
        tile_bounds, tile_anchor, tile_picks, rmo_picks, sensitivity, dip_class, strength, couple
    )


def solution(mesh):
    return jax.shard_map(
        shards,
        mesh=mesh,
        in_specs=(
            P(),
            P(("cols", "par"), None),
            P(("cols", "par")),
            P(("cols", "par"), None),
            P(("cols", "par"), None, None, None, None),
            P(("cols", "par"), None, None),
            P(),
            P(),
        ),
        out_specs=P(None, ("cols", "par"), None, None),
        check_vma=False,
    )
```

```python
import functools

import jax
import jax.numpy as jnp
from jax import lax
from jax.experimental import pallas as pl
from jax.experimental.pallas import tpu as pltpu
from jax.sharding import PartitionSpec as P

CAP = 384
PASSES = 6


def extended(block, sides, width):
    for axis, dim in sides:
        count = lax.axis_size(axis)
        forward = [(i, i + 1) for i in range(count - 1)]
        backward = [(target, source) for source, target in forward]
        low = lax.ppermute(
            lax.slice_in_dim(block, block.shape[dim] - width, None, axis=dim), axis, forward
        )
        high = lax.ppermute(lax.slice_in_dim(block, 0, width, axis=dim), axis, backward)
        block = jnp.concatenate([low, block, high], axis=dim)
    return block


def next_cells(values, along_dim):
    count = values.shape[along_dim]
    kept = lax.slice_in_dim(values, 1, count, axis=along_dim)
    zeros = jnp.zeros_like(lax.slice_in_dim(values, 0, 1, axis=along_dim))
    return jnp.concatenate([kept, zeros], axis=along_dim)


def prev_cells(values, along_dim):
    count = values.shape[along_dim]
    kept = lax.slice_in_dim(values, 0, count - 1, axis=along_dim)
    zeros = jnp.zeros_like(lax.slice_in_dim(values, 0, 1, axis=along_dim))
    return jnp.concatenate([zeros, kept], axis=along_dim)


def at_depth(padded, tilt):
    return jnp.where(tilt < 0, padded[:, :-2], jnp.where(tilt > 0, padded[:, 2:], padded[:, 1:-1]))


def smooth_pass(padded, dip_class, strength, mixing):
    centre = padded[:, 1:-1]
    tilt_across = (dip_class // 3 - 1)[None]
    tilt_along = (dip_class % 3 - 1)[None]
    east_side = at_depth(next_cells(padded, 2), tilt_across)
    west_side = at_depth(prev_cells(padded, 2), -tilt_across)
    north_side = at_depth(next_cells(padded, 3), tilt_along)
    south_side = at_depth(prev_cells(padded, 3), -tilt_along)
    laplace = east_side + west_side + north_side + south_side - 4.0 * centre
    smooth = centre + strength[:, None, None, None] * laplace
    return jnp.tensordot(mixing, smooth, axes=1, precision=lax.Precision.HIGHEST)


def shards_any(
    tile_bounds, tile_anchor, tile_picks, rmo_picks, sensitivity, dip_class, strength, couple
):
    tile_count, ray_count, param_count, depth_cells, tile_columns = sensitivity.shape
    col_devices = lax.axis_size("cols")
    par_devices = lax.axis_size("par")
    slab_depth, rows_x, rows_y = dip_class.shape
    total_depth = slab_depth * col_devices * par_devices
    live = jnp.arange(ray_count, dtype=jnp.int32)[None, :] < tile_picks[:, None]
    ray_weight = jnp.where(live, rmo_picks, jnp.zeros_like(rmo_picks))
    contribution = jnp.einsum(
        "tr,trk->tk",
        ray_weight,
        sensitivity.reshape(tile_count, ray_count, -1),
        preferred_element_type=jnp.float32,
    )
    contribution = contribution.reshape(tile_count, param_count, depth_cells, tile_columns)

    def add_tile(tile_number, gradient):
        anchor = (jnp.int32(0), tile_anchor[tile_number, 0], tile_anchor[tile_number, 1])
        current = lax.dynamic_slice(gradient, anchor, (param_count, depth_cells, tile_columns))
        return lax.dynamic_update_slice(gradient, current + contribution[tile_number], anchor)

    gradient = jnp.zeros((param_count, total_depth, CAP), jnp.float32)
    gradient = lax.fori_loop(0, tile_count, add_tile, gradient)
    blocks = gradient.reshape(param_count, col_devices, par_devices, slab_depth, CAP)
    reduced = lax.psum_scatter(blocks, "par", scatter_dimension=2, tiled=True)
    summed = lax.all_to_all(reduced, "cols", split_axis=1, concat_axis=4, tiled=True)
    padded_slots = summed.reshape(param_count, slab_depth, col_devices * CAP)
    columns = rows_x * rows_y
    column_ids = jnp.arange(columns, dtype=jnp.int32)
    starts = tile_bounds[:-1]
    below = starts[None, :] <= column_ids[:, None]
    owner_tile = jnp.sum(below.astype(jnp.int32), axis=1) - 1
    tile_start = jnp.max(jnp.where(below, starts[None, :], jnp.zeros_like(starts)[None, :]), axis=1)
    slot_index = owner_tile * CAP + column_ids - tile_start
    field = jnp.take(padded_slots, slot_index, axis=2).reshape(
        param_count, slab_depth, rows_x, rows_y
    )
    mixing = couple / jnp.sum(couple, axis=1, keepdims=True)
    for _ in range(PASSES):
        padded = extended(field, ((("cols", "par"), 1),), 1)
        field = smooth_pass(padded, dip_class, strength, mixing)
    return field


LANES = 128
SUBLANES = 8
RAY_CHUNKS = 2


def exchange_order(cols, par):
    return sorted(range(cols * par), key=lambda i: (i // par % 2, i % par % 2, i % par // 2, i // par // 2))


def block_index():
    col, replica = lax.axis_index("cols"), lax.axis_index("par")
    odd = lax.rem(col, 2) * 2 + lax.rem(replica, 2)
    return (odd * (lax.axis_size("par") // 2) + replica // 2) * (lax.axis_size("cols") // 2) + col // 2


def lane_ids(shape):
    return lax.broadcasted_iota(jnp.int32, shape, len(shape) - 1)


def roll_lanes(values, shift):
    width = values.shape[-1]
    shift = shift % width
    return values if shift == 0 else pltpu.roll(values, shift, values.ndim - 1)


def source_kernel(
    bounds_hbm, anchor_hbm, picks_hbm, rmo_hbm, sens_hbm, dip_hbm, strength_hbm, couple_hbm,
    out_ref,
    bounds_ref, anchor_ref, picks_ref, rmo_ref, sens_ref, dip_ref, strength_ref, couple_ref,
    weight_ref, small_sems, sens_sems,
):
    tiles, rays, params, tile_depth, tile_columns = sens_ref.shape
    _, rows_x, rows_y = dip_ref.shape
    devices, width, _ = out_ref.shape
    halves = rows_y // LANES
    per_tile = sens_sems.shape[1]
    chunk = rays // per_tile
    small = [
        pltpu.make_async_copy(hbm, ref, small_sems.at[number])
        for number, (hbm, ref) in enumerate(
            [
                (picks_hbm, picks_ref),
                (rmo_hbm, rmo_ref),
                (bounds_hbm, bounds_ref),
                (anchor_hbm, anchor_ref),
                (dip_hbm, dip_ref),
                (strength_hbm, strength_ref),
                (couple_hbm, couple_ref),
            ]
        )
    ]
    large = [
        [
            pltpu.make_async_copy(
                sens_hbm.at[tile, pl.ds(part * chunk, chunk)],
                sens_ref.at[tile, pl.ds(part * chunk, chunk)],
                sens_sems.at[tile, part],
            )
            for part in range(per_tile)
        ]
        for tile in range(tiles)
    ]
    for copy in small[:2]:
        copy.start()
    for row in large:
        for copy in row:
            copy.start()
    for copy in small[2:]:
        copy.start()

    diagonal = lax.broadcasted_iota(jnp.int32, (rays, rays), 0) == lane_ids((rays, rays))
    for copy in small:
        copy.wait()
    residuals = rmo_ref[...].astype(jnp.float32)
    for tile in range(tiles):
        live = lane_ids((1, rays)) < picks_ref[tile]
        weight = jnp.where(live, residuals[tile : tile + 1], 0.0)
        column = jnp.sum(jnp.where(diagonal, weight, 0.0), axis=1, keepdims=True)
        weight_ref[tile] = jnp.broadcast_to(column, (rays, LANES))

    side = 3 * width
    lane = lane_ids((width, LANES))
    row = lax.broadcasted_iota(jnp.int32, (width, LANES), 0)
    factors = [jnp.full((width, LANES), strength_ref[q], jnp.float32) for q in range(params)]
    for p in range(params):
        weights = [jnp.full((width, LANES), couple_ref[p, q], jnp.float32) for q in range(params)]
        whole = weights[0]
        for weight in weights[1:]:
            whole = whole + weight
        factors.extend(weight / whole for weight in weights)
    note = jnp.zeros((width, LANES), jnp.float32)
    for number, factor in enumerate(factors):
        at = side + 2 * tiles + 1 + number // (2 * params)
        note = jnp.where(jnp.logical_and(lane == at, row == number % (2 * params)), factor, note)

    column_first = bounds_ref[lax.axis_index("cols")]
    column_x = column_first // rows_y
    column_y = column_first - column_x * rows_y
    first_depth, lane_first, first_half = [], [], []
    whole_note = jnp.where(lane == side + 2 * tiles, column_x, 0)
    more_below = jnp.where(lane == side + 2 * tiles, column_y, 0)
    less_below = jnp.zeros((width, LANES), jnp.int32)
    for tile in range(tiles):
        first_depth.append(anchor_ref[tile, 0])
        first = column_first + anchor_ref[tile, 1]
        first_x = first // rows_y
        first_y = first - first_x * rows_y
        first_half.append(first_y // LANES)
        lane_first.append(first_y - first_half[tile] * LANES)
        whole_note = jnp.where(lane == side + tile, first_x - column_x, whole_note)
        whole_note = jnp.where(lane == side + tiles + tile, first_depth[tile], whole_note)
        more_below = jnp.where(lane == side + tile, first_y, more_below)
        less_below = jnp.where(lane == side + tile, column_y, less_below)
    note = note + whole_note.astype(jnp.float32)
    dip = dip_ref[0].astype(jnp.float32)
    count = LANES // width
    in_window = lane < side
    for device in range(devices):
        y = row + device * width
        steps = jnp.where(y < more_below, 1.0, 0.0) - jnp.where(y < less_below, 1.0, 0.0)
        window = roll_lanes(dip, width - device * width)[:, :LANES]
        out_ref[device] = jnp.where(in_window, window, note + steps)

    row_ids = lax.broadcasted_iota(jnp.int32, (LANES, LANES), 0)
    first_tile = lane_ids((LANES, LANES)) % devices < tile_depth
    half_before = jnp.where(first_tile, first_half[0], first_half[1])
    half_after = jnp.where(half_before == halves - 1, 0, half_before + 1)
    half_of = jnp.where(
        row_ids >= jnp.where(first_tile, lane_first[0], lane_first[1]), half_before, half_after
    )

    parts = [[None] * tiles for _ in range(params)]
    for tile in range(tiles):
        total = jnp.zeros((params, tile_depth, tile_columns), jnp.float32)
        for ray in range(rays):
            if ray % chunk == 0:
                large[tile][ray // chunk].wait()
            weight = weight_ref[tile, ray : ray + 1, :]
            total = total + weight[None] * sens_ref[tile, ray].astype(jnp.float32)
        for param in range(params):
            turned = pltpu.roll(total[param], lax.rem(first_depth[tile], tile_depth), 0)
            parts[param][tile] = pltpu.roll(turned, lane_first[tile], 1)
    rows = [jnp.zeros((devices, tile_columns), jnp.float32)]
    for param in range(params):
        rows.extend(parts[param])
    turned = jnp.transpose(jnp.concatenate(rows, axis=0))
    for half in range(halves):
        kept = jnp.where(half_of == half, turned, 0.0)
        for place in range(count):
            device = half * count + place
            out_ref[device] = out_ref[device] + kept[place * width : (place + 1) * width]


def smooth_kernel(in_ref, out_ref, layer_ref, *, params, tiles, replicas, rows_x, rows_y):
    depth, width, _ = in_ref.shape
    groups = LANES // depth
    halves = rows_x // groups
    rows = 3 * width
    side = rows
    lane = lane_ids((width, LANES))
    low = lane % depth < depth // 2
    in_tile = (lane % (depth // 2)).astype(jnp.float32)
    zero = jnp.zeros((width, LANES), jnp.float32)
    run = depth // replicas // 2
    stride = 2 * replicas
    order = exchange_order(depth // replicas, replicas)
    dip = []
    for half in range(halves):
        for group in range(groups):
            for place in range(0, depth, run):
                layer_ref[half, pl.ds(group * depth + order[place], run, stride), :] = in_ref[
                    place : place + run, group * halves + half, :
                ]
        dip.append(jnp.transpose(layer_ref[half])[:rows])

    stays = [zero] * rows_x
    moves = [zero] * rows_x
    from_lane = lax.broadcasted_iota(jnp.int32, (LANES, 3 * LANES), 0)
    to_lane = lane_ids((LANES, 3 * LANES))
    tile_of = (to_lane % depth) // (depth // 2)
    spread = from_lane == side + jnp.where(
        to_lane < 2 * LANES, tile_of + jnp.where(to_lane < LANES, 0, tiles), 2 * tiles
    )
    packets = in_ref[...].reshape(depth * width, LANES)
    packet_lanes = lane_ids(packets.shape)
    is_note = jnp.logical_and(packet_lanes >= side, packet_lanes <= side + 2 * tiles)
    notes = jnp.dot(
        jnp.where(is_note, packets, 0.0).astype(jnp.bfloat16),
        jnp.where(spread, 1.0, 0.0).astype(jnp.bfloat16),
        preferred_element_type=jnp.float32,
    )
    columns = depth // replicas
    places = {device: place for place, device in enumerate(exchange_order(columns, replicas))}
    for column in range(columns):
        near = [[zero, zero], [zero, zero]]
        for replica in range(replicas):
            place = places[column * replicas + replica]
            message = in_ref[place]
            rows_of = slice(place * width, (place + 1) * width)
            second = notes[rows_of, :LANES] > 0.5
            stay = jnp.logical_xor(low, in_tile < notes[rows_of, LANES : 2 * LANES])
            for sums, values in zip(near, (jnp.where(stay, message, 0.0), jnp.where(stay, 0.0, message))):
                sums[0] = sums[0] + jnp.where(second, 0.0, values)
                sums[1] = sums[1] + jnp.where(second, values, 0.0)
        from_x = notes[rows_of, 2 * LANES :]
        for x in range(rows_x):
            here = from_x == float(x)
            for field, sums in zip((stays, moves), near):
                field[x] = field[x] + jnp.where(here, sums[0], 0.0)
                if x + 1 < rows_x:
                    field[x + 1] = field[x + 1] + jnp.where(here, sums[1], 0.0)

    block = lane // depth
    current = []
    for param in range(params):
        current.append([])
        for half in range(halves):
            centre = zero
            for group in range(groups):
                x = group * halves + half
                shift = depth * (group - param - 1)
                moved = jnp.where(
                    low,
                    roll_lanes(moves[x], shift - depth // 2),
                    roll_lanes(moves[x], shift + depth // 2),
                )
                centre = jnp.where(block == group, roll_lanes(stays[x], shift) + moved, centre)
            current[param].append([None, centre, None])

    lanes = lane_ids((rows, LANES))
    z = lanes % depth
    block = lanes // depth
    first = block == 0
    last = block == groups - 1
    bands = range(3)
    own = block_index()
    in_grid = [
        jnp.where(own > 0, 1.0, 0.0),
        1.0,
        jnp.where(own < rows_y // width - 1, 1.0, 0.0),
    ]

    def by_band(values):
        return [values[band * width : (band + 1) * width] for band in bands]

    def factor(lane, q):
        number = lane * params + q
        at = side + 2 * tiles + 1 + number // (2 * params)
        row = number % (2 * params)
        return jnp.broadcast_to(in_ref[0, row : row + 1, at : at + 1], (width, LANES))

    strengths = [factor(0, q) for q in range(params)]
    keeps = [1.0 / strength - 4.0 for strength in strengths]
    mixing = [
        [
            [factor(p + 1, q) * strengths[q] * in_grid[band] for band in bands]
            for q in range(params)
        ]
        for p in range(params)
    ]

    def codes(tilt, inside=True):
        level = jnp.where(jnp.abs(tilt) < 0.5, 1.0, 0.0)
        above = jnp.where(jnp.logical_and(tilt < -0.5, z > 0), 1.0, 0.0)
        below = jnp.where(jnp.logical_and(tilt > 0.5, z < depth - 1), 1.0, 0.0)
        weights = [by_band(jnp.where(inside, weight, 0.0)) for weight in (level, above, below)]
        return list(zip(*weights))

    def chosen(weights, many):
        results = []
        for values in many:
            if values is None:
                results.append(None)
                continue
            total = values[0] * weights[0]
            for value, weight in zip(values[1:], weights[1:]):
                total = total + value * weight
            results.append(total)
        return results

    def candidates(values, shift):
        if values is None:
            return None
        return [roll_lanes(values, shift + step) for step in (0, 1, -1)]

    row_ids = lax.broadcasted_iota(jnp.int32, (width, LANES), 0)

    def moved_y(here, there, step):
        if here is None and there is None:
            return None
        parts = [
            0.0 if values is None else pltpu.roll(values, step % width, 0) for values in (here, there)
        ]
        return jnp.where(row_ids == (width - 1 if step < 0 else 0), parts[1], parts[0])

    def added(terms):
        terms = [term for term in terms if term is not None]
        total = terms[0] if terms else None
        for term in terms[1:]:
            total = total + term
        return total

    east, west, north, south = [], [], [], []
    for half in range(halves):
        tilt_x = jnp.where(dip[half] < 2.5, -1.0, jnp.where(dip[half] > 5.5, 1.0, 0.0))
        tilt_y = dip[half] - 3.0 * tilt_x - 4.0
        east.append(codes(tilt_x, jnp.logical_or(half + 1 < halves, jnp.logical_not(last))))
        west.append(codes(-tilt_x, jnp.logical_or(half > 0, jnp.logical_not(first))))
        north.append(codes(pltpu.roll(tilt_y, 1, 0)))
        south.append(codes(-pltpu.roll(tilt_y, rows - 1, 0)))

    def prepare(u, half):
        return [
            (
                v,
                candidates(v, 0),
                candidates(v, -depth) if half == 0 else None,
                candidates(v, depth) if half == halves - 1 else None,
            )
            for v in u
        ]

    ready = {
        (half, band): prepare([current[p][half][band] for p in range(params)], half)
        for band in bands
        for half in range(halves)
    }
    def in_turn(weight, earlier):
        return weight if earlier is None else jnp.maximum(weight, jnp.minimum(earlier, -1e30))

    for step in range(PASSES):
        turned_south, turned_north = {}, {}
        following = {}
        done = None

        def to_south(half, band):
            if (half, band) not in turned_south:
                many = [item[1] for item in ready[half, band]]
                turned_south[half, band] = chosen(north[half][band], many)
            return turned_south[half, band]

        def to_north(half, band):
            if (half, band) not in turned_north:
                many = [item[1] for item in ready[half, band]]
                turned_north[half, band] = chosen(south[half][band], many)
            return turned_north[half, band]

        for band in bands:
            for half in range(halves):
                if half + 1 < halves:
                    ahead = [item[1] for item in ready[half + 1, band]]
                else:
                    ahead = [item[2] for item in ready[0, band]]
                if half > 0:
                    behind = [item[1] for item in ready[half - 1, band]]
                else:
                    behind = [item[3] for item in ready[halves - 1, band]]
                level, above, below = east[half][band]
                to_west = chosen((in_turn(level, done), above, below), ahead)
                to_east = chosen(west[half][band], behind)
                sums = []
                for q in range(params):
                    u = ready[half, band][q][0]
                    upper = to_south(half, band + 1)[q] if band + 1 < len(bands) else None
                    lower = to_north(half, band - 1)[q] if band > 0 else None
                    sums.append(
                        added(
                            [
                                to_west[q],
                                to_east[q],
                                None if u is None else keeps[q] * u,
                                moved_y(to_south(half, band)[q], upper, -1),
                                moved_y(to_north(half, band)[q], lower, 1),
                            ]
                        )
                    )
                new = [
                    added([mixing[p][q][band] * sums[q] for q in range(params)])
                    for p in range(params)
                ]
                done = new[0]
                if step + 1 < PASSES:
                    following[half, band] = prepare(new, half)
                else:
                    for p in range(params):
                        current[p][half][band] = new[p]
        ready = following
    current = [[jnp.concatenate(bands_of, axis=0) for bands_of in u] for u in current]

    pieces = []
    for half in range(halves):
        for p in range(params):
            pieces.append(current[p][half][width - PASSES : 2 * width + PASSES])
    used = halves * params * (width + 2 * PASSES)
    pieces.append(jnp.zeros((LANES - used, LANES), jnp.float32))
    layer_ref[0] = jnp.transpose(jnp.concatenate(pieces, axis=0))
    for group in range(groups):
        for place in range(0, depth, run):
            out_ref[place : place + run, group, :] = layer_ref[
                0, pl.ds(group * depth + order[place], run, stride), :
            ]


def collect_kernel(in_ref, out_ref, *, width):
    params, _, rows_x, rows_y = out_ref.shape
    sources, groups, _ = in_ref.shape
    span = width + 2 * PASSES
    halves = rows_x // groups
    lane = lane_ids((rows_x, LANES))
    totals = [[jnp.zeros((rows_x, LANES), jnp.float32) for _ in range(rows_y // LANES)] for _ in range(params)]
    for source in range(sources):
        message = in_ref[source]
        stacked = jnp.concatenate(
            [roll_lanes(message, -half * params * span) for half in range(halves)], axis=0
        )
        first = source * width - PASSES
        for param in range(params):
            placed = roll_lanes(stacked, first - param * span)
            for column in range(rows_y // LANES):
                low, high = first - column * LANES, first - column * LANES + span
                if high <= 0 or low >= LANES:
                    continue
                inside = jnp.logical_and(lane >= low, lane < high)
                totals[param][column] = totals[param][column] + jnp.where(inside, placed, 0.0)
    for param in range(params):
        for column in range(rows_y // LANES):
            for x in range(rows_x):
                row = (x % halves) * groups + x // halves
                out_ref[param, 0, x : x + 1, column * LANES : (column + 1) * LANES] = totals[param][
                    column
                ][row : row + 1]


def fits(sensitivity, dip_class, devices):
    tiles, rays, params, tile_depth, tile_columns = sensitivity.shape
    slab_depth, rows_x, rows_y = dip_class.shape
    depth = slab_depth * devices
    return (
        slab_depth == 1
        and rows_y == devices * SUBLANES
        and PASSES <= SUBLANES
        and rows_y % LANES == 0
        and tile_columns == LANES
        and rows_x == SUBLANES
        and tiles == 2
        and tiles * tile_depth == depth
        and (params + 1) * depth == LANES
        and 2 * params <= SUBLANES
        and 3 * SUBLANES + 2 * tiles + 1 + (params + 2) // 2 < depth
        and CAP <= 2 * rows_y
        and rays % RAY_CHUNKS == 0
        and lax.axis_size("cols") % 2 == 0
        and lax.axis_size("par") % 2 == 0
        and rows_x * params * (SUBLANES + 2 * PASSES) <= 4 * LANES
    )


def shards_by_y(
    tile_bounds, tile_anchor, tile_picks, rmo_picks, sensitivity, dip_class, strength, couple
):
    tiles, rays, params, _, _ = sensitivity.shape
    _, rows_x, rows_y = dip_class.shape
    replicas = lax.axis_size("par")
    devices = lax.axis_size("cols") * replicas
    exchange = [exchange_order(devices // replicas, replicas)]
    width = rows_y // devices
    groups = LANES // devices
    hbm = pl.BlockSpec(memory_space=pltpu.HBM)
    vmem = pl.BlockSpec(memory_space=pltpu.VMEM)
    arguments = (
        tile_bounds, tile_anchor, tile_picks, rmo_picks, sensitivity, dip_class, strength, couple
    )
    homes = (
        pltpu.SMEM, pltpu.SMEM, pltpu.SMEM, pltpu.VMEM, pltpu.VMEM, pltpu.VMEM, pltpu.SMEM, pltpu.SMEM
    )
    sent = pl.pallas_call(
        source_kernel,
        out_shape=pltpu.VMEM((devices, width, LANES), jnp.float32),
        in_specs=[hbm] * len(arguments),
        out_specs=vmem,
        scratch_shapes=[home(array.shape, array.dtype) for home, array in zip(homes, arguments)]
        + [
            pltpu.VMEM((tiles, rays, LANES), jnp.float32),
            pltpu.SemaphoreType.DMA((len(arguments) - 1,)),
            pltpu.SemaphoreType.DMA((tiles, RAY_CHUNKS)),
        ],
        compiler_params=pltpu.CompilerParams(vmem_limit_bytes=32 << 20),
        name="sum_rays",
    )(*(pltpu.with_memory_space_constraint(array, pltpu.HBM) for array in arguments))
    received = lax.all_to_all(sent, ("cols", "par"), 0, 0, axis_index_groups=exchange)
    layers = pl.pallas_call(
        functools.partial(
            smooth_kernel,
            params=params,
            tiles=tiles,
            replicas=replicas,
            rows_x=rows_x,
            rows_y=rows_y,
        ),
        out_shape=jax.ShapeDtypeStruct((devices, groups, LANES), jnp.float32),
        in_specs=[vmem],
        out_specs=vmem,
        scratch_shapes=[pltpu.VMEM((rows_x // groups, LANES, LANES), jnp.float32)],
        compiler_params=pltpu.CompilerParams(vmem_limit_bytes=32 << 20),
        name="smooth_block",
    )(received)
    windows = lax.all_to_all(layers, ("cols", "par"), 0, 0, axis_index_groups=exchange)
    return pl.pallas_call(
        functools.partial(collect_kernel, width=width),
        out_shape=jax.ShapeDtypeStruct((params, 1, rows_x, rows_y), jnp.float32),
        in_specs=[vmem],
        out_specs=vmem,
        compiler_params=pltpu.CompilerParams(vmem_limit_bytes=32 << 20),
        name="collect_windows",
    )(windows)


def shards(
    tile_bounds, tile_anchor, tile_picks, rmo_picks, sensitivity, dip_class, strength, couple
):
    devices = lax.axis_size("cols") * lax.axis_size("par")
    plan = shards_by_y if fits(sensitivity, dip_class, devices) else shards_any
    return plan(
        tile_bounds, tile_anchor, tile_picks, rmo_picks, sensitivity, dip_class, strength, couple
    )


def solution(mesh):
    return jax.shard_map(
        shards,
        mesh=mesh,
        in_specs=(
            P(),
            P(("cols", "par"), None),
            P(("cols", "par")),
            P(("cols", "par"), None),
            P(("cols", "par"), None, None, None, None),
            P(("cols", "par"), None, None),
            P(),
            P(),
        ),
        out_specs=P(None, ("cols", "par"), None, None),
        check_vma=False,
    )
```
